128 devices in a mesh: segment: 8 (over x, core), tp: 16 (over z, y).
Axes of the slice: x: 4, y: 4, z: 4, core: 2. Of those that a mesh axis runs over, the one named last changes fastest.
Arguments:
- latents: bfloat16 [2, 128, 3072], P(None, 'tp'), may hold values from -6 to 6
- cotangent: bfloat16 [2, 128, 3072], P(None, 'tp'), may hold values from -1.5 to 1.5
- token_counts: int32 [2], replicated, may hold values from 32 to 128, as said below
- job_ids: int32 [2], replicated, may hold values from 0 to 15
- modulation: float32 [8, 2, 3, 3072], P('segment'), may hold values from -3 to 3
- w_in: bfloat16 [8, 3072, 12288], P('segment', None, 'tp'), may hold values from -0.109375 to 0.109375
- w_out: bfloat16 [8, 12288, 3072], P('segment', 'tp'), may hold values from -0.0546875 to 0.0546875
- down_in: bfloat16 [8, 16, 16, 3072], P('segment'), may hold values from -0.109375 to 0.109375
- up_in: bfloat16 [8, 16, 16, 12288], P('segment', None, None, 'tp'), may hold values from -0.69921875 to 0.69921875
- down_out: bfloat16 [8, 16, 16, 12288], P('segment', None, None, 'tp'), may hold values from -0.0546875 to 0.0546875
- up_out: bfloat16 [8, 16, 16, 3072], P('segment'), may hold values from -0.69921875 to 0.69921875
Outputs:
- grad_down_in: float32 [8, 16, 16, 3072], P('segment', 'tp')
- grad_up_in: float32 [8, 16, 16, 12288], P('segment', None, None, 'tp')
- grad_down_out: float32 [8, 16, 16, 12288], P('segment', None, None, 'tp')
- grad_up_out: float32 [8, 16, 16, 3072], P('segment', 'tp')
The draws below stay inside these ranges and needn't reach their ends.
Inputs may be any that keep to these rules, and one draw needn't show every extreme that they name: `token_counts`: at least 32; some micro-batch holds exactly 128 tokens.
All inputs are finite; a program needn't handle non-finite values.
Results may differ from the reference program's by a relative error of at most 0.035.
Values may be sent and summed in bfloat16 or wider, within the bound.
No kernel may reach another device: no remote copies, remote signals or barrier semaphores. Data moves between devices by JAX's collectives and lax.ppermute only.
A program may use at most 128 MiB of HBM per device.

```python
import math
import jax
import jax.numpy as jnp
from jax import lax

D = 3072
FF = 12288
RANK = 16
MICRO = 2
MB_ROWS = 128
JOBS = 16
SEGMENTS = 8
N_TP = 16


def draw_token_counts(key, part):
    key = jax.random.fold_in(key, 11)
    first_key, second_key = jax.random.split(key)
    counts = jax.random.randint(first_key, (MICRO,), MB_ROWS // 4, MB_ROWS + 1)
    fullest = jax.random.randint(second_key, (), 0, MICRO)
    return counts.at[fullest].set(MB_ROWS).astype(jnp.int32)


def block_scale(rng, extent, cuts, low, high):
    factor_of = 1.0
    for dim, shards_of in cuts:
        steps = jax.random.uniform(jax.random.fold_in(jax.random.fold_in(rng, 6), dim), (shards_of,), jnp.float32, low / len(cuts), high / len(cuts))
        factor_of = factor_of * jnp.repeat(jnp.exp(steps), extent[dim] // shards_of).reshape((-1,) + (1,) * (len(extent) - 1 - dim))
    return factor_of


def normal_values(stream_key, extent, spread, reach, cuts=(), kind=jnp.bfloat16):
    level = block_scale(stream_key, extent, cuts, -0.22, 0.18) if cuts else 1.0
    array = jax.random.normal(stream_key, extent, jnp.float32) * spread * level
    return jnp.minimum(jnp.maximum(array, -reach), reach).astype(kind)


def setup_inputs(seed: int = 0) -> dict:
    seeds = jax.random.split(jax.random.key(seed), 12)
    return {
        "latents": normal_values(seeds[0], (MICRO, MB_ROWS, D), 1.0, 6.0, ((1, 16),)),
        "cotangent": normal_values(seeds[1], (MICRO, MB_ROWS, D), 0.25, 1.5, ((1, 16),)),
        "token_counts": draw_token_counts(jax.random.fold_in(seeds[11], 71), 0),
        "job_ids": jax.random.randint(seeds[3], (MICRO,), 0, JOBS).astype(jnp.int32),
        "modulation": normal_values(seeds[4], (SEGMENTS, MICRO, 3, D), 0.5, 3.0, ((0, 8),), jnp.float32),
        "w_in": normal_values(seeds[5], (SEGMENTS, D, FF), D ** -0.5, 0.109375, ((0, 8), (2, 16))),
        "w_out": normal_values(seeds[6], (SEGMENTS, FF, D), FF ** -0.5, 0.0546875, ((0, 8), (1, 16))),
        "down_in": normal_values(seeds[7], (SEGMENTS, JOBS, RANK, D), D ** -0.5, 0.109375, ((0, 8),)),
        "up_in": normal_values(seeds[8], (SEGMENTS, JOBS, RANK, FF), 0.12, 0.69921875, ((0, 8), (3, 16))),
        "down_out": normal_values(seeds[9], (SEGMENTS, JOBS, RANK, FF), FF ** -0.5, 0.0546875, ((0, 8), (3, 16))),
        "up_out": normal_values(seeds[10], (SEGMENTS, JOBS, RANK, D), 0.12, 0.69921875, ((0, 8),)),
    }


EPS = 1e-06
ROOT_TWO_PI = math.sqrt(2.0 / math.pi)

def gelu_tanh(values):
    inner = ROOT_TWO_PI * (values + 0.044715 * values * values * values)
    return 0.5 * values * (1.0 + jnp.tanh(inner))

def gelu_slope(values):
    inner = ROOT_TWO_PI * (values + 0.044715 * values * values * values)
    tangent = jnp.tanh(inner)
    return 0.5 * (1.0 + tangent) + 0.5 * values * (1.0 - tangent * tangent) * ROOT_TWO_PI * (1.0 + 3.0 * 0.044715 * values * values)

def rounded(values):
    return lax.optimization_barrier(values.astype(jnp.bfloat16)).astype(jnp.float32)

def modulate(resid, mod_shift, mod_scale):
    wide = resid.astype(jnp.float32)
    inv_rms = lax.rsqrt(lax.optimization_barrier(jnp.mean(wide * wide, axis=-1, keepdims=True)) + EPS)
    normed = wide * inv_rms
    return ((normed * (1.0 + mod_scale) + mod_shift).astype(jnp.bfloat16), normed, inv_rms)

def reference(latents, cotangent, token_counts, job_ids, modulation, w_in, w_out, down_in, up_in, down_out, up_out):
    block_cols = FF // N_TP
    grad_dn_in = jnp.zeros((SEGMENTS, JOBS, RANK, D), jnp.float32)
    grad_upp_in = jnp.zeros((SEGMENTS, JOBS, RANK, FF), jnp.float32)
    grad_dn_out = jnp.zeros((SEGMENTS, JOBS, RANK, FF), jnp.float32)
    grad_upp_out = jnp.zeros((SEGMENTS, JOBS, RANK, D), jnp.float32)
    positions = jnp.arange(MB_ROWS, dtype=jnp.int32)
    for micro_id in range(MICRO):
        row_mask = (positions < token_counts[micro_id]).astype(jnp.float32)[:, None]
        job_id = job_ids[micro_id]
        resid = (latents[micro_id].astype(jnp.float32) * row_mask).astype(jnp.bfloat16)
        saved = []
        for section in range(SEGMENTS):
            mod_shift = modulation[section, micro_id, 0]
            mod_scale = modulation[section, micro_id, 1]
            mod_gate = modulation[section, micro_id, 2]
            normed_in, normed, inv_rms = modulate(resid, mod_shift, mod_scale)
            low_in = jnp.dot(normed_in, down_in[section, job_id].T, preferred_element_type=jnp.float32).astype(jnp.bfloat16)
            total_out = jnp.zeros((MB_ROWS, D), jnp.float32)
            total_low = jnp.zeros((MB_ROWS, RANK), jnp.float32)
            for block_id in range(N_TP):
                cols = slice(block_id * block_cols, (block_id + 1) * block_cols)
                pre_act = jnp.dot(normed_in, w_in[section][:, cols], preferred_element_type=jnp.float32) + jnp.dot(low_in, up_in[section, job_id][:, cols], preferred_element_type=jnp.float32)
                activ = gelu_tanh(pre_act).astype(jnp.bfloat16)
                total_out = total_out + rounded(jnp.dot(activ, w_out[section][cols, :], preferred_element_type=jnp.float32))
                total_low = total_low + rounded(jnp.dot(activ, down_out[section, job_id][:, cols].T, preferred_element_type=jnp.float32))
            low_out = total_low.astype(jnp.bfloat16)
            branch = total_out + jnp.dot(low_out, up_out[section, job_id], preferred_element_type=jnp.float32)
            saved.append((resid, normed_in, low_in, low_out))
            resid = (resid.astype(jnp.float32) + mod_gate * branch * row_mask).astype(jnp.bfloat16)
        upstream = (cotangent[micro_id].astype(jnp.float32) * row_mask).astype(jnp.bfloat16)
        for section in range(SEGMENTS - 1, -1, -1):
            resid_in, normed_in, low_in, low_out = saved[section]
            mod_shift = modulation[section, micro_id, 0]
            mod_scale = modulation[section, micro_id, 1]
            mod_gate = modulation[section, micro_id, 2]
            unused_in, normed, inv_rms = modulate(resid_in, mod_shift, mod_scale)
            up_wide = upstream.astype(jnp.float32)
            grad_branch = (mod_gate * up_wide).astype(jnp.bfloat16)
            grad_low_out = jnp.dot(grad_branch, up_out[section, job_id].T, preferred_element_type=jnp.float32).astype(jnp.bfloat16)
            grad_upp_out = grad_upp_out.at[section, job_id].add(jnp.dot(low_out.T, grad_branch, preferred_element_type=jnp.float32))
            grad_normed = jnp.zeros((MB_ROWS, D), jnp.float32)
            for block_id in range(N_TP):
                cols = slice(block_id * block_cols, (block_id + 1) * block_cols)
                pre_act = jnp.dot(normed_in, w_in[section][:, cols], preferred_element_type=jnp.float32) + jnp.dot(low_in, up_in[section, job_id][:, cols], preferred_element_type=jnp.float32)
                activ = gelu_tanh(pre_act).astype(jnp.bfloat16)
                grad_activ = jnp.dot(grad_branch, w_out[section][cols, :].T, preferred_element_type=jnp.float32) + jnp.dot(grad_low_out, down_out[section, job_id][:, cols], preferred_element_type=jnp.float32)
                grad_dn_out = grad_dn_out.at[section, job_id, :, cols].add(jnp.dot(grad_low_out.T, activ, preferred_element_type=jnp.float32))
                grad_pre = (grad_activ * gelu_slope(pre_act)).astype(jnp.bfloat16)
                grad_upp_in = grad_upp_in.at[section, job_id, :, cols].add(jnp.dot(low_in.T, grad_pre, preferred_element_type=jnp.float32))
                grad_low_in = jnp.dot(grad_pre, up_in[section, job_id][:, cols].T, preferred_element_type=jnp.float32).astype(jnp.bfloat16)
                grad_dn_in = grad_dn_in.at[section, job_id].add(jnp.dot(grad_low_in.T, normed_in, preferred_element_type=jnp.float32))
                grad_normed = grad_normed + rounded(jnp.dot(grad_pre, w_in[section][:, cols].T, preferred_element_type=jnp.float32) + jnp.dot(grad_low_in, down_in[section, job_id], preferred_element_type=jnp.float32))
            scaled = grad_normed * (1.0 + mod_scale)
            upstream = (up_wide + inv_rms * (scaled - normed * lax.optimization_barrier(jnp.mean(scaled * normed, axis=-1, keepdims=True)))).astype(jnp.bfloat16)
    return (grad_dn_in, grad_upp_in, grad_dn_out, grad_upp_out)
```

```python
import math

import jax
import jax.numpy as jnp
from jax import lax
from jax.sharding import PartitionSpec as P

EPS = 1e-06
ROOT_TWO_PI = math.sqrt(2.0 / math.pi)
F32 = jnp.float32
BF16 = jnp.bfloat16
PAD = 128


def gelu_and_slope(values):
    inner = ROOT_TWO_PI * (values + 0.044715 * values * values * values)
    tangent = jnp.tanh(inner)
    activ = 0.5 * values * (1.0 + tangent)
    slope = 0.5 * (1.0 + tangent) + 0.5 * values * (1.0 - tangent * tangent) * ROOT_TWO_PI * (
        1.0 + 3.0 * 0.044715 * values * values
    )
    return activ, slope


def rms_stats(resid):
    wide = resid.astype(F32)
    inv_rms = lax.rsqrt(jnp.mean(wide * wide, axis=-1, keepdims=True) + EPS)
    return wide, wide * inv_rms, inv_rms


def dot(a, b, a_dim, b_dim):
    return lax.dot_general(a, b, (((a_dim,), (b_dim,)), ((), ())), preferred_element_type=F32)


def gathered(rows, tp):
    spread = jnp.broadcast_to(rows[None], (tp,) + rows.shape)
    got = lax.all_to_all(spread, "tp", 0, 0)
    return got.reshape(tp * rows.shape[0], rows.shape[1])


def scattered(parts, tp):
    cut = parts.reshape(tp, parts.shape[0] // tp, parts.shape[1])
    return lax.all_to_all(cut, "tp", 0, 0).astype(F32).sum(0)


def shards(
    latents,
    cotangent,
    token_counts,
    job_ids,
    modulation,
    w_in,
    w_out,
    down_in,
    up_in,
    down_out,
    up_out,
):
    tp = lax.axis_size("tp")
    segments = lax.axis_size("segment")
    planes = segments // 2
    seg = lax.axis_index("segment")
    plane, core = seg // 2, seg % 2
    tp_pos = lax.axis_index("tp")
    micro, own_rows, width = latents.shape
    cols = w_in.shape[2]
    jobs, rank = down_in.shape[1], down_in.shape[2]
    rows = own_rows * tp
    swap = [(s, s ^ 1) for s in range(segments)]
    onward = [(s, (s + 2) % segments) for s in range(segments)]
    back = [(d, s) for s, d in onward]

    job = job_ids[core]
    other_job = job_ids[1 - core]
    adapters = [a[0] for a in (down_in, up_in, down_out, up_out)]

    def packed(which):
        return jnp.concatenate([a[which] for a in adapters], axis=1)

    def ordered(own, other):
        return (jnp.where(core == 0, own, other), jnp.where(core == 0, other, own))

    w_first = ordered(w_in[0], lax.ppermute(w_in[0], "segment", swap))
    w_second = ordered(w_out[0], lax.ppermute(w_out[0], "segment", swap))
    low_own, low_other = packed(job), lax.ppermute(packed(other_job), "segment", swap)
    mods = ordered(
        modulation[0, core], lax.ppermute(modulation[0, 1 - core], "segment", swap)
    )
    cuts = (width, width + cols, width + 2 * cols)
    lows = [jnp.split(pack, cuts, axis=1) for pack in ordered(low_own, low_other)]

    row_index = tp_pos * own_rows + lax.iota(jnp.int32, own_rows)
    mask = (row_index < token_counts[core]).astype(F32)[:, None]
    x = (latents[core].astype(F32) * mask).astype(BF16)
    e_last = (cotangent[core].astype(F32) * mask).astype(BF16)

    def gate_rows(e, i):
        return (mods[i][2:3] * e.astype(F32)).astype(BF16)

    def forward(x, i, last):
        low_d_in, low_u_in, low_d_out, low_u_out = lows[i]
        wide, normed, inv_rms = rms_stats(x)
        u = gathered((normed * (1.0 + mods[i][1:2]) + mods[i][0:1]).astype(BF16), tp)
        low_in = dot(u, low_d_in, 1, 1).astype(BF16)
        pre = dot(u, w_first[i], 1, 0) + dot(low_in, low_u_in, 1, 0)
        activ = gelu_and_slope(pre)[0].astype(BF16)
        low_part = dot(activ, low_d_out, 1, 1).astype(BF16)
        saved = (x, u, pre, low_in, low_part)
        if last:
            return x, saved
        main_part = dot(activ, w_second[i], 1, 0).astype(BF16)
        sent = jnp.concatenate([main_part, jnp.pad(low_part, ((0, 0), (0, PAD - rank)))], axis=1)
        sums = scattered(sent, tp)
        low_out = sums[:, width : width + rank].astype(BF16)
        branch = sums[:, :width] + dot(low_out, low_u_out, 1, 0)
        return (wide + mods[i][2:3] * branch * mask).astype(BF16), saved

    def backward(e, i, saved, g_branch, first):
        low_d_in, low_u_in, low_d_out, low_u_out = lows[i]
        x, u, pre, low_in, low_part = saved
        if g_branch is None:
            g_branch = gathered(gate_rows(e, i), tp)
        g_low_out = dot(g_branch, low_u_out, 1, 1).astype(BF16)
        g_act = dot(g_branch, w_second[i], 1, 1) + dot(g_low_out, low_d_out, 1, 0)
        activ, slope = gelu_and_slope(pre)
        grad_down_out = dot(g_low_out, activ.astype(BF16), 0, 0)
        g_pre = (g_act * slope).astype(BF16)
        grad_up_in = dot(low_in, g_pre, 0, 0)
        g_low_in = dot(g_pre, low_u_in, 1, 1).astype(BF16)
        kept = (g_branch, g_low_in, grad_up_in, grad_down_out)
        if first:
            return e, kept
        part = dot(g_pre, w_first[i], 1, 1) + dot(g_low_in, low_d_in, 1, 0)
        g_u = scattered(part.astype(BF16), tp)
        wide, normed, inv_rms = rms_stats(x)
        q = g_u * (1.0 + mods[i][1:2])
        mean = jnp.mean(q * normed, axis=-1, keepdims=True)
        return (e.astype(F32) + inv_rms * (q - normed * mean)).astype(BF16), kept

    def zeros(*shape, dtype=BF16):
        return jnp.zeros(shape, dtype)

    def no_saved():
        return (
            zeros(own_rows, width),
            zeros(rows, width),
            zeros(rows, cols, dtype=F32),
            zeros(rows, rank),
            zeros(rows, rank),
        )

    def no_kept():
        return (
            zeros(rows, width),
            zeros(rows, rank),
            zeros(rank, cols, dtype=F32),
            zeros(rank, cols, dtype=F32),
        )

    def forward_plane(x, p):
        x, saved0 = forward(x, 0, False)
        x, saved1 = forward(x, 1, p == planes - 1)
        return x, (saved0, saved1)

    def backward_plane(e, saved, p, g_branch=None):
        e, kept1 = backward(e, 1, saved[1], g_branch, False)
        e, kept0 = backward(e, 0, saved[0], None, p == 0)
        return e, (kept0, kept1)

    g_last = lax.cond(
        plane == planes - 1,
        lambda e: gathered(gate_rows(e, 1), tp),
        lambda e: zeros(rows, width),
        e_last,
    )
    saved = (no_saved(), no_saved())
    kept = (no_kept(), no_kept())
    for p in range(planes - 1):
        x, saved = lax.cond(
            plane == p,
            lambda x, saved: forward_plane(x, p),
            lambda x, saved: (x, saved),
            x,
            saved,
        )
        x = lax.ppermute(x, "segment", onward)

    def turn(x, saved, kept):
        x, saved = forward_plane(x, planes - 1)
        e, kept = backward_plane(e_last, saved, planes - 1, g_last)
        return e, saved, kept

    e, saved, kept = lax.cond(
        plane == planes - 1, turn, lambda x, saved, kept: (x, saved, kept), x, saved, kept
    )
    for p in range(planes - 2, -1, -1):
        e = lax.ppermute(e, "segment", back)
        e, kept = lax.cond(
            plane == p,
            lambda e, saved, kept: backward_plane(e, saved, p),
            lambda e, saved, kept: (e, kept),
            e,
            saved,
            kept,
        )

    narrow = jnp.stack([saved[0][4].T, saved[1][4].T, kept[0][1].T, kept[1][1].T])
    got = lax.all_to_all(jnp.broadcast_to(narrow[None], (tp,) + narrow.shape), "tp", 0, 0)
    narrow_sum = got.astype(F32).sum(0)
    grads = []
    for i in range(2):
        low_out = narrow_sum[i].astype(BF16)
        grad_up_out = dot(low_out, kept[i][0], 1, 0)
        g_low = narrow_sum[2 + i]
        high = g_low.astype(BF16)
        rest = (g_low - high.astype(F32)).astype(BF16)
        grad_down_in = dot(high, saved[i][1], 1, 0) + dot(rest, saved[i][1], 1, 0)
        grads.append(jnp.concatenate([grad_down_in, kept[i][2], kept[i][3], grad_up_out], axis=1))
    mine = jnp.where(core == 0, grads[0], grads[1])
    theirs = lax.ppermute(jnp.where(core == 0, grads[1], grads[0]), "segment", swap)

    def by_job(own, other):
        index = lax.iota(jnp.int32, jobs)[:, None, None]
        return jnp.where(index == job, own[None], 0.0) + jnp.where(
            index == other_job, other[None], 0.0
        )

    def owned(own, other):
        owners = jobs // tp
        index = tp_pos * owners + lax.iota(jnp.int32, owners)[:, None, None]
        return jnp.where(index == job, own[None], 0.0) + jnp.where(
            index == other_job, other[None], 0.0
        )

    own_d_in, own_u_in, own_d_out, own_u_out = jnp.split(mine, cuts, axis=1)
    oth_d_in, oth_u_in, oth_d_out, oth_u_out = jnp.split(theirs, cuts, axis=1)
    return (
        owned(own_d_in, oth_d_in)[None],
        by_job(own_u_in, oth_u_in)[None],
        by_job(own_d_out, oth_d_out)[None],
        owned(own_u_out, oth_u_out)[None],
    )


def solution(mesh):
    return jax.shard_map(
        shards,
        mesh=mesh,
        in_specs=(
            P(None, "tp", None),
            P(None, "tp", None),
            P(),
            P(),
            P("segment", None, None, None),
            P("segment", None, "tp"),
            P("segment", "tp", None),
            P("segment", None, None, None),
            P("segment", None, None, "tp"),
            P("segment", None, None, "tp"),
            P("segment", None, None, None),
        ),
        out_specs=(
            P("segment", "tp", None, None),
            P("segment", None, None, "tp"),
            P("segment", None, None, "tp"),
            P("segment", "tp", None, None),
        ),
        check_vma=False,
    )
```

```python
import functools
import math

import jax
import jax.numpy as jnp
from jax import lax
from jax.experimental import pallas as pl
from jax.experimental.pallas import tpu as pltpu
from jax.sharding import PartitionSpec as P

EPS = 1e-06
ROOT_TWO_PI = math.sqrt(2.0 / math.pi)
F32 = jnp.float32
BF16 = jnp.bfloat16
PAD = 128
CUTS = 2
PAIR = 16
VMEM = pl.BlockSpec(memory_space=pltpu.VMEM)
HBM = pl.BlockSpec(memory_space=pltpu.HBM)
SMEM = pl.BlockSpec(memory_space=pltpu.SMEM)
PARAMS = pltpu.CompilerParams(vmem_limit_bytes=40 * 1024 * 1024)


def shape_of(*shape, dtype=BF16):
    return jax.ShapeDtypeStruct(shape, dtype)


def gelu_and_slope(values):
    inner = ROOT_TWO_PI * (values + 0.044715 * values * values * values)
    tangent = jnp.tanh(inner)
    half = 0.5 * (1.0 + tangent)
    slope = half + 0.5 * values * (1.0 - tangent * tangent) * ROOT_TWO_PI * (
        1.0 + 3.0 * 0.044715 * values * values
    )
    return values * half, slope


def rms_stats(wide):
    inv_rms = lax.rsqrt(jnp.mean(wide * wide, axis=-1, keepdims=True) + EPS)
    return wide * inv_rms, inv_rms


def dot(a, b, a_dim, b_dim):
    return lax.dot_general(a, b, (((a_dim,), (b_dim,)), ((), ())), preferred_element_type=F32)


def fetch(own, ours, theirs, buf, sem, at):
    @pl.when(own == 1)
    def _():
        pltpu.make_async_copy(ours.at[at], buf.at[at], sem).start()

    @pl.when(own != 1)
    def _():
        pltpu.make_async_copy(theirs.at[at], buf.at[at], sem).start()


def arrived(ours, buf, sem, at):
    pltpu.make_async_copy(ours.at[at], buf.at[at], sem).wait()


def cut(c, size):
    return pl.ds(c * (size // CUTS), size // CUTS)


def forward_kernel(
    own_ref,
    u_ref,
    wi_own,
    wi_other,
    wo_own,
    wo_other,
    di_ref,
    ui_ref,
    do_ref,
    act_ref,
    slope_ref,
    low_in_ref,
    low_ref,
    *rest,
    last,
):
    sent_ref, (wi_buf, wo_buf, sems) = (None, rest) if last else (rest[0], rest[1:])
    own = own_ref[0]
    width, rank = u_ref.shape[1], di_ref.shape[0]
    for c in range(CUTS):
        fetch(own, wi_own, wi_other, wi_buf, sems.at[c], (cut(c, width),))
    if not last:
        for c in range(CUTS):
            at = (slice(None), cut(c, width))
            fetch(own, wo_own, wo_other, wo_buf, sems.at[CUTS + c], at)
    low_in = dot(u_ref[...], di_ref[...], 1, 1).astype(BF16)
    low_in_ref[...] = low_in
    pre = dot(low_in, ui_ref[...], 1, 0)
    for c in range(CUTS):
        at = cut(c, width)
        arrived(wi_own, wi_buf, sems.at[c], (at,))
        pre = pre + dot(u_ref[:, at], wi_buf[at], 1, 0)
    act, slope = gelu_and_slope(pre)
    act = act.astype(BF16)
    act_ref[...] = act
    slope_ref[...] = slope
    low = dot(act, do_ref[...], 1, 1).astype(BF16)
    low_ref[...] = low
    if last:
        return
    sent_ref[:, width:] = jnp.zeros((sent_ref.shape[0], PAD), BF16)
    sent_ref[:, width : width + rank] = low
    for c in range(CUTS):
        at = (slice(None), cut(c, width))
        arrived(wo_own, wo_buf, sems.at[CUTS + c], at)
        sent_ref[at] = dot(act, wo_buf[at], 1, 0).astype(BF16)


def backward_kernel(
    own_ref,
    g_ref,
    slope_ref,
    act_ref,
    low_in_ref,
    wi_own,
    wi_other,
    wo_own,
    wo_other,
    di_ref,
    ui_ref,
    do_ref,
    uo_ref,
    g_low_in_ref,
    grad_ui_ref,
    grad_do_ref,
    *rest,
    first,
):
    part_ref, (wi_buf, wo_buf, sems) = (None, rest) if first else (rest[0], rest[1:])
    own = own_ref[0]
    width = g_ref.shape[1]
    for c in range(CUTS):
        at = (slice(None), cut(c, width))
        fetch(own, wo_own, wo_other, wo_buf, sems.at[c], at)
    if not first:
        for c in range(CUTS):
            fetch(own, wi_own, wi_other, wi_buf, sems.at[CUTS + c], (cut(c, width),))
    g_low_out = dot(g_ref[...], uo_ref[...], 1, 1).astype(BF16)
    grad_do_ref[...] = dot(g_low_out, act_ref[...], 0, 0)
    g_act = dot(g_low_out, do_ref[...], 1, 0)
    for c in range(CUTS):
        at = (slice(None), cut(c, width))
        arrived(wo_own, wo_buf, sems.at[c], at)
        g_act = g_act + dot(g_ref[at], wo_buf[at], 1, 1)
    g_pre = (g_act * slope_ref[...]).astype(BF16)
    g_low_in = dot(g_pre, ui_ref[...], 1, 1).astype(BF16)
    g_low_in_ref[...] = g_low_in
    grad_ui_ref[...] = dot(low_in_ref[...], g_pre, 0, 0)
    if first:
        return
    for c in range(CUTS):
        at = cut(c, width)
        arrived(wi_own, wi_buf, sems.at[CUTS + c], (at,))
        part = dot(g_pre, wi_buf[at], 1, 1) + dot(g_low_in, di_ref[:, at], 1, 0)
        part_ref[:, at] = part.astype(BF16)


def block_scratch(width, cols, without):
    return [
        pltpu.VMEM((PAIR, PAD) if without == "in" else (width, cols), BF16),
        pltpu.VMEM((PAIR, PAD) if without == "out" else (cols, width), BF16),
        pltpu.SemaphoreType.DMA((2 * CUTS,)),
    ]


def block_cost(rows, width, cols, matmuls):
    return pl.CostEstimate(
        flops=2 * matmuls * rows * width * cols,
        bytes_accessed=2 * matmuls * width * cols,
        transcendentals=rows * cols,
    )


def block_forward(own, u, w_first, w_second, low, last):
    rows, width = u.shape
    cols, rank = w_first[0].shape[1], low[0].shape[0]
    out = [
        shape_of(rows, cols),
        shape_of(rows, cols, dtype=F32),
        shape_of(rows, rank),
        shape_of(rows, rank),
    ]
    out += [] if last else [shape_of(rows, width + PAD)]
    return pl.pallas_call(
        functools.partial(forward_kernel, last=last),
        out_shape=out,
        in_specs=[SMEM, VMEM, HBM, HBM, HBM, HBM, VMEM, VMEM, VMEM],
        out_specs=[VMEM] * len(out),
        scratch_shapes=block_scratch(width, cols, "out" if last else None),
        compiler_params=PARAMS,
        cost_estimate=block_cost(rows, width, cols, 1 if last else 2),
        name="block_forward",
    )(own, u, *w_first, *w_second, *low[:3])


def block_backward(own, g, saved, w_first, w_second, low, first):
    rows, width = g.shape
    cols, rank = w_first[0].shape[1], low[0].shape[0]
    out = [
        shape_of(rows, rank),
        shape_of(rank, cols, dtype=F32),
        shape_of(rank, cols, dtype=F32),
    ]
    out += [] if first else [shape_of(rows, width)]
    act, slope, low_in = saved
    return pl.pallas_call(
        functools.partial(backward_kernel, first=first),
        out_shape=out,
        in_specs=[SMEM] + [VMEM] * 4 + [HBM] * 4 + [VMEM] * 4,
        out_specs=[VMEM] * len(out),
        scratch_shapes=block_scratch(width, cols, "in" if first else None),
        compiler_params=PARAMS,
        cost_estimate=block_cost(rows, width, cols, 1 if first else 2),
        name="block_backward",
    )(own, g, slope, act, low_in, *w_first, *w_second, *low)


def summed(got_ref, own_rows, at):
    total = None
    for k in range(0, got_ref.shape[0], PAIR):
        part = got_ref[k : k + PAIR, at].astype(F32)
        part = part.reshape(PAIR // own_rows, own_rows, part.shape[1]).sum(0)
        total = part if total is None else total + part
    return total


def spread(out_ref, rows):
    pair = jnp.concatenate([rows] * (PAIR // rows.shape[0]), axis=0).astype(BF16)
    for k in range(0, out_ref.shape[0], PAIR):
        out_ref[k : k + PAIR] = pair


def modulated(wide, mod_ref):
    return rms_stats(wide)[0] * (1.0 + mod_ref[1:2]) + mod_ref[0:1]


def first_rows_kernel(pick_ref, x_ref, e_ref, mod_ref, gate_ref, out_ref):
    u = modulated(x_ref[...].astype(F32), mod_ref)
    g = gate_ref[2:3] * e_ref[...].astype(F32)
    spread(out_ref, jnp.where(pick_ref[0] == 1, u, g))


def rows_in_kernel(x_ref, mod_ref, out_ref):
    spread(out_ref, modulated(x_ref[...].astype(F32), mod_ref))


def gate_rows_kernel(e_ref, mod_ref, out_ref):
    spread(out_ref, mod_ref[2:3] * e_ref[...].astype(F32))


def forward_rows_kernel(got_ref, x_ref, mask_ref, mod_ref, uo_ref, next_ref, x_out, *spread_out):
    own_rows, width = x_ref.shape
    rank = uo_ref.shape[0]
    low = summed(got_ref, own_rows, pl.ds(width, PAD)).astype(BF16)[:, :rank]
    branch = summed(got_ref, own_rows, pl.ds(0, width)) + dot(low, uo_ref[...], 1, 0)
    x = x_ref[...].astype(F32) + mod_ref[2:3] * branch * mask_ref[...]
    x = x.astype(BF16)
    x_out[...] = x
    for out_ref in spread_out:
        spread(out_ref, modulated(x.astype(F32), next_ref))


def backward_rows_kernel(got_ref, e_ref, x_ref, mod_ref, next_ref, e_out, *spread_out):
    own_rows, width = x_ref.shape
    normed, inv_rms = rms_stats(x_ref[...].astype(F32))
    q = summed(got_ref, own_rows, pl.ds(0, width)) * (1.0 + mod_ref[1:2])
    mean = jnp.mean(q * normed, axis=-1, keepdims=True)
    e = (e_ref[...].astype(F32) + inv_rms * (q - normed * mean)).astype(BF16)
    e_out[...] = e
    for out_ref in spread_out:
        spread(out_ref, next_ref[2:3] * e.astype(F32))


def rows_call(kernel, out, *operands, scalars=0):
    return pl.pallas_call(
        kernel,
        out_shape=out,
        in_specs=[SMEM] * scalars + [VMEM] * (len(operands) - scalars),
        out_specs=jax.tree.map(lambda _: VMEM, out),
        compiler_params=PARAMS,
        name=kernel.__name__,
    )(*operands)


def exchanged(parts, tp):
    rows, width = parts.shape
    got = lax.all_to_all(parts.reshape(tp, rows // tp, width), "tp", 0, 0)
    return got.reshape(rows, width)


def shards(
    latents,
    cotangent,
    token_counts,
    job_ids,
    modulation,
    w_in,
    w_out,
    down_in,
    up_in,
    down_out,
    up_out,
):
    tp = lax.axis_size("tp")
    segments = lax.axis_size("segment")
    planes = segments // 2
    seg = lax.axis_index("segment")
    plane, core = seg // 2, seg % 2
    tp_pos = lax.axis_index("tp")
    micro, own_rows, width = latents.shape
    cols = w_in.shape[2]
    jobs, rank = down_in.shape[1], down_in.shape[2]
    rows = own_rows * tp
    swap = [(s, s ^ 1) for s in range(segments)]
    onward = [(s, (s + 2) % segments) for s in range(segments)]
    back = [(d, s) for s, d in onward]
    last_plane = planes - 1

    job = job_ids[core]
    other_job = job_ids[1 - core]
    adapters = [a[0] for a in (down_in, up_in, down_out, up_out)]

    def packed(which):
        return jnp.concatenate([a[which] for a in adapters], axis=1)

    def ordered(own, other):
        return (jnp.where(core == 0, own, other), jnp.where(core == 0, other, own))

    mods = ordered(
        modulation[0, core], lax.ppermute(modulation[0, 1 - core], "segment", swap)
    )
    w_first = (w_in[0], lax.ppermute(w_in[0], "segment", swap))
    w_second = (w_out[0], lax.ppermute(w_out[0], "segment", swap))
    low_own, low_other = packed(job), lax.ppermute(packed(other_job), "segment", swap)
    cuts = (width, width + cols, width + 2 * cols)
    lows = [jnp.split(pack, cuts, axis=1) for pack in ordered(low_own, low_other)]
    owns = [(core == i).astype(jnp.int32).reshape(1) for i in range(2)]

    row_index = tp_pos * own_rows + lax.iota(jnp.int32, own_rows)
    mask = (row_index < token_counts[core]).astype(F32)[:, None]
    x = (latents[core].astype(F32) * mask).astype(BF16)
    e_last = (cotangent[core].astype(F32) * mask).astype(BF16)

    full = shape_of(rows, width)
    some = shape_of(own_rows, width)
    ends = exchanged(
        rows_call(
            first_rows_kernel,
            full,
            (plane == 0).astype(jnp.int32).reshape(1),
            x,
            e_last,
            mods[0],
            mods[1],
            scalars=1,
        ),
        tp,
    )

    def forward_plane(x, p):
        saved = []
        for i in range(2):
            if i:
                u = exchanged(sent, tp)
            else:
                u = ends if p == 0 else exchanged(rows_call(rows_in_kernel, full, x, mods[0]), tp)
            last = p == last_plane and i == 1
            act, slope, low_in, low_part, *part = block_forward(
                owns[i], u, w_first, w_second, lows[i], last
            )
            saved.append((x, u, (act, slope, low_in), low_part))
            if last:
                break
            got = exchanged(part[0], tp)
            out = [some] if i else [some, full]
            x, *sent = rows_call(
                forward_rows_kernel, out, got, x, mask, mods[i], lows[i][3], mods[1]
            )
            sent = sent[0] if sent else None
        return x, tuple(saved)

    def backward_plane(e, saved, p):
        kept = [None, None]
        for i in (1, 0):
            if i == 0:
                g = exchanged(sent, tp)
            elif p == last_plane:
                g = ends
            else:
                g = exchanged(rows_call(gate_rows_kernel, full, e, mods[1]), tp)
            x, u, acts, low_part = saved[i]
            first = p == 0 and i == 0
            g_low_in, grad_ui, grad_do, *part = block_backward(
                owns[i], g, acts, w_first, w_second, lows[i], first
            )
            kept[i] = (g, g_low_in, grad_ui, grad_do)
            if first:
                break
            got = exchanged(part[0], tp)
            out = [some, full] if i else [some]
            e, *sent = rows_call(backward_rows_kernel, out, got, e, x, mods[i], mods[0])
            sent = sent[0] if sent else None
        return e, tuple(kept)

    def zeros(*shape, dtype=BF16):
        return jnp.zeros(shape, dtype)

    def no_saved():
        acts = (zeros(rows, cols), zeros(rows, cols, dtype=F32), zeros(rows, rank))
        return (zeros(own_rows, width), zeros(rows, width), acts, zeros(rows, rank))

    def no_kept():
        return (
            zeros(rows, width),
            zeros(rows, rank),
            zeros(rank, cols, dtype=F32),
            zeros(rank, cols, dtype=F32),
        )

    saved = (no_saved(), no_saved())
    kept = (no_kept(), no_kept())
    for p in range(last_plane):
        x, saved = lax.cond(
            plane == p,
            lambda x, saved: forward_plane(x, p),
            lambda x, saved: (x, saved),
            x,
            saved,
        )
        x = lax.ppermute(x, "segment", onward)

    def turn(x, saved, kept):
        x, saved = forward_plane(x, last_plane)
        e, kept = backward_plane(e_last, saved, last_plane)
        return e, saved, kept

    e, saved, kept = lax.cond(
        plane == last_plane, turn, lambda x, saved, kept: (x, saved, kept), x, saved, kept
    )
    for p in range(last_plane - 1, -1, -1):
        e = lax.ppermute(e, "segment", back)
        e, kept = lax.cond(
            plane == p,
            lambda e, saved, kept: backward_plane(e, saved, p),
            lambda e, saved, kept: (e, kept),
            e,
            saved,
            kept,
        )

    narrow = jnp.stack([saved[0][3].T, saved[1][3].T, kept[0][1].T, kept[1][1].T])
    got = lax.all_to_all(jnp.broadcast_to(narrow[None], (tp,) + narrow.shape), "tp", 0, 0)
    narrow_sum = got.astype(F32).sum(0)
    grads = []
    for i in range(2):
        low_out = narrow_sum[i].astype(BF16)
        grad_up_out = dot(low_out, kept[i][0], 1, 0)
        g_low = narrow_sum[2 + i]
        high = g_low.astype(BF16)
        rest = (g_low - high.astype(F32)).astype(BF16)
        grad_down_in = dot(high, saved[i][1], 1, 0) + dot(rest, saved[i][1], 1, 0)
        grads.append(jnp.concatenate([grad_down_in, kept[i][2], kept[i][3], grad_up_out], axis=1))
    mine = jnp.where(core == 0, grads[0], grads[1])
    theirs = lax.ppermute(jnp.where(core == 0, grads[1], grads[0]), "segment", swap)

    def by_job(own, other):
        index = lax.iota(jnp.int32, jobs)[:, None, None]
        return jnp.where(index == job, own[None], 0.0) + jnp.where(
            index == other_job, other[None], 0.0
        )

    def owned(own, other):
        owners = jobs // tp
        index = tp_pos * owners + lax.iota(jnp.int32, owners)[:, None, None]
        return jnp.where(index == job, own[None], 0.0) + jnp.where(
            index == other_job, other[None], 0.0
        )

    own_d_in, own_u_in, own_d_out, own_u_out = jnp.split(mine, cuts, axis=1)
    oth_d_in, oth_u_in, oth_d_out, oth_u_out = jnp.split(theirs, cuts, axis=1)
    return (
        owned(own_d_in, oth_d_in)[None],
        by_job(own_u_in, oth_u_in)[None],
        by_job(own_d_out, oth_d_out)[None],
        owned(own_u_out, oth_u_out)[None],
    )


def solution(mesh):
    return jax.shard_map(
        shards,
        mesh=mesh,
        in_specs=(
            P(None, "tp", None),
            P(None, "tp", None),
            P(),
            P(),
            P("segment", None, None, None),
            P("segment", None, "tp"),
            P("segment", "tp", None),
            P("segment", None, None, None),
            P("segment", None, None, "tp"),
            P("segment", None, None, "tp"),
            P("segment", None, None, None),
        ),
        out_specs=(
            P("segment", "tp", None, None),
            P("segment", None, None, "tp"),
            P("segment", None, None, "tp"),
            P("segment", "tp", None, None),
        ),
        check_vma=False,
    )
```

```python
import functools
import math

import jax
import jax.numpy as jnp
from jax import lax
from jax.experimental import pallas as pl
from jax.experimental.pallas import tpu as pltpu
from jax.sharding import PartitionSpec as P

EPS = 1e-06
ROOT_TWO_PI = math.sqrt(2.0 / math.pi)
F32 = jnp.float32
BF16 = jnp.bfloat16
PAD = 128
CUTS = 2
PAIR = 16
VMEM = pl.BlockSpec(memory_space=pltpu.VMEM)
HBM = pl.BlockSpec(memory_space=pltpu.HBM)
SMEM = pl.BlockSpec(memory_space=pltpu.SMEM)
PARAMS = pltpu.CompilerParams(vmem_limit_bytes=16 * 1024 * 1024)


def shape_of(*shape, dtype=BF16):
    return jax.ShapeDtypeStruct(shape, dtype)


def gelu_and_slope(values):
    inner = ROOT_TWO_PI * (values + 0.044715 * values * values * values)
    tangent = jnp.tanh(inner)
    half = 0.5 * (1.0 + tangent)
    slope = half + 0.5 * values * (1.0 - tangent * tangent) * ROOT_TWO_PI * (
        1.0 + 3.0 * 0.044715 * values * values
    )
    return values * half, slope


def rms_stats(wide):
    inv_rms = lax.rsqrt(jnp.mean(wide * wide, axis=-1, keepdims=True) + EPS)
    return wide * inv_rms, inv_rms


def dot(a, b, a_dim, b_dim):
    return lax.dot_general(a, b, (((a_dim,), (b_dim,)), ((), ())), preferred_element_type=F32)


def fetch(own, ours, theirs, buf, sem):
    @pl.when(own)
    def _():
        pltpu.make_async_copy(ours, buf, sem).start()

    @pl.when(jnp.logical_not(own))
    def _():
        pltpu.make_async_copy(theirs, buf, sem).start()


def cut(c, size):
    return pl.ds(c * (size // CUTS), size // CUTS)


def keep(buf, out, sem):
    copy = pltpu.make_async_copy(buf, out, sem)
    copy.start()
    return copy


def in_hbm(*arrays):
    return [pltpu.with_memory_space_constraint(a, pltpu.HBM) for a in arrays]


def order_kernel(flag_ref, wi_own, wi_other, wo_own, wo_other, *refs):
    outs, (wi_buf, wo_buf, in_sems, out_sems) = refs[:2], refs[2:]
    sources = ((wi_own, wi_other, wi_buf), (wo_own, wo_other, wo_buf))

    @pl.when(flag_ref[0] == 1)
    def _():
        for k, (ours, theirs, buf) in enumerate(sources):
            fetch(flag_ref[1] == 1, ours, theirs, buf, in_sems.at[k])
        for k, (ours, theirs, buf) in enumerate(sources):
            pltpu.make_async_copy(ours, buf, in_sems.at[k]).wait()
            pltpu.make_async_copy(buf, outs[k], out_sems.at[k]).start()
        for k, (ours, theirs, buf) in enumerate(sources):
            pltpu.make_async_copy(buf, outs[k], out_sems.at[k]).wait()


def second_weights(flag, weights):
    out = [shape_of(*weights[0].shape), shape_of(*weights[2].shape)]
    return pl.pallas_call(
        order_kernel,
        out_shape=out,
        in_specs=[SMEM] + [HBM] * 4,
        out_specs=[HBM] * 2,
        scratch_shapes=[
            pltpu.VMEM(out[0].shape, BF16),
            pltpu.VMEM(out[1].shape, BF16),
            pltpu.SemaphoreType.DMA((2,)),
            pltpu.SemaphoreType.DMA((2,)),
        ],
        compiler_params=PARAMS,
        name="second_weights",
    )(flag, *in_hbm(*weights))


def forward_kernel(*refs, last, streamed):
    if streamed:
        own_ref, u_ref, wi_own, wi_other, wo_own, wo_other, *refs = refs
        wi_ref, wo_ref, w_sems = refs[-3:]
        refs = refs[:-3]
        width = u_ref.shape[1]
        for c in range(CUTS):
            at = (cut(c, width),)
            fetch(own_ref[0] == 1, wi_own.at[at], wi_other.at[at], wi_ref.at[at], w_sems.at[c])
        for c in range(CUTS):
            at = (slice(None), cut(c, width))
            fetch(
                own_ref[0] == 1, wo_own.at[at], wo_other.at[at], wo_ref.at[at], w_sems.at[CUTS + c]
            )
    else:
        u_ref, wi_ref, *refs = refs
        wo_ref, refs = (None, refs) if last else (refs[0], refs[1:])

    def arrived(source, held, n, at):
        if streamed:
            pltpu.make_async_copy(source.at[at], held.at[at], w_sems.at[n]).wait()

    wi_own, wo_own = (wi_own, wo_own) if streamed else (None, None)
    di_ref, ui_ref, do_ref, act_out, slope_out, low_in_out, low_out, u_out, *rest = refs
    sent_ref, rest = (None, rest) if last else (rest[0], rest[1:])
    act_ref, slope_ref, low_in_ref, low_ref, out_sems = rest
    width, rank = u_ref.shape[1], di_ref.shape[0]
    low_in = dot(u_ref[...], di_ref[...], 1, 1).astype(BF16)
    low_in_ref[...] = low_in
    copies = [keep(u_ref, u_out, out_sems.at[4]), keep(low_in_ref, low_in_out, out_sems.at[0])]
    pre = dot(low_in, ui_ref[...], 1, 0)
    for c in range(CUTS if streamed else 1):
        at = cut(c, width) if streamed else slice(None)
        arrived(wi_own, wi_ref, c, (at,))
        pre = pre + dot(u_ref[:, at], wi_ref[at], 1, 0)
    act, slope = gelu_and_slope(pre)
    act = act.astype(BF16)
    act_ref[...] = act
    slope_ref[...] = slope
    copies.append(keep(act_ref, act_out, out_sems.at[1]))
    copies.append(keep(slope_ref, slope_out, out_sems.at[2]))
    low_ref[...] = dot(do_ref[...], act, 1, 1).astype(BF16)
    copies.append(keep(low_ref, low_out, out_sems.at[3]))
    if not last:
        sent_ref[:, width:] = jnp.zeros((sent_ref.shape[0], PAD), BF16)
        sent_ref[:, width : width + rank] = dot(act, do_ref[...], 1, 1).astype(BF16)
        for c in range(CUTS):
            at = cut(c, width)
            arrived(wo_own, wo_ref, CUTS + c, (slice(None), at))
            sent_ref[:, at] = dot(act, wo_ref[:, at], 1, 0).astype(BF16)
    for copy in copies:
        copy.wait()


def backward_kernel(*refs, first, streamed):
    if streamed:
        wi_ref, wo_ref, w_sems = refs[-3:]
        g_ref, slope_in, act_in, low_in_in, wo_hbm, wi_hbm, *refs = refs[:-3]
        width = g_ref.shape[1]
        for c in range(CUTS):
            at = (cut(c, width),)
            pltpu.make_async_copy(wo_hbm.at[at], wo_ref.at[at], w_sems.at[c]).start()
        for c in range(CUTS):
            at = (slice(None), cut(c, width))
            pltpu.make_async_copy(wi_hbm.at[at], wi_ref.at[at], w_sems.at[CUTS + c]).start()
    else:
        wi_hbm = wo_hbm = None
        g_ref, slope_in, act_in, low_in_in, wo_ref, *refs = refs
        wi_ref, refs = (None, refs) if first else (refs[0], refs[1:])

    def arrived(source, held, n, at):
        if streamed:
            pltpu.make_async_copy(source.at[at], held.at[at], w_sems.at[n]).wait()

    di_ref, ui_ref, do_ref, uo_ref, g_low_out_ref, grad_ui_out, grad_do_out, g_out, *rest = refs
    part_ref, rest = (None, rest) if first else (rest[0], rest[1:])
    act_ref, slope_ref, low_in_ref, g_low_ref, grad_ui, grad_do, io_sems = rest
    width = g_ref.shape[1]
    slope_copy = keep(slope_in, slope_ref, io_sems.at[1])
    low_in_copy = keep(low_in_in, low_in_ref, io_sems.at[2])
    act_copy = keep(act_in, act_ref, io_sems.at[0])
    g_low_out = dot(g_ref[...], uo_ref[...], 1, 1).astype(BF16)
    g_act = dot(g_low_out, do_ref[...], 1, 0)
    for c in range(CUTS if streamed else 1):
        at = cut(c, width) if streamed else slice(None)
        arrived(wo_hbm, wo_ref, c, (at,))
        g_act = g_act + dot(g_ref[:, at], wo_ref[at], 1, 0)
    slope_copy.wait()
    g_pre = (g_act * slope_ref[...]).astype(BF16)
    g_low_ref[...] = dot(ui_ref[...], g_pre, 1, 1).astype(BF16)
    copies = [keep(g_ref, g_out, io_sems.at[6]), keep(g_low_ref, g_low_out_ref, io_sems.at[3])]
    low_in_copy.wait()
    grad_ui[...] = dot(low_in_ref[...], g_pre, 0, 0)
    copies.append(keep(grad_ui, grad_ui_out, io_sems.at[4]))
    act_copy.wait()
    grad_do[...] = dot(g_low_out, act_ref[...], 0, 0)
    copies.append(keep(grad_do, grad_do_out, io_sems.at[5]))
    if not first:
        g_low_in = dot(g_pre, ui_ref[...], 1, 1).astype(BF16)
        for c in range(CUTS):
            at = (slice(None), cut(c, width))
            arrived(wi_hbm, wi_ref, CUTS + c, at)
            part = dot(g_pre, wi_ref[at], 1, 0) + dot(g_low_in, di_ref[at], 1, 0)
            part_ref[at] = part.astype(BF16)
    for copy in copies:
        copy.wait()


def block_cost(rows, width, cols, matmuls):
    return pl.CostEstimate(
        flops=2 * matmuls * rows * width * cols,
        bytes_accessed=2 * matmuls * width * cols,
        transcendentals=rows * cols,
    )


def in_vmem(*arrays):
    return [pltpu.with_memory_space_constraint(a, pltpu.VMEM) for a in arrays]


def block_forward(u, weights, low, own=None):
    rows, width = u.shape
    streamed, last = own is not None, len(weights) == 1
    rank, cols = low[1].shape
    kept = [((rows, cols), BF16), ((rows, cols), F32), ((rows, rank), BF16), ((rank, rows), BF16)]
    out = [shape_of(*s, dtype=t) for s, t in kept] + [shape_of(rows, width)]
    out += [] if last else [shape_of(rows, width + PAD)]
    stream_scratch = [
        pltpu.VMEM((width, cols), BF16),
        pltpu.VMEM((cols, width), BF16),
        pltpu.SemaphoreType.DMA((2 * CUTS,)),
    ]
    first_specs = [SMEM, VMEM] + [HBM] * 4 if streamed else [VMEM] * (1 + len(weights))
    return pl.pallas_call(
        functools.partial(forward_kernel, last=last, streamed=streamed),
        out_shape=out,
        in_specs=first_specs + [VMEM] * 3,
        out_specs=[HBM] * (len(kept) + 1) + ([] if last else [VMEM]),
        scratch_shapes=[
            *(pltpu.VMEM(s, t) for s, t in kept),
            pltpu.SemaphoreType.DMA((len(kept) + 1,)),
            *(stream_scratch if streamed else []),
        ],
        compiler_params=PARAMS,
        cost_estimate=block_cost(rows, width, cols, 1 if last else 2),
        name="block_forward",
    )(*((own, u, *in_hbm(*weights)) if streamed else (u, *in_vmem(*weights))), *low[:3])


def block_backward(g, acts, weights, low, streamed):
    rows, width = g.shape
    first = len(weights) == 1
    rank, cols = low[1].shape
    kept = [((rank, rows), BF16), ((rank, cols), F32), ((rank, cols), F32)]
    out = [shape_of(*s, dtype=t) for s, t in kept] + [shape_of(rows, width)]
    out += [] if first else [shape_of(rows, width)]
    act, slope, low_in = acts
    stream_scratch = [
        pltpu.VMEM((cols, width), BF16),
        pltpu.VMEM((width, cols), BF16),
        pltpu.SemaphoreType.DMA((2 * CUTS,)),
    ]
    return pl.pallas_call(
        functools.partial(backward_kernel, first=first, streamed=streamed),
        out_shape=out,
        in_specs=[VMEM] + [HBM] * 3 + [HBM if streamed else VMEM] * len(weights) + [VMEM] * 4,
        out_specs=[HBM] * (len(kept) + 1) + ([] if first else [VMEM]),
        scratch_shapes=[
            pltpu.VMEM((rows, cols), BF16),
            pltpu.VMEM((rows, cols), F32),
            pltpu.VMEM((rows, rank), BF16),
            *(pltpu.VMEM(s, t) for s, t in kept),
            pltpu.SemaphoreType.DMA((7,)),
            *(stream_scratch if streamed else []),
        ],
        compiler_params=PARAMS,
        cost_estimate=block_cost(rows, width, cols, len(weights)),
        name="block_backward",
    )(g, slope, act, low_in, *(in_hbm if streamed else in_vmem)(*weights), *low)


def turn_kernel(flag_ref, *refs):
    narrow_buf, wide_buf, in_sems, out_sems = refs[-4:]
    outs, sources = refs[-8:-4], refs[:4]
    step = narrow_buf.shape[1]

    def turn(own, ours, theirs, target, in_buf, out_buf, by_rows):
        count = ours.shape[0 if by_rows else 1] // step

        def cut_of(ref, c, rows):
            at = pl.ds(pl.multiple_of(c * step, step), step)
            return ref.at[at] if rows else ref.at[:, at]

        def come(c):
            slot = lax.rem(c, 2)
            source, other = (cut_of(ref, c, by_rows) for ref in (ours, theirs))
            fetch(own, source, other, in_buf.at[slot], in_sems.at[slot])

        def going(c, slot):
            target_cut = cut_of(target, c, not by_rows)
            return pltpu.make_async_copy(out_buf.at[slot], target_cut, out_sems.at[slot])

        come(0)

        def body(c, carry):
            slot = lax.rem(c, 2)

            @pl.when(c + 1 < count)
            def _():
                come(c + 1)

            source = cut_of(ours, c, by_rows)
            pltpu.make_async_copy(source, in_buf.at[slot], in_sems.at[slot]).wait()

            @pl.when(c >= 2)
            def _():
                going(c - 2, slot).wait()

            out_buf[slot] = in_buf[slot].T
            going(c, slot).start()
            return carry

        lax.fori_loop(0, count, body, 0)
        going(count - 2, count % 2).wait()
        going(count - 1, 1 - count % 2).wait()

    @pl.when(flag_ref[0] == 1)
    def _():
        for i in range(2):
            own = flag_ref[1] == i
            turn(own, *sources[:2], outs[2 * i], narrow_buf, wide_buf, True)
            turn(own, *sources[2:], outs[2 * i + 1], wide_buf, narrow_buf, False)


def turned_weights(flag, weights, held):
    width, cols = weights[0].shape
    step = 384
    out = pl.pallas_call(
        turn_kernel,
        out_shape=[shape_of(cols, width), shape_of(width, cols)] * 2,
        in_specs=[SMEM] + [HBM] * (4 + len(held)),
        out_specs=[HBM] * 4,
        scratch_shapes=[
            pltpu.VMEM((2, step, cols), BF16),
            pltpu.VMEM((2, cols, step), BF16),
            pltpu.SemaphoreType.DMA((2,)),
            pltpu.SemaphoreType.DMA((2,)),
        ],
        input_output_aliases={5 + k: k for k in range(len(held))},
        compiler_params=PARAMS,
        name="turned_weights",
    )(flag, *in_hbm(*weights), *held)
    return tuple(out)


def summed(got_ref, own_rows, at):
    total = None
    for k in range(0, got_ref.shape[0], PAIR):
        part = got_ref[k : k + PAIR, at].astype(F32)
        part = part.reshape(PAIR // own_rows, own_rows, part.shape[1]).sum(0)
        total = part if total is None else total + part
    return total


def spread(out_ref, rows):
    pair = jnp.concatenate([rows] * (PAIR // rows.shape[0]), axis=0).astype(BF16)
    for k in range(0, out_ref.shape[0], PAIR):
        out_ref[k : k + PAIR] = pair


def modulated(wide, mod_ref):
    return rms_stats(wide)[0] * (1.0 + mod_ref[1:2]) + mod_ref[0:1]


def first_rows_kernel(
    ids_ref,
    counts_ref,
    x_ref,
    e_ref,
    mod_own,
    mod_other,
    out_ref,
    x_out,
    e_out,
    mask_out,
    mod_0,
    mod_1,
    x_in,
    e_in,
    mod_in,
    sems,
):
    copies = [
        keep(source, held, sems.at[k])
        for k, (source, held) in enumerate(((x_ref, x_in), (e_ref, e_in), (mod_own, mod_in)))
    ]
    for copy in copies:
        copy.wait()
    at_start, core, tp_pos = ids_ref[0], ids_ref[1], ids_ref[2]
    own_rows = x_ref.shape[1]
    row = tp_pos * own_rows + lax.broadcasted_iota(jnp.int32, (own_rows, 1), 0)
    mask = (row < counts_ref[core]).astype(F32)
    mask_out[...] = mask
    ours, theirs = mod_in[core], mod_other[core]
    mod_0[...] = jnp.where(core == 0, ours, theirs)
    mod_1[...] = jnp.where(core == 0, theirs, ours)
    x = (x_in[core].astype(F32) * mask).astype(BF16)
    e = (e_in[core].astype(F32) * mask).astype(BF16)
    x_out[...] = x
    e_out[...] = e
    u = modulated(x.astype(F32), mod_0)
    g = mod_1[2:3] * e.astype(F32)
    spread(out_ref, jnp.where(at_start == 1, u, g))


def pack_kernel(ids_ref, jobs_ref, *refs):
    sources, ours, theirs, sems = refs[:-3], refs[-3], refs[-2], refs[-1]
    core = ids_ref[1]
    copies = []
    for n, (job, out) in enumerate(((jobs_ref[core], ours), (jobs_ref[1 - core], theirs))):
        start = 0
        for k, source in enumerate(sources):
            at = pl.ds(start, source.shape[2])
            copies.append(keep(source.at[job], out.at[:, at], sems.at[n * len(sources) + k]))
            start += source.shape[2]
    for copy in copies:
        copy.wait()


def rows_in_kernel(x_ref, mod_ref, out_ref):
    spread(out_ref, modulated(x_ref[...].astype(F32), mod_ref))


def gate_rows_kernel(e_ref, mod_ref, out_ref):
    spread(out_ref, mod_ref[2:3] * e_ref[...].astype(F32))


def forward_rows_kernel(got_ref, x_ref, mask_ref, mod_ref, uo_ref, next_ref, x_out, *outs):
    own_rows, width = x_ref.shape
    rank = uo_ref.shape[0]
    low = summed(got_ref, own_rows, pl.ds(width, PAD)).astype(BF16)[:, :rank]
    branch = summed(got_ref, own_rows, pl.ds(0, width)) + dot(low, uo_ref[...], 1, 0)
    x = x_ref[...].astype(F32) + mod_ref[2:3] * branch * mask_ref[...]
    x = x.astype(BF16)
    x_out[...] = x
    if outs:
        x_saved, spread_out = outs
        x_saved[...] = x_ref[...]
        spread(spread_out, modulated(x.astype(F32), next_ref))


def backward_rows_kernel(got_ref, e_ref, x_ref, mod_ref, next_ref, e_out, *spread_out):
    own_rows, width = x_ref.shape
    normed, inv_rms = rms_stats(x_ref[...].astype(F32))
    q = summed(got_ref, own_rows, pl.ds(0, width)) * (1.0 + mod_ref[1:2])
    mean = jnp.mean(q * normed, axis=-1, keepdims=True)
    e = (e_ref[...].astype(F32) + inv_rms * (q - normed * mean)).astype(BF16)
    e_out[...] = e
    for out_ref in spread_out:
        spread(out_ref, next_ref[2:3] * e.astype(F32))


def narrow_kernel(*refs):
    parts, out_ref = refs[:-1], refs[-1]
    rows = jnp.concatenate([part[...].astype(F32) for part in parts], axis=0).astype(BF16)
    for k in range(0, out_ref.shape[0], rows.shape[0]):
        out_ref[k : k + rows.shape[0]] = rows


def gradients_kernel(ids_ref, got_ref, *refs):
    per_block, (ours, theirs) = refs[:8], refs[8:]
    rank, cols = per_block[2].shape
    width = per_block[0].shape[1]
    deep = 4 * rank
    total = None
    for k in range(0, got_ref.shape[0], deep):
        part = got_ref[k : k + deep].astype(F32)
        total = part if total is None else total + part
    for i in range(2):
        g_ref, u_ref, ui_ref, do_ref = per_block[4 * i : 4 * i + 4]
        low_out = total[i * rank : (i + 1) * rank].astype(BF16)
        g_low = total[(2 + i) * rank : (3 + i) * rank]
        high = g_low.astype(BF16)
        rest = (g_low - high.astype(F32)).astype(BF16)
        grads = (
            dot(high, u_ref[...], 1, 0) + dot(rest, u_ref[...], 1, 0),
            ui_ref[...],
            do_ref[...],
            dot(low_out, g_ref[...], 1, 0),
        )

        def put(out, grads=grads):
            start = 0
            for grad in grads:
                out[:, start : start + grad.shape[1]] = grad
                start += grad.shape[1]

        pl.when(ids_ref[1] == i)(functools.partial(put, ours))
        pl.when(ids_ref[1] != i)(functools.partial(put, theirs))


def by_job_kernel(ids_ref, jobs_ref, ours, theirs, di_ref, ui_ref, do_ref, uo_ref):
    core, tp_pos = ids_ref[1], ids_ref[2]
    owners, _, width = di_ref.shape
    cols = ui_ref.shape[2]
    for out in (di_ref, ui_ref, do_ref, uo_ref):
        out[...] = jnp.zeros(out.shape, F32)
    for job, grads in ((jobs_ref[core], ours), (jobs_ref[1 - core], theirs)):
        ui_ref[job] += grads[:, width : width + cols]
        do_ref[job] += grads[:, width + cols : width + 2 * cols]
        place = job - tp_pos * owners

        def owned(place=place, grads=grads):
            di_ref[place] += grads[:, :width]
            uo_ref[place] += grads[:, width + 2 * cols :]

        pl.when((place >= 0) & (place < owners))(owned)


def rows_call(kernel, out, *operands, scalars=0):
    return pl.pallas_call(
        kernel,
        out_shape=out,
        in_specs=[SMEM] * scalars + [VMEM] * (len(operands) - scalars),
        out_specs=jax.tree.map(lambda _: VMEM, out),
        compiler_params=PARAMS,
        name=kernel.__name__,
    )(*operands)


def exchanged(parts, tp):
    rows, width = parts.shape
    got = lax.all_to_all(parts.reshape(tp, rows // tp, width), "tp", 0, 0)
    return got.reshape(rows, width)


def shards(
    latents,
    cotangent,
    token_counts,
    job_ids,
    modulation,
    w_in,
    w_out,
    down_in,
    up_in,
    down_out,
    up_out,
):
    tp = lax.axis_size("tp")
    segments = lax.axis_size("segment")
    planes = segments // 2
    seg = lax.axis_index("segment")
    plane, core = seg // 2, seg % 2
    tp_pos = lax.axis_index("tp")
    micro, own_rows, width = latents.shape
    cols = w_in.shape[2]
    jobs, rank = down_in.shape[1], down_in.shape[2]
    rows = own_rows * tp
    swap = [(s, s ^ 1) for s in range(segments)]
    onward = [(s, (s + 2) % segments) for s in range(segments)]
    back = [(d, s) for s, d in onward]
    last_plane = planes - 1

    ids = jnp.stack([(plane == 0).astype(jnp.int32), core, tp_pos]).astype(jnp.int32)
    full = shape_of(rows, width)
    some = shape_of(own_rows, width)
    mod = modulation[0]
    mod_other = lax.ppermute(mod, "segment", swap)
    w_first = (w_in[0], lax.ppermute(w_in[0], "segment", swap))
    w_second = (w_out[0], lax.ppermute(w_out[0], "segment", swap))

    mod_shape = shape_of(*mod.shape[1:], dtype=F32)
    sources = (latents, cotangent, mod)
    ends, x, e_last, mask, *mods = pl.pallas_call(
        first_rows_kernel,
        out_shape=[full, some, some, shape_of(own_rows, 1, dtype=F32), mod_shape, mod_shape],
        in_specs=[SMEM, SMEM, HBM, HBM, HBM, VMEM],
        out_specs=[VMEM] * 6,
        scratch_shapes=[pltpu.VMEM(a.shape, a.dtype) for a in sources]
        + [pltpu.SemaphoreType.DMA((len(sources),))],
        compiler_params=PARAMS,
        name="first_rows_kernel",
    )(
        ids,
        token_counts,
        *in_hbm(*sources),
        mod_other,
    )

    adapters = [a[0] for a in (down_in, up_in, down_out, up_out)]
    packed = shape_of(rank, sum(a.shape[2] for a in adapters))
    low_own, low_sent = pl.pallas_call(
        pack_kernel,
        out_shape=[packed, packed],
        in_specs=[SMEM, SMEM] + [HBM] * len(adapters),
        out_specs=[VMEM, VMEM],
        scratch_shapes=[pltpu.SemaphoreType.DMA((2 * len(adapters),))],
        compiler_params=PARAMS,
        cost_estimate=pl.CostEstimate(
            flops=0, bytes_accessed=4 * math.prod(packed.shape), transcendentals=0
        ),
        name="pack_kernel",
    )(ids, job_ids, *in_hbm(*adapters))
    low_other = lax.ppermute(low_sent, "segment", swap)
    cuts = (width, width + cols, width + 2 * cols)
    lows = [
        jnp.split(jnp.where(core == i, low_own, low_other), cuts, axis=1) for i in range(2)
    ]

    ends = exchanged(ends, tp)

    def turn_weights(which, held, x):
        flag = jnp.stack([which.astype(jnp.int32), core])
        turned = turned_weights(flag, (*w_first, *w_second), held)
        return lax.optimization_barrier((turned, x))

    owns = [(core == i).astype(jnp.int32).reshape(1) for i in range(2)]
    flag = jnp.stack([(plane > 0).astype(jnp.int32), core])
    turn_flag = (plane >= planes // 2).astype(jnp.int32)
    ends, flag, turn_flag = lax.optimization_barrier((ends, flag, turn_flag))
    second, x = lax.optimization_barrier((second_weights(flag, (*w_first, *w_second)), x))
    turned, x = turn_weights(turn_flag, (), x)

    def forward_plane(x, second, p):
        saved = []
        for i in range(2):
            if i:
                u = exchanged(sent, tp)
            else:
                u = ends if p == 0 else exchanged(rows_call(rows_in_kernel, full, x, mods[0]), tp)
            last = p == last_plane and i == 1
            if i == 0 or p == 0:
                done = block_forward(u, (*w_first, *w_second), lows[i], owns[i])
            else:
                done = block_forward(u, second[:1] if last else second, lows[i])
            act, slope, low_in, low_part, u, *part = done
            kept = (u, (act, slope, low_in), low_part)
            if last:
                saved.append((x, *kept))
                break
            got = exchanged(part[0], tp)
            if i == 0:
                x_next, x, sent = rows_call(
                    forward_rows_kernel,
                    [some, some, full],
                    got,
                    x,
                    mask,
                    mods[0],
                    lows[0][3],
                    mods[1],
                )
            else:
                (x_next,) = rows_call(
                    forward_rows_kernel, [some], got, x, mask, mods[1], lows[1][3], mods[1]
                )
            saved.append((x, *kept))
            x = x_next
        return x, tuple(saved)

    def backward_plane(e, saved, turned, p):
        kept = [None, None]
        for i in (1, 0):
            if i == 0:
                g = exchanged(sent, tp)
            elif p == last_plane:
                g = ends
            else:
                g = exchanged(rows_call(gate_rows_kernel, full, e, mods[1]), tp)
            x, u, acts, low_part = saved[i]
            first = p == 0 and i == 0
            w_in_t, w_out_t = turned[2 * i : 2 * i + 2]
            g_low_in, grad_ui, grad_do, g, *part = block_backward(
                g, acts, [w_out_t] if first else [w_out_t, w_in_t], lows[i], i == 1
            )
            kept[i] = (g, g_low_in, grad_ui, grad_do)
            if first:
                break
            got = exchanged(part[0], tp)
            out = [some, full] if i else [some]
            e, *sent = rows_call(backward_rows_kernel, out, got, e, x, mods[i], mods[0])
            sent = sent[0] if sent else None
        return e, tuple(kept)

    def zeros(*shape, dtype=BF16):
        return jnp.zeros(shape, dtype)

    def no_saved():
        acts = (zeros(rows, cols), zeros(rows, cols, dtype=F32), zeros(rows, rank))
        return (zeros(own_rows, width), zeros(rows, width), acts, zeros(rank, rows))

    def no_kept():
        return (
            zeros(rows, width),
            zeros(rank, rows),
            zeros(rank, cols, dtype=F32),
            zeros(rank, cols, dtype=F32),
        )

    saved = (no_saved(), no_saved())
    kept = (no_kept(), no_kept())
    for p in range(last_plane):
        x, saved = lax.cond(
            plane == p,
            lambda x, saved: forward_plane(x, second, p),
            lambda x, saved: (x, saved),
            x,
            saved,
        )
        x = lax.ppermute(x, "segment", onward)
        if p == planes // 2 - 1:
            turned, x = turn_weights(plane < planes // 2, turned, x)

    def turn(x, saved, kept):
        x, saved = forward_plane(x, second, last_plane)
        e, kept = backward_plane(e_last, saved, turned, last_plane)
        return e, saved, kept

    e, saved, kept = lax.cond(
        plane == last_plane, turn, lambda x, saved, kept: (x, saved, kept), x, saved, kept
    )
    for p in range(last_plane - 1, -1, -1):
        e = lax.ppermute(e, "segment", back)
        e, kept = lax.cond(
            plane == p,
            lambda e, saved, kept: backward_plane(e, saved, turned, p),
            lambda e, saved, kept: (e, kept),
            e,
            saved,
            kept,
        )

    narrow = (saved[0][3], saved[1][3], kept[0][1], kept[1][1])
    got = exchanged(rows_call(narrow_kernel, shape_of(tp * 4 * rank, rows), *narrow), tp)
    wide = [shape_of(*packed.shape, dtype=F32)] * 2
    per_block = [(kept[i][0], saved[i][1], kept[i][2], kept[i][3]) for i in range(2)]
    mine, sent = rows_call(
        gradients_kernel, wide, ids, got, *per_block[0], *per_block[1], scalars=1
    )
    theirs = lax.ppermute(sent, "segment", swap)
    owned = shape_of(jobs // tp, rank, width, dtype=F32)
    split = shape_of(jobs, rank, cols, dtype=F32)
    grads = rows_call(
        by_job_kernel, [owned, split, split, owned], ids, job_ids, mine, theirs, scalars=2
    )
    return tuple(grad[None] for grad in grads)


def solution(mesh):
    return jax.shard_map(
        shards,
        mesh=mesh,
        in_specs=(
            P(None, "tp", None),
            P(None, "tp", None),
            P(),
            P(),
            P("segment", None, None, None),
            P("segment", None, "tp"),
            P("segment", "tp", None),
            P("segment", None, None, None),
            P("segment", None, None, "tp"),
            P("segment", None, None, "tp"),
            P("segment", None, None, None),
        ),
        out_specs=(
            P("segment", "tp", None, None),
            P("segment", None, None, "tp"),
            P("segment", None, None, "tp"),
            P("segment", "tp", None, None),
        ),
        check_vma=False,
    )
```

```python
import functools
import math

import jax
import jax.numpy as jnp
from jax import lax
from jax.experimental import pallas as pl
from jax.experimental.pallas import tpu as pltpu
from jax.sharding import PartitionSpec as P

EPS = 1e-06
ROOT_TWO_PI = math.sqrt(2.0 / math.pi)
F32 = jnp.float32
BF16 = jnp.bfloat16
PAD = 128
CUTS = 2
PAIR = 16
VMEM = pl.BlockSpec(memory_space=pltpu.VMEM)
HBM = pl.BlockSpec(memory_space=pltpu.HBM)
SMEM = pl.BlockSpec(memory_space=pltpu.SMEM)
PARAMS = pltpu.CompilerParams(vmem_limit_bytes=16 * 1024 * 1024)


def shape_of(*shape, dtype=BF16):
    return jax.ShapeDtypeStruct(shape, dtype)


def gelu_and_slope(values):
    inner = ROOT_TWO_PI * (values + 0.044715 * values * values * values)
    tangent = jnp.tanh(inner)
    half = 0.5 * (1.0 + tangent)
    slope = half + 0.5 * values * (1.0 - tangent * tangent) * ROOT_TWO_PI * (
        1.0 + 3.0 * 0.044715 * values * values
    )
    return values * half, slope


def rms_stats(wide):
    inv_rms = lax.rsqrt(jnp.mean(wide * wide, axis=-1, keepdims=True) + EPS)
    return wide * inv_rms, inv_rms


def dot(a, b, a_dim, b_dim):
    return lax.dot_general(a, b, (((a_dim,), (b_dim,)), ((), ())), preferred_element_type=F32)


def fetch(own, ours, theirs, buf, sem):
    @pl.when(own)
    def _():
        pltpu.make_async_copy(ours, buf, sem).start()

    @pl.when(jnp.logical_not(own))
    def _():
        pltpu.make_async_copy(theirs, buf, sem).start()


def cut(c, size):
    return pl.ds(c * (size // CUTS), size // CUTS)


def keep(buf, out, sem):
    copy = pltpu.make_async_copy(buf, out, sem)
    copy.start()
    return copy


def in_hbm(*arrays):
    return [pltpu.with_memory_space_constraint(a, pltpu.HBM) for a in arrays]


def forward_kernel(*refs, last, streamed):
    if streamed:
        own_ref, u_ref, wi_own, wi_other, wo_own, wo_other, *refs = refs
        wi_ref, wo_ref, w_sems = refs[-3:]
        refs = refs[:-3]
        width = u_ref.shape[1]
        for c in range(CUTS):
            at = (cut(c, width),)
            fetch(own_ref[0] == 1, wi_own.at[at], wi_other.at[at], wi_ref.at[at], w_sems.at[c])
        for c in range(CUTS):
            at = (slice(None), cut(c, width))
            fetch(
                own_ref[0] == 1, wo_own.at[at], wo_other.at[at], wo_ref.at[at], w_sems.at[CUTS + c]
            )
    else:
        u_ref, wi_ref, *refs = refs
        wo_ref, refs = (None, refs) if last else (refs[0], refs[1:])

    def arrived(source, held, n, at):
        if streamed:
            pltpu.make_async_copy(source.at[at], held.at[at], w_sems.at[n]).wait()

    wi_own, wo_own = (wi_own, wo_own) if streamed else (None, None)
    di_ref, ui_ref, do_ref, act_out, slope_out, low_in_out, low_out, u_out, *rest = refs
    sent_ref, rest = (None, rest) if last else (rest[0], rest[1:])
    act_ref, slope_ref, low_in_ref, low_ref, out_sems = rest
    width, rank = u_ref.shape[1], di_ref.shape[0]
    low_in = dot(u_ref[...], di_ref[...], 1, 1).astype(BF16)
    low_in_ref[...] = low_in
    copies = [keep(u_ref, u_out, out_sems.at[4]), keep(low_in_ref, low_in_out, out_sems.at[0])]
    pre = dot(low_in, ui_ref[...], 1, 0)
    for c in range(CUTS if streamed else 1):
        at = cut(c, width) if streamed else slice(None)
        arrived(wi_own, wi_ref, c, (at,))
        pre = pre + dot(u_ref[:, at], wi_ref[at], 1, 0)
    act, slope = gelu_and_slope(pre)
    act = act.astype(BF16)
    act_ref[...] = act
    slope_ref[...] = slope
    copies.append(keep(act_ref, act_out, out_sems.at[1]))
    copies.append(keep(slope_ref, slope_out, out_sems.at[2]))
    low_ref[...] = dot(do_ref[...], act, 1, 1).astype(BF16)
    copies.append(keep(low_ref, low_out, out_sems.at[3]))
    if not last:
        sent_ref[:, width:] = jnp.zeros((sent_ref.shape[0], PAD), BF16)
        sent_ref[:, width : width + rank] = dot(act, do_ref[...], 1, 1).astype(BF16)
        for c in range(CUTS):
            at = cut(c, width)
            arrived(wo_own, wo_ref, CUTS + c, (slice(None), at))
            sent_ref[:, at] = dot(act, wo_ref[:, at], 1, 0).astype(BF16)
    for copy in copies:
        copy.wait()


def backward_kernel(*refs, first, streamed):
    if streamed:
        wi_ref, wo_ref, w_sems = refs[-3:]
        g_ref, slope_in, act_in, low_in_in, wo_hbm, wi_hbm, *refs = refs[:-3]
        width = g_ref.shape[1]
        for c in range(CUTS):
            at = (cut(c, width),)
            pltpu.make_async_copy(wo_hbm.at[at], wo_ref.at[at], w_sems.at[c]).start()
        for c in range(CUTS):
            at = (slice(None), cut(c, width))
            pltpu.make_async_copy(wi_hbm.at[at], wi_ref.at[at], w_sems.at[CUTS + c]).start()
    else:
        wi_hbm = wo_hbm = None
        g_ref, slope_in, act_in, low_in_in, wo_ref, *refs = refs
        wi_ref, refs = (None, refs) if first else (refs[0], refs[1:])

    def arrived(source, held, n, at):
        if streamed:
            pltpu.make_async_copy(source.at[at], held.at[at], w_sems.at[n]).wait()

    di_ref, ui_ref, do_ref, uo_ref, g_low_out_ref, grad_ui_out, grad_do_out, g_out, *rest = refs
    part_ref, rest = (None, rest) if first else (rest[0], rest[1:])
    act_ref, slope_ref, low_in_ref, g_low_ref, grad_ui, grad_do, io_sems = rest
    width = g_ref.shape[1]
    slope_copy = keep(slope_in, slope_ref, io_sems.at[1])
    low_in_copy = keep(low_in_in, low_in_ref, io_sems.at[2])
    act_copy = keep(act_in, act_ref, io_sems.at[0])
    g_low_out = dot(g_ref[...], uo_ref[...], 1, 1).astype(BF16)
    g_act = dot(g_low_out, do_ref[...], 1, 0)
    for c in range(CUTS if streamed else 1):
        at = cut(c, width) if streamed else slice(None)
        arrived(wo_hbm, wo_ref, c, (at,))
        g_act = g_act + dot(g_ref[:, at], wo_ref[at], 1, 0)
    slope_copy.wait()
    g_pre = (g_act * slope_ref[...]).astype(BF16)
    g_low_ref[...] = dot(ui_ref[...], g_pre, 1, 1).astype(BF16)
    copies = [keep(g_ref, g_out, io_sems.at[6]), keep(g_low_ref, g_low_out_ref, io_sems.at[3])]
    low_in_copy.wait()
    grad_ui[...] = dot(low_in_ref[...], g_pre, 0, 0)
    copies.append(keep(grad_ui, grad_ui_out, io_sems.at[4]))
    act_copy.wait()
    grad_do[...] = dot(g_low_out, act_ref[...], 0, 0)
    copies.append(keep(grad_do, grad_do_out, io_sems.at[5]))
    if not first:
        g_low_in = dot(g_pre, ui_ref[...], 1, 1).astype(BF16)
        for c in range(CUTS):
            at = (slice(None), cut(c, width))
            arrived(wi_hbm, wi_ref, CUTS + c, at)
            part = dot(g_pre, wi_ref[at], 1, 0) + dot(g_low_in, di_ref[at], 1, 0)
            part_ref[at] = part.astype(BF16)
    for copy in copies:
        copy.wait()


def block_cost(rows, width, cols, matmuls):
    return pl.CostEstimate(
        flops=2 * matmuls * rows * width * cols,
        bytes_accessed=2 * matmuls * width * cols,
        transcendentals=rows * cols,
    )


def in_vmem(*arrays):
    return [pltpu.with_memory_space_constraint(a, pltpu.VMEM) for a in arrays]


def block_forward(u, weights, low, own=None):
    rows, width = u.shape
    streamed, last = own is not None, len(weights) == 1
    rank, cols = low[1].shape
    kept = [((rows, cols), BF16), ((rows, cols), F32), ((rows, rank), BF16), ((rank, rows), BF16)]
    out = [shape_of(*s, dtype=t) for s, t in kept] + [shape_of(rows, width)]
    out += [] if last else [shape_of(rows, width + PAD)]
    stream_scratch = [
        pltpu.VMEM((width, cols), BF16),
        pltpu.VMEM((cols, width), BF16),
        pltpu.SemaphoreType.DMA((2 * CUTS,)),
    ]
    first_specs = [SMEM, VMEM] + [HBM] * 4 if streamed else [VMEM] * (1 + len(weights))
    return pl.pallas_call(
        functools.partial(forward_kernel, last=last, streamed=streamed),
        out_shape=out,
        in_specs=first_specs + [VMEM] * 3,
        out_specs=[HBM] * (len(kept) + 1) + ([] if last else [VMEM]),
        scratch_shapes=[
            *(pltpu.VMEM(s, t) for s, t in kept),
            pltpu.SemaphoreType.DMA((len(kept) + 1,)),
            *(stream_scratch if streamed else []),
        ],
        compiler_params=PARAMS,
        cost_estimate=block_cost(rows, width, cols, 1 if last else 2),
        name="block_forward",
    )(*((own, u, *in_hbm(*weights)) if streamed else (u, *in_vmem(*weights))), *low[:3])


def block_backward(g, acts, weights, low, streamed):
    rows, width = g.shape
    first = len(weights) == 1
    rank, cols = low[1].shape
    kept = [((rank, rows), BF16), ((rank, cols), F32), ((rank, cols), F32)]
    out = [shape_of(*s, dtype=t) for s, t in kept] + [shape_of(rows, width)]
    out += [] if first else [shape_of(rows, width)]
    act, slope, low_in = acts
    stream_scratch = [
        pltpu.VMEM((cols, width), BF16),
        pltpu.VMEM((width, cols), BF16),
        pltpu.SemaphoreType.DMA((2 * CUTS,)),
    ]
    return pl.pallas_call(
        functools.partial(backward_kernel, first=first, streamed=streamed),
        out_shape=out,
        in_specs=[VMEM] + [HBM] * 3 + [HBM if streamed else VMEM] * len(weights) + [VMEM] * 4,
        out_specs=[HBM] * (len(kept) + 1) + ([] if first else [VMEM]),
        scratch_shapes=[
            pltpu.VMEM((rows, cols), BF16),
            pltpu.VMEM((rows, cols), F32),
            pltpu.VMEM((rows, rank), BF16),
            *(pltpu.VMEM(s, t) for s, t in kept),
            pltpu.SemaphoreType.DMA((7,)),
            *(stream_scratch if streamed else []),
        ],
        compiler_params=PARAMS,
        cost_estimate=block_cost(rows, width, cols, len(weights)),
        name="block_backward",
    )(g, slope, act, low_in, *(in_hbm if streamed else in_vmem)(*weights), *low)


def ready_kernel(flag_ref, *refs, order):
    if order:
        ordered, wi_buf, wo_buf, buf_sems = refs[8:12], *refs[-3:]
        refs = refs[:8] + refs[12:-3]

        @pl.when(flag_ref[2] == 1)
        def _():
            order_weights(flag_ref, refs[:4], ordered, (wi_buf, wo_buf), buf_sems)

    turn_weights(flag_ref, *refs)


def order_weights(flag_ref, refs, outs, bufs, sems):
    sources = ((refs[0], refs[1], bufs[0]), (refs[2], refs[3], bufs[1]))
    for i in range(2):
        for k, (ours, theirs, buf) in enumerate(sources):
            if i:
                pltpu.make_async_copy(buf, outs[k], sems.at[2 + k]).wait()
            fetch(flag_ref[1] == i, ours, theirs, buf, sems.at[k])
        for k, (ours, theirs, buf) in enumerate(sources):
            pltpu.make_async_copy(ours, buf, sems.at[k]).wait()
            pltpu.make_async_copy(buf, outs[2 * i + k], sems.at[2 + k]).start()
    for k, (ours, theirs, buf) in enumerate(sources):
        pltpu.make_async_copy(buf, outs[2 + k], sems.at[2 + k]).wait()


def turn_weights(flag_ref, *refs):
    narrow_buf, wide_buf, in_sems, out_sems = refs[-4:]
    outs, sources = refs[-8:-4], refs[:4]
    step = narrow_buf.shape[1]

    def turn(own, ours, theirs, target, in_buf, out_buf, by_rows):
        count = ours.shape[0 if by_rows else 1] // step

        def cut_of(ref, c, rows):
            at = pl.ds(pl.multiple_of(c * step, step), step)
            return ref.at[at] if rows else ref.at[:, at]

        def come(c):
            slot = lax.rem(c, 2)
            source, other = (cut_of(ref, c, by_rows) for ref in (ours, theirs))
            fetch(own, source, other, in_buf.at[slot], in_sems.at[slot])

        def going(c, slot):
            target_cut = cut_of(target, c, not by_rows)
            return pltpu.make_async_copy(out_buf.at[slot], target_cut, out_sems.at[slot])

        come(0)

        def body(c, carry):
            slot = lax.rem(c, 2)

            @pl.when(c + 1 < count)
            def _():
                come(c + 1)

            source = cut_of(ours, c, by_rows)
            pltpu.make_async_copy(source, in_buf.at[slot], in_sems.at[slot]).wait()

            @pl.when(c >= 2)
            def _():
                going(c - 2, slot).wait()

            out_buf[slot] = in_buf[slot].T
            going(c, slot).start()
            return carry

        lax.fori_loop(0, count, body, 0)
        going(count - 2, count % 2).wait()
        going(count - 1, 1 - count % 2).wait()

    @pl.when(flag_ref[0] == 1)
    def _():
        for i in range(2):
            own = flag_ref[1] == i
            turn(own, *sources[:2], outs[2 * i], narrow_buf, wide_buf, True)
            turn(own, *sources[2:], outs[2 * i + 1], wide_buf, narrow_buf, False)


def ready_weights(flag, weights, held):
    width, cols = weights[0].shape
    step = 384
    turned = [shape_of(cols, width), shape_of(width, cols)] * 2
    ordered = [] if held else [shape_of(width, cols), shape_of(cols, width)] * 2
    buffers = [
        pltpu.VMEM((width, cols), BF16),
        pltpu.VMEM((cols, width), BF16),
        pltpu.SemaphoreType.DMA((4,)),
    ]
    out = pl.pallas_call(
        functools.partial(ready_kernel, order=not held),
        out_shape=turned + ordered,
        in_specs=[SMEM] + [HBM] * (4 + len(held)),
        out_specs=[HBM] * (4 + len(ordered)),
        scratch_shapes=[
            pltpu.VMEM((2, step, cols), BF16),
            pltpu.VMEM((2, cols, step), BF16),
            pltpu.SemaphoreType.DMA((2,)),
            pltpu.SemaphoreType.DMA((2,)),
            *([] if held else buffers),
        ],
        input_output_aliases={5 + k: k for k in range(len(held))},
        compiler_params=PARAMS,
        name="ready_weights",
    )(flag, *in_hbm(*weights), *held)
    return tuple(out[:4]), tuple(out[4:])


def summed(got_ref, own_rows, at):
    total = None
    for k in range(0, got_ref.shape[0], PAIR):
        part = got_ref[k : k + PAIR, at].astype(F32)
        part = part.reshape(PAIR // own_rows, own_rows, part.shape[1]).sum(0)
        total = part if total is None else total + part
    return total


def spread(out_ref, rows):
    pair = jnp.concatenate([rows] * (PAIR // rows.shape[0]), axis=0).astype(BF16)
    for k in range(0, out_ref.shape[0], PAIR):
        out_ref[k : k + PAIR] = pair


def modulated(wide, mod_ref):
    return rms_stats(wide)[0] * (1.0 + mod_ref[1:2]) + mod_ref[0:1]


def first_rows_kernel(ids_ref, counts_ref, x_ref, e_ref, out_ref, x_out, e_out, mask_out):
    at_start, core, tp_pos = ids_ref[0], ids_ref[1], ids_ref[2]
    own_rows = x_ref.shape[1]
    row = tp_pos * own_rows + lax.broadcasted_iota(jnp.int32, (own_rows, 1), 0)
    mask = (row < counts_ref[core]).astype(F32)
    mask_out[...] = mask
    x = x_ref[core].astype(F32) * mask
    e = e_ref[core].astype(F32) * mask
    x_out[...] = x.astype(BF16)
    e_out[...] = e.astype(BF16)
    spread(out_ref, jnp.where(at_start == 1, x, e))


def modulate_kernel(x_ref, mod_ref, out_ref):
    out_ref[...] = modulated(x_ref[...].astype(F32), mod_ref).astype(BF16)


def gate_kernel(e_ref, mod_ref, out_ref):
    out_ref[...] = (mod_ref[2:3] * e_ref[...].astype(F32)).astype(BF16)


def pack_kernel(ids_ref, jobs_ref, *refs):
    sources, ours, theirs, sems = refs[:-3], refs[-3], refs[-2], refs[-1]
    core = ids_ref[1]
    copies = []
    for n, (job, out) in enumerate(((jobs_ref[core], ours), (jobs_ref[1 - core], theirs))):
        start = 0
        for k, source in enumerate(sources):
            at = pl.ds(start, source.shape[2])
            copies.append(keep(source.at[job], out.at[:, at], sems.at[n * len(sources) + k]))
            start += source.shape[2]
    for copy in copies:
        copy.wait()


def rows_in_kernel(x_ref, mod_ref, out_ref):
    spread(out_ref, modulated(x_ref[...].astype(F32), mod_ref))


def gate_rows_kernel(e_ref, mod_ref, out_ref):
    spread(out_ref, mod_ref[2:3] * e_ref[...].astype(F32))


def forward_rows_kernel(got_ref, x_ref, mask_ref, mod_ref, uo_ref, next_ref, x_out, *outs):
    own_rows, width = x_ref.shape
    rank = uo_ref.shape[0]
    low = summed(got_ref, own_rows, pl.ds(width, PAD)).astype(BF16)[:, :rank]
    branch = summed(got_ref, own_rows, pl.ds(0, width)) + dot(low, uo_ref[...], 1, 0)
    x = x_ref[...].astype(F32) + mod_ref[2:3] * branch * mask_ref[...]
    x = x.astype(BF16)
    x_out[...] = x
    if outs:
        x_saved, spread_out = outs
        x_saved[...] = x_ref[...]
        spread(spread_out, modulated(x.astype(F32), next_ref))


def backward_rows_kernel(got_ref, e_ref, x_ref, mod_ref, next_ref, e_out, *spread_out):
    own_rows, width = x_ref.shape
    normed, inv_rms = rms_stats(x_ref[...].astype(F32))
    q = summed(got_ref, own_rows, pl.ds(0, width)) * (1.0 + mod_ref[1:2])
    mean = jnp.mean(q * normed, axis=-1, keepdims=True)
    e = (e_ref[...].astype(F32) + inv_rms * (q - normed * mean)).astype(BF16)
    e_out[...] = e
    for out_ref in spread_out:
        spread(out_ref, next_ref[2:3] * e.astype(F32))


def narrow_kernel(*refs):
    parts, out_ref = refs[:-1], refs[-1]
    rows = jnp.concatenate([part[...].astype(F32) for part in parts], axis=0).astype(BF16)
    for k in range(0, out_ref.shape[0], rows.shape[0]):
        out_ref[k : k + rows.shape[0]] = rows


def gradients_kernel(ids_ref, got_ref, *refs):
    per_block, (ours, theirs) = refs[:8], refs[8:]
    rank, cols = per_block[2].shape
    width = per_block[0].shape[1]
    deep = 4 * rank
    total = None
    for k in range(0, got_ref.shape[0], deep):
        part = got_ref[k : k + deep].astype(F32)
        total = part if total is None else total + part
    for i in range(2):
        g_ref, u_ref, ui_ref, do_ref = per_block[4 * i : 4 * i + 4]
        low_out = total[i * rank : (i + 1) * rank].astype(BF16)
        g_low = total[(2 + i) * rank : (3 + i) * rank]
        high = g_low.astype(BF16)
        rest = (g_low - high.astype(F32)).astype(BF16)
        grads = (
            dot(high, u_ref[...], 1, 0) + dot(rest, u_ref[...], 1, 0),
            ui_ref[...],
            do_ref[...],
            dot(low_out, g_ref[...], 1, 0),
        )

        def put(out, grads=grads):
            start = 0
            for grad in grads:
                out[:, start : start + grad.shape[1]] = grad
                start += grad.shape[1]

        pl.when(ids_ref[1] == i)(functools.partial(put, ours))
        pl.when(ids_ref[1] != i)(functools.partial(put, theirs))


def by_job_kernel(ids_ref, jobs_ref, ours, theirs, di_ref, ui_ref, do_ref, uo_ref):
    core, tp_pos = ids_ref[1], ids_ref[2]
    owners, _, width = di_ref.shape
    cols = ui_ref.shape[2]
    for out in (di_ref, ui_ref, do_ref, uo_ref):
        out[...] = jnp.zeros(out.shape, F32)
    for job, grads in ((jobs_ref[core], ours), (jobs_ref[1 - core], theirs)):
        ui_ref[job] += grads[:, width : width + cols]
        do_ref[job] += grads[:, width + cols : width + 2 * cols]
        place = job - tp_pos * owners

        def owned(place=place, grads=grads):
            di_ref[place] += grads[:, :width]
            uo_ref[place] += grads[:, width + 2 * cols :]

        pl.when((place >= 0) & (place < owners))(owned)


def rows_call(kernel, out, *operands, scalars=0, cost=None):
    return pl.pallas_call(
        kernel,
        out_shape=out,
        in_specs=[SMEM] * scalars + [VMEM] * (len(operands) - scalars),
        out_specs=jax.tree.map(lambda _: VMEM, out),
        compiler_params=PARAMS,
        cost_estimate=cost,
        name=kernel.__name__,
    )(*operands)


def exchanged(parts, tp):
    rows, width = parts.shape
    got = lax.all_to_all(parts.reshape(tp, rows // tp, width), "tp", 0, 0)
    return got.reshape(rows, width)


def shards(
    latents,
    cotangent,
    token_counts,
    job_ids,
    modulation,
    w_in,
    w_out,
    down_in,
    up_in,
    down_out,
    up_out,
):
    tp = lax.axis_size("tp")
    segments = lax.axis_size("segment")
    planes = segments // 2
    seg = lax.axis_index("segment")
    plane, core = seg // 2, seg % 2
    tp_pos = lax.axis_index("tp")
    micro, own_rows, width = latents.shape
    cols = w_in.shape[2]
    jobs, rank = down_in.shape[1], down_in.shape[2]
    rows = own_rows * tp
    swap = [(s, s ^ 1) for s in range(segments)]
    onward = [(s, (s + 2) % segments) for s in range(segments)]
    back = [(d, s) for s, d in onward]
    last_plane = planes - 1

    ids = jnp.stack([(plane == 0).astype(jnp.int32), core, tp_pos]).astype(jnp.int32)
    full = shape_of(rows, width)
    some = shape_of(own_rows, width)
    w_first = (w_in[0], lax.ppermute(w_in[0], "segment", swap))
    w_second = (w_out[0], lax.ppermute(w_out[0], "segment", swap))

    ends, x, e_last, mask = rows_call(
        first_rows_kernel,
        [full, some, some, shape_of(own_rows, 1, dtype=F32)],
        ids,
        token_counts,
        latents,
        cotangent,
        scalars=2,
    )
    ends, ids, mod = lax.optimization_barrier((ends, ids, modulation[0]))
    mod_other = lax.ppermute(mod, "segment", swap)
    mods = [jnp.where(core == i, mod, mod_other)[core] for i in range(2)]

    adapters = [a[0] for a in (down_in, up_in, down_out, up_out)]
    packed = shape_of(rank, sum(a.shape[2] for a in adapters))
    low_own, low_sent = pl.pallas_call(
        pack_kernel,
        out_shape=[packed, packed],
        in_specs=[SMEM, SMEM] + [HBM] * len(adapters),
        out_specs=[VMEM, VMEM],
        scratch_shapes=[pltpu.SemaphoreType.DMA((2 * len(adapters),))],
        compiler_params=PARAMS,
        cost_estimate=pl.CostEstimate(
            flops=0, bytes_accessed=4 * math.prod(packed.shape), transcendentals=0
        ),
        name="pack_kernel",
    )(ids, job_ids, *in_hbm(*adapters))
    low_other = lax.ppermute(low_sent, "segment", swap)
    cuts = (width, width + cols, width + 2 * cols)
    lows = [
        jnp.split(jnp.where(core == i, low_own, low_other), cuts, axis=1) for i in range(2)
    ]

    ends = exchanged(ends, tp)
    ahead = pl.CostEstimate(
        flops=16 * rows * width * cols, bytes_accessed=16 * width * cols, transcendentals=rows * width
    )
    owns = [(core == i).astype(jnp.int32).reshape(1) for i in range(2)]
    flag = jnp.stack([plane >= planes // 2, core, plane > 0]).astype(jnp.int32)
    ends, flag = lax.optimization_barrier((ends, flag))
    (turned, ordered), x = lax.optimization_barrier(
        (ready_weights(flag, (*w_first, *w_second), ()), x)
    )

    def forward_plane(x, ordered, p):
        saved = []
        for i in range(2):
            if i:
                u = exchanged(sent, tp)
            elif p == 0:
                u = rows_call(modulate_kernel, full, ends, mods[0])
            else:
                u = exchanged(rows_call(rows_in_kernel, full, x, mods[0], cost=ahead), tp)
            last = p == last_plane and i == 1
            if p == 0:
                done = block_forward(u, (*w_first, *w_second), lows[i], owns[i])
            else:
                pair = ordered[2 * i : 2 * i + 2]
                done = block_forward(u, pair[:1] if last else pair, lows[i])
            act, slope, low_in, low_part, u, *part = done
            kept = (u, (act, slope, low_in), low_part)
            if last:
                saved.append((x, *kept))
                break
            got = exchanged(part[0], tp)
            if i == 0:
                x_next, x, sent = rows_call(
                    forward_rows_kernel,
                    [some, some, full],
                    got,
                    x,
                    mask,
                    mods[0],
                    lows[0][3],
                    mods[1],
                )
            else:
                (x_next,) = rows_call(
                    forward_rows_kernel, [some], got, x, mask, mods[1], lows[1][3], mods[1]
                )
            saved.append((x, *kept))
            x = x_next
        return x, tuple(saved)

    def backward_plane(e, saved, turned, p):
        kept = [None, None]
        for i in (1, 0):
            if i == 0:
                g = exchanged(sent, tp)
            elif p == last_plane:
                g = rows_call(gate_kernel, full, ends, mods[1])
            else:
                g = exchanged(rows_call(gate_rows_kernel, full, e, mods[1], cost=ahead), tp)
            x, u, acts, low_part = saved[i]
            first = p == 0 and i == 0
            w_in_t, w_out_t = turned[2 * i : 2 * i + 2]
            g_low_in, grad_ui, grad_do, g, *part = block_backward(
                g, acts, [w_out_t] if first else [w_out_t, w_in_t], lows[i], False
            )
            kept[i] = (g, g_low_in, grad_ui, grad_do)
            if first:
                break
            got = exchanged(part[0], tp)
            out = [some, full] if i else [some]
            e, *sent = rows_call(backward_rows_kernel, out, got, e, x, mods[i], mods[0])
            sent = sent[0] if sent else None
        return e, tuple(kept)

    def zeros(*shape, dtype=BF16):
        return jnp.zeros(shape, dtype)

    def no_saved():
        acts = (zeros(rows, cols), zeros(rows, cols, dtype=F32), zeros(rows, rank))
        return (zeros(own_rows, width), zeros(rows, width), acts, zeros(rank, rows))

    def no_kept():
        return (
            zeros(rows, width),
            zeros(rank, rows),
            zeros(rank, cols, dtype=F32),
            zeros(rank, cols, dtype=F32),
        )

    saved = (no_saved(), no_saved())
    kept = (no_kept(), no_kept())
    for p in range(last_plane):
        x, saved = lax.cond(
            plane == p,
            lambda x, saved: forward_plane(x, ordered, p),
            lambda x, saved: (x, saved),
            x,
            saved,
        )
        x = lax.ppermute(x, "segment", onward)
        if p == planes // 2 - 1:
            flag = jnp.stack([plane < planes // 2, core]).astype(jnp.int32)
            (turned, _), x = lax.optimization_barrier(
                (ready_weights(flag, (*w_first, *w_second), turned), x)
            )

    def turn(x, saved, kept):
        x, saved = forward_plane(x, ordered, last_plane)
        e, kept = backward_plane(e_last, saved, turned, last_plane)
        return e, saved, kept

    e, saved, kept = lax.cond(
        plane == last_plane, turn, lambda x, saved, kept: (x, saved, kept), x, saved, kept
    )
    for p in range(last_plane - 1, -1, -1):
        e = lax.ppermute(e, "segment", back)
        e, kept = lax.cond(
            plane == p,
            lambda e, saved, kept: backward_plane(e, saved, turned, p),
            lambda e, saved, kept: (e, kept),
            e,
            saved,
            kept,
        )

    narrow = (saved[0][3], saved[1][3], kept[0][1], kept[1][1])
    narrow_out = shape_of(tp * 4 * rank, rows)
    got = exchanged(rows_call(narrow_kernel, narrow_out, *narrow, cost=ahead), tp)
    wide = [shape_of(*packed.shape, dtype=F32)] * 2
    per_block = [(*in_vmem(kept[i][0], saved[i][1]), kept[i][2], kept[i][3]) for i in range(2)]
    mine, sent = rows_call(
        gradients_kernel, wide, ids, got, *per_block[0], *per_block[1], scalars=1
    )
    theirs = lax.ppermute(sent, "segment", swap)
    owned = shape_of(jobs // tp, rank, width, dtype=F32)
    split = shape_of(jobs, rank, cols, dtype=F32)
    grads = rows_call(
        by_job_kernel, [owned, split, split, owned], ids, job_ids, mine, theirs, scalars=2
    )
    return tuple(grad[None] for grad in grads)


def solution(mesh):
    return jax.shard_map(
        shards,
        mesh=mesh,
        in_specs=(
            P(None, "tp", None),
            P(None, "tp", None),
            P(),
            P(),
            P("segment", None, None, None),
            P("segment", None, "tp"),
            P("segment", "tp", None),
            P("segment", None, None, None),
            P("segment", None, None, "tp"),
            P("segment", None, None, "tp"),
            P("segment", None, None, None),
        ),
        out_specs=(
            P("segment", "tp", None, None),
            P("segment", None, None, "tp"),
            P("segment", None, None, "tp"),
            P("segment", "tp", None, None),
        ),
        check_vma=False,
    )
```

```python
import functools
import math

import jax
import jax.numpy as jnp
from jax import lax
from jax.experimental import pallas as pl
from jax.experimental.pallas import tpu as pltpu
from jax.sharding import PartitionSpec as P

EPS = 1e-06
ROOT_TWO_PI = math.sqrt(2.0 / math.pi)
F32 = jnp.float32
BF16 = jnp.bfloat16
PAD = 128
CUTS = 2
PARTS = 4
PAIR = 16
CROSSED = (0, 1, 0, 1)
STAGGERED = 0
VMEM = pl.BlockSpec(memory_space=pltpu.VMEM)
HBM = pl.BlockSpec(memory_space=pltpu.HBM)
SMEM = pl.BlockSpec(memory_space=pltpu.SMEM)
PARAMS = pltpu.CompilerParams(vmem_limit_bytes=16 * 1024 * 1024)


def shape_of(*shape, dtype=BF16):
    return jax.ShapeDtypeStruct(shape, dtype)


def gelu_and_slope(values):
    inner = ROOT_TWO_PI * (values + 0.044715 * values * values * values)
    tangent = jnp.tanh(inner)
    half = 0.5 * (1.0 + tangent)
    slope = half + 0.5 * values * (1.0 - tangent * tangent) * ROOT_TWO_PI * (
        1.0 + 3.0 * 0.044715 * values * values
    )
    return values * half, slope


def rms_stats(wide):
    inv_rms = lax.rsqrt(jnp.mean(wide * wide, axis=-1, keepdims=True) + EPS)
    return wide * inv_rms, inv_rms


def dot(a, b, a_dim, b_dim):
    return lax.dot_general(a, b, (((a_dim,), (b_dim,)), ((), ())), preferred_element_type=F32)


def fetch(own, ours, theirs, buf, sem):
    @pl.when(own)
    def _():
        pltpu.make_async_copy(ours, buf, sem).start()

    @pl.when(jnp.logical_not(own))
    def _():
        pltpu.make_async_copy(theirs, buf, sem).start()


def cut(c, size, parts=CUTS):
    return pl.ds(c * (size // parts), size // parts)


def keep(buf, out, sem):
    copy = pltpu.make_async_copy(buf, out, sem)
    copy.start()
    return copy


def in_hbm(*arrays):
    return [pltpu.with_memory_space_constraint(a, pltpu.HBM) for a in arrays]


def forward_kernel(*refs, last, streamed):
    if streamed:
        own_ref, u_ref, wi_own, wi_other, wo_own, wo_other, *refs = refs
        wi_ref, wo_ref, w_sems = refs[-3:]
        refs = refs[:-3]
        width = u_ref.shape[1]
        for c in range(CUTS):
            at = (cut(c, width),)
            fetch(own_ref[0] == 1, wi_own.at[at], wi_other.at[at], wi_ref.at[at], w_sems.at[c])
        for c in range(CUTS):
            at = (slice(None), cut(c, width))
            fetch(
                own_ref[0] == 1, wo_own.at[at], wo_other.at[at], wo_ref.at[at], w_sems.at[CUTS + c]
            )
    else:
        u_ref, wi_ref, *refs = refs
        wo_ref, refs = (None, refs) if last else (refs[0], refs[1:])

    def arrived(source, held, n, at):
        if streamed:
            pltpu.make_async_copy(source.at[at], held.at[at], w_sems.at[n]).wait()

    wi_own, wo_own = (wi_own, wo_own) if streamed else (None, None)
    di_ref, ui_ref, do_ref, act_out, slope_out, low_in_out, low_out, u_out, *rest = refs
    sent_ref, rest = (None, rest) if last else (rest[0], rest[1:])
    act_ref, slope_ref, low_in_ref, low_ref, out_sems = rest
    width, rank = u_ref.shape[1], di_ref.shape[0]
    low_in = dot(u_ref[...], di_ref[...], 1, 1).astype(BF16)
    low_in_ref[...] = low_in
    copies = [keep(u_ref, u_out, out_sems.at[4]), keep(low_in_ref, low_in_out, out_sems.at[0])]
    pre = dot(low_in, ui_ref[...], 1, 0)
    for c in range(CUTS if streamed else 1):
        at = cut(c, width) if streamed else slice(None)
        arrived(wi_own, wi_ref, c, (at,))
        pre = pre + dot(u_ref[:, at], wi_ref[at], 1, 0)
    act, slope = gelu_and_slope(pre)
    act = act.astype(BF16)
    act_ref[...] = act
    slope_ref[...] = slope
    copies.append(keep(act_ref, act_out, out_sems.at[1]))
    copies.append(keep(slope_ref, slope_out, out_sems.at[2]))
    low_ref[...] = dot(do_ref[...], act, 1, 1).astype(BF16)
    copies.append(keep(low_ref, low_out, out_sems.at[3]))
    if not last:
        sent_ref[:, width:] = jnp.zeros((sent_ref.shape[0], PAD), BF16)
        sent_ref[:, width : width + rank] = dot(act, do_ref[...], 1, 1).astype(BF16)
        for c in range(CUTS):
            at = cut(c, width)
            arrived(wo_own, wo_ref, CUTS + c, (slice(None), at))
            sent_ref[:, at] = dot(act, wo_ref[:, at], 1, 0).astype(BF16)
    for copy in copies:
        copy.wait()


def backward_kernel(*refs, first, streamed):
    if streamed:
        wi_ref, wo_ref, w_sems = refs[-3:]
        g_ref, slope_in, act_in, low_in_in, wo_hbm, wi_hbm, *refs = refs[:-3]
        width = g_ref.shape[1]
        for c in range(CUTS):
            at = (cut(c, width),)
            pltpu.make_async_copy(wo_hbm.at[at], wo_ref.at[at], w_sems.at[c]).start()
        for c in range(CUTS):
            at = (slice(None), cut(c, width))
            pltpu.make_async_copy(wi_hbm.at[at], wi_ref.at[at], w_sems.at[CUTS + c]).start()
    else:
        wi_hbm = wo_hbm = None
        g_ref, slope_in, act_in, low_in_in, wo_ref, *refs = refs
        wi_ref, refs = (None, refs) if first else (refs[0], refs[1:])

    def arrived(source, held, n, at):
        if streamed:
            pltpu.make_async_copy(source.at[at], held.at[at], w_sems.at[n]).wait()

    di_ref, ui_ref, do_ref, uo_ref, g_low_out_ref, grad_ui_out, grad_do_out, g_out, *rest = refs
    part_ref, rest = (None, rest) if first else (rest[0], rest[1:])
    act_ref, slope_ref, low_in_ref, g_low_ref, grad_ui, grad_do, io_sems = rest
    width = g_ref.shape[1]
    slope_copy = keep(slope_in, slope_ref, io_sems.at[1])
    low_in_copy = keep(low_in_in, low_in_ref, io_sems.at[2])
    act_copy = keep(act_in, act_ref, io_sems.at[0])
    g_copy = keep(g_ref, g_out, io_sems.at[6])
    g_low_out = dot(g_ref[...], uo_ref[...], 1, 1).astype(BF16)
    g_act = dot(g_low_out, do_ref[...], 1, 0)
    for c in range(CUTS if streamed else 1):
        at = cut(c, width) if streamed else slice(None)
        arrived(wo_hbm, wo_ref, c, (at,))
        g_act = g_act + dot(g_ref[:, at], wo_ref[at], 1, 0)
    slope_copy.wait()
    g_pre = (g_act * slope_ref[...]).astype(BF16)
    g_low_ref[...] = dot(ui_ref[...], g_pre, 1, 1).astype(BF16)
    copies = [g_copy, keep(g_low_ref, g_low_out_ref, io_sems.at[3])]
    low_in_copy.wait()
    grad_ui[...] = dot(low_in_ref[...], g_pre, 0, 0)
    copies.append(keep(grad_ui, grad_ui_out, io_sems.at[4]))
    act_copy.wait()
    grad_do[...] = dot(g_low_out, act_ref[...], 0, 0)
    copies.append(keep(grad_do, grad_do_out, io_sems.at[5]))
    if not first:
        g_low_in = dot(g_pre, ui_ref[...], 1, 1).astype(BF16)
        for c in range(CUTS if streamed else PARTS):
            at = (slice(None), cut(c, width, CUTS if streamed else PARTS))
            arrived(wi_hbm, wi_ref, CUTS + c, at)
            part = dot(g_pre, wi_ref[at], 1, 0) + dot(g_low_in, di_ref[at], 1, 0)
            part_ref[at] = part.astype(BF16)
    for copy in copies:
        copy.wait()


def block_cost(rows, width, cols, matmuls):
    return pl.CostEstimate(
        flops=2 * matmuls * rows * width * cols,
        bytes_accessed=2 * matmuls * width * cols,
        transcendentals=rows * cols,
    )


def in_vmem(*arrays):
    return [pltpu.with_memory_space_constraint(a, pltpu.VMEM) for a in arrays]


def block_forward(u, weights, low, own=None):
    rows, width = u.shape
    streamed, last = own is not None, len(weights) == 1
    rank, cols = low[1].shape
    kept = [((rows, cols), BF16), ((rows, cols), F32), ((rows, rank), BF16), ((rank, rows), BF16)]
    out = [shape_of(*s, dtype=t) for s, t in kept] + [shape_of(rows, width)]
    out += [] if last else [shape_of(rows, width + PAD)]
    stream_scratch = [
        pltpu.VMEM((width, cols), BF16),
        pltpu.VMEM((cols, width), BF16),
        pltpu.SemaphoreType.DMA((2 * CUTS,)),
    ]
    first_specs = [SMEM, VMEM] + [HBM] * 4 if streamed else [VMEM] * (1 + len(weights))
    return pl.pallas_call(
        functools.partial(forward_kernel, last=last, streamed=streamed),
        out_shape=out,
        in_specs=first_specs + [VMEM] * 3,
        out_specs=[HBM] * (len(kept) + 1) + ([] if last else [VMEM]),
        scratch_shapes=[
            *(pltpu.VMEM(s, t) for s, t in kept),
            pltpu.SemaphoreType.DMA((len(kept) + 1,)),
            *(stream_scratch if streamed else []),
        ],
        compiler_params=PARAMS,
        cost_estimate=block_cost(rows, width, cols, 1 if last else 2),
        name="block_forward",
    )(*((own, u, *in_hbm(*weights)) if streamed else (u, *in_vmem(*weights))), *low[:3])


def block_backward(g, acts, weights, low, streamed):
    rows, width = g.shape
    first = len(weights) == 1
    rank, cols = low[1].shape
    kept = [((rank, rows), BF16), ((rank, cols), F32), ((rank, cols), F32)]
    out = [shape_of(*s, dtype=t) for s, t in kept] + [shape_of(rows, width)]
    out += [] if first else [shape_of(rows, width)]
    act, slope, low_in = acts
    stream_scratch = [
        pltpu.VMEM((cols, width), BF16),
        pltpu.VMEM((width, cols), BF16),
        pltpu.SemaphoreType.DMA((2 * CUTS,)),
    ]
    return pl.pallas_call(
        functools.partial(backward_kernel, first=first, streamed=streamed),
        out_shape=out,
        in_specs=[VMEM] + [HBM] * 3 + [HBM if streamed else VMEM] * len(weights) + [VMEM] * 4,
        out_specs=[HBM] * (len(kept) + 1) + ([] if first else [VMEM]),
        scratch_shapes=[
            pltpu.VMEM((rows, cols), BF16),
            pltpu.VMEM((rows, cols), F32),
            pltpu.VMEM((rows, rank), BF16),
            *(pltpu.VMEM(s, t) for s, t in kept),
            pltpu.SemaphoreType.DMA((7,)),
            *(stream_scratch if streamed else []),
        ],
        compiler_params=PARAMS,
        cost_estimate=block_cost(rows, width, cols, len(weights)),
        name="block_backward",
    )(g, slope, act, low_in, *(in_hbm if streamed else in_vmem)(*weights), *low)


def ready_kernel(flag_ref, *refs, order):
    if order:
        ordered, wi_buf, wo_buf, buf_sems = refs[8:12], *refs[-3:]
        refs = refs[:8] + refs[12:-3]

        @pl.when(flag_ref[5] == 1)
        def _():
            order_weights(flag_ref, refs[:4], ordered, (wi_buf, wo_buf), buf_sems)

    turn_weights(flag_ref, *refs)


def order_weights(flag_ref, refs, outs, bufs, sems):
    sources = ((refs[0], refs[1], bufs[0]), (refs[2], refs[3], bufs[1]))
    for i in range(2):
        for k, (ours, theirs, buf) in enumerate(sources):
            if i:
                pltpu.make_async_copy(buf, outs[k], sems.at[2 + k]).wait()
            fetch(flag_ref[0] == i, ours, theirs, buf, sems.at[k])
        for k, (ours, theirs, buf) in enumerate(sources):
            pltpu.make_async_copy(ours, buf, sems.at[k]).wait()
            pltpu.make_async_copy(buf, outs[2 * i + k], sems.at[2 + k]).start()
    for k, (ours, theirs, buf) in enumerate(sources):
        pltpu.make_async_copy(buf, outs[2 + k], sems.at[2 + k]).wait()


def turn_weights(flag_ref, *refs):
    narrow_buf, wide_buf, in_sems, out_sems = refs[-4:]
    outs, sources = refs[-8:-4], refs[:4]
    step = narrow_buf.shape[1]

    def turn(own, ours, theirs, target, in_buf, out_buf, by_rows):
        count = ours.shape[0 if by_rows else 1] // step

        def cut_of(ref, c, rows):
            at = pl.ds(pl.multiple_of(c * step, step), step)
            return ref.at[at] if rows else ref.at[:, at]

        def come(c):
            slot = lax.rem(c, 2)
            source, other = (cut_of(ref, c, by_rows) for ref in (ours, theirs))
            fetch(own, source, other, in_buf.at[slot], in_sems.at[slot])

        def going(c, slot):
            target_cut = cut_of(target, c, not by_rows)
            return pltpu.make_async_copy(out_buf.at[slot], target_cut, out_sems.at[slot])

        come(0)

        def body(c, carry):
            slot = lax.rem(c, 2)

            @pl.when(c + 1 < count)
            def _():
                come(c + 1)

            source = cut_of(ours, c, by_rows)
            pltpu.make_async_copy(source, in_buf.at[slot], in_sems.at[slot]).wait()

            @pl.when(c >= 2)
            def _():
                going(c - 2, slot).wait()

            out_buf[slot] = in_buf[slot].T
            going(c, slot).start()
            return carry

        lax.fori_loop(0, count, body, 0)
        going(count - 2, count % 2).wait()
        going(count - 1, 1 - count % 2).wait()

    for i in range(2):
        own = flag_ref[0] == i
        into = functools.partial(turn, own, *sources[:2], outs[2 * i], narrow_buf, wide_buf, True)
        pl.when(flag_ref[1 + 2 * i] == 1)(into)
        out = functools.partial(
            turn, own, *sources[2:], outs[2 * i + 1], wide_buf, narrow_buf, False
        )
        pl.when(flag_ref[2 + 2 * i] == 1)(out)


def ready_weights(flag, weights, held):
    width, cols = weights[0].shape
    step = 384
    turned = [shape_of(cols, width), shape_of(width, cols)] * 2
    ordered = [] if held else [shape_of(width, cols), shape_of(cols, width)] * 2
    buffers = [
        pltpu.VMEM((width, cols), BF16),
        pltpu.VMEM((cols, width), BF16),
        pltpu.SemaphoreType.DMA((4,)),
    ]
    out = pl.pallas_call(
        functools.partial(ready_kernel, order=not held),
        out_shape=turned + ordered,
        in_specs=[SMEM] + [HBM] * (4 + len(held)),
        out_specs=[HBM] * (4 + len(ordered)),
        scratch_shapes=[
            pltpu.VMEM((2, step, cols), BF16),
            pltpu.VMEM((2, cols, step), BF16),
            pltpu.SemaphoreType.DMA((2,)),
            pltpu.SemaphoreType.DMA((2,)),
            *([] if held else buffers),
        ],
        input_output_aliases={5 + k: k for k in range(len(held))},
        compiler_params=PARAMS,
        name="ready_weights",
    )(flag, *in_hbm(*weights), *held)
    return tuple(out[:4]), tuple(out[4:])


def summed(got_ref, own_rows, at):
    total = None
    for k in range(0, got_ref.shape[0], PAIR):
        part = got_ref[k : k + PAIR, at].astype(F32)
        part = part.reshape(PAIR // own_rows, own_rows, part.shape[1]).sum(0)
        total = part if total is None else total + part
    return total


def spread(out_ref, rows):
    pair = jnp.concatenate([rows] * (PAIR // rows.shape[0]), axis=0).astype(BF16)
    for k in range(0, out_ref.shape[0], PAIR):
        out_ref[k : k + PAIR] = pair


def modulated(wide, mod_ref):
    return rms_stats(wide)[0] * (1.0 + mod_ref[1:2]) + mod_ref[0:1]


def first_rows_kernel(ids_ref, counts_ref, x_ref, e_ref, out_ref, x_out, e_out, mask_out):
    at_start, tp_pos, mb = ids_ref[0], ids_ref[2], ids_ref[3]
    own_rows = x_ref.shape[1]
    row = tp_pos * own_rows + lax.broadcasted_iota(jnp.int32, (own_rows, 1), 0)
    mask = (row < counts_ref[mb]).astype(F32)
    mask_out[...] = mask
    x = x_ref[mb].astype(F32) * mask
    e = e_ref[mb].astype(F32) * mask
    x_out[...] = x.astype(BF16)
    e_out[...] = e.astype(BF16)
    spread(out_ref, jnp.where(at_start == 1, x, e))


def modulate_kernel(x_ref, mod_ref, out_ref):
    out_ref[...] = modulated(x_ref[...].astype(F32), mod_ref).astype(BF16)


def gate_kernel(e_ref, mod_ref, out_ref):
    out_ref[...] = (mod_ref[2:3] * e_ref[...].astype(F32)).astype(BF16)


def pack_kernel(ids_ref, jobs_ref, *refs):
    sources, ours, theirs, sems = refs[:-3], refs[-3], refs[-2], refs[-1]
    mb = ids_ref[3]
    copies = []
    for n, (job, out) in enumerate(((jobs_ref[mb], ours), (jobs_ref[1 - mb], theirs))):
        start = 0
        for k, source in enumerate(sources):
            at = pl.ds(start, source.shape[2])
            copies.append(keep(source.at[job], out.at[:, at], sems.at[n * len(sources) + k]))
            start += source.shape[2]
    for copy in copies:
        copy.wait()


def rows_in_kernel(x_ref, mod_ref, out_ref):
    spread(out_ref, modulated(x_ref[...].astype(F32), mod_ref))


def gate_rows_kernel(e_ref, mod_ref, out_ref):
    spread(out_ref, mod_ref[2:3] * e_ref[...].astype(F32))


def forward_rows_kernel(got_ref, x_ref, mask_ref, mod_ref, uo_ref, next_ref, x_out, *outs):
    own_rows, width = x_ref.shape
    rank = uo_ref.shape[0]
    low = summed(got_ref, own_rows, pl.ds(width, PAD)).astype(BF16)[:, :rank]
    branch = summed(got_ref, own_rows, pl.ds(0, width)) + dot(low, uo_ref[...], 1, 0)
    x = x_ref[...].astype(F32) + mod_ref[2:3] * branch * mask_ref[...]
    x = x.astype(BF16)
    x_out[...] = x
    if outs:
        x_saved, spread_out = outs
        x_saved[...] = x_ref[...]
        spread(spread_out, modulated(x.astype(F32), next_ref))


def backward_rows_kernel(got_ref, e_ref, x_ref, mod_ref, next_ref, e_out, *spread_out):
    own_rows, width = x_ref.shape
    normed, inv_rms = rms_stats(x_ref[...].astype(F32))
    q = summed(got_ref, own_rows, pl.ds(0, width)) * (1.0 + mod_ref[1:2])
    mean = jnp.mean(q * normed, axis=-1, keepdims=True)
    e = (e_ref[...].astype(F32) + inv_rms * (q - normed * mean)).astype(BF16)
    e_out[...] = e
    for out_ref in spread_out:
        spread(out_ref, next_ref[2:3] * e.astype(F32))


def narrow_kernel(*refs):
    parts, out_ref = refs[:-1], refs[-1]
    rows = jnp.concatenate([part[...].astype(F32) for part in parts], axis=0).astype(BF16)
    for k in range(0, out_ref.shape[0], rows.shape[0]):
        out_ref[k : k + rows.shape[0]] = rows


def gradients_kernel(ids_ref, got_ref, *refs):
    per_block, (ours, theirs) = refs[:8], refs[8:]
    rank, cols = per_block[2].shape
    width = per_block[0].shape[1]
    deep = 4 * rank
    total = None
    for k in range(0, got_ref.shape[0], deep):
        part = got_ref[k : k + deep].astype(F32)
        total = part if total is None else total + part
    for i in range(2):
        g_ref, u_ref, ui_ref, do_ref = per_block[4 * i : 4 * i + 4]
        low_out = total[i * rank : (i + 1) * rank].astype(BF16)
        g_low = total[(2 + i) * rank : (3 + i) * rank]
        high = g_low.astype(BF16)
        rest = (g_low - high.astype(F32)).astype(BF16)
        grads = (
            dot(high, u_ref[...], 1, 0) + dot(rest, u_ref[...], 1, 0),
            ui_ref[...],
            do_ref[...],
            dot(low_out, g_ref[...], 1, 0),
        )

        def put(out, grads=grads):
            start = 0
            for grad in grads:
                out[:, start : start + grad.shape[1]] = grad
                start += grad.shape[1]

        pl.when(ids_ref[1] == i)(functools.partial(put, ours))
        pl.when(ids_ref[1] != i)(functools.partial(put, theirs))


def by_job_kernel(ids_ref, jobs_ref, ours, theirs, di_ref, ui_ref, do_ref, uo_ref):
    tp_pos, mb = ids_ref[2], ids_ref[3]
    owners, _, width = di_ref.shape
    cols = ui_ref.shape[2]
    for out in (di_ref, ui_ref, do_ref, uo_ref):
        out[...] = jnp.zeros(out.shape, F32)
    for job, grads in ((jobs_ref[mb], ours), (jobs_ref[1 - mb], theirs)):
        ui_ref[job] += grads[:, width : width + cols]
        do_ref[job] += grads[:, width + cols : width + 2 * cols]
        place = job - tp_pos * owners

        def owned(place=place, grads=grads):
            di_ref[place] += grads[:, :width]
            uo_ref[place] += grads[:, width + 2 * cols :]

        pl.when((place >= 0) & (place < owners))(owned)


def rows_call(kernel, out, *operands, scalars=0, cost=None):
    return pl.pallas_call(
        kernel,
        out_shape=out,
        in_specs=[SMEM] * scalars + [VMEM] * (len(operands) - scalars),
        out_specs=jax.tree.map(lambda _: VMEM, out),
        compiler_params=PARAMS,
        cost_estimate=cost,
        name=kernel.__name__,
    )(*operands)


def exchanged(parts, tp):
    rows, width = parts.shape
    got = lax.all_to_all(parts.reshape(tp, rows // tp, width), "tp", 0, 0)
    return got.reshape(rows, width)


def shards(
    latents,
    cotangent,
    token_counts,
    job_ids,
    modulation,
    w_in,
    w_out,
    down_in,
    up_in,
    down_out,
    up_out,
):
    tp = lax.axis_size("tp")
    segments = lax.axis_size("segment")
    planes = segments // 2
    seg = lax.axis_index("segment")
    plane, core = seg // 2, seg % 2
    tp_pos = lax.axis_index("tp")
    micro, own_rows, width = latents.shape
    cols = w_in.shape[2]
    jobs, rank = down_in.shape[1], down_in.shape[2]
    rows = own_rows * tp
    swap = [(s, s ^ 1) for s in range(segments)]
    onward = [(s, (s + 2) % segments) for s in range(segments)]
    across = [(s, d ^ 1) for s, d in onward]
    last_plane = planes - 1

    mb = core ^ sum((plane == p).astype(core.dtype) for p in range(planes) if CROSSED[p])
    ids = jnp.stack([(plane == 0).astype(jnp.int32), core, tp_pos, mb]).astype(jnp.int32)
    full = shape_of(rows, width)
    some = shape_of(own_rows, width)
    w_first = (w_in[0], lax.ppermute(w_in[0], "segment", swap))
    w_second = (w_out[0], lax.ppermute(w_out[0], "segment", swap))

    ends, x, e_last, mask = rows_call(
        first_rows_kernel,
        [full, some, some, shape_of(own_rows, 1, dtype=F32)],
        ids,
        token_counts,
        latents,
        cotangent,
        scalars=2,
    )
    ends, ids, mod = lax.optimization_barrier((ends, ids, modulation[0]))
    mod_other = lax.ppermute(mod, "segment", swap)
    mods = [jnp.where(core == i, mod, mod_other)[mb] for i in range(2)]

    adapters = [a[0] for a in (down_in, up_in, down_out, up_out)]
    packed = shape_of(rank, sum(a.shape[2] for a in adapters))
    low_own, low_sent = pl.pallas_call(
        pack_kernel,
        out_shape=[packed, packed],
        in_specs=[SMEM, SMEM] + [HBM] * len(adapters),
        out_specs=[VMEM, VMEM],
        scratch_shapes=[pltpu.SemaphoreType.DMA((2 * len(adapters),))],
        compiler_params=PARAMS,
        cost_estimate=pl.CostEstimate(
            flops=0, bytes_accessed=4 * math.prod(packed.shape), transcendentals=0
        ),
        name="pack_kernel",
    )(ids, job_ids, *in_hbm(*adapters))
    low_other = lax.ppermute(low_sent, "segment", swap)
    cuts = (width, width + cols, width + 2 * cols)
    lows = [
        jnp.split(jnp.where(core == i, low_own, low_other), cuts, axis=1) for i in range(2)
    ]

    ends = exchanged(ends, tp)
    ahead = pl.CostEstimate(
        flops=16 * rows * width * cols, bytes_accessed=16 * width * cols, transcendentals=rows * width
    )
    owns = [(core == i).astype(jnp.int32).reshape(1) for i in range(2)]
    late, early = plane >= planes // 2, (plane == 0) & (core == STAGGERED)
    flag = jnp.stack([core, late | early, late, late, late, plane > 0]).astype(jnp.int32)
    ends, flag = lax.optimization_barrier((ends, flag))
    (turned, ordered), x = lax.optimization_barrier(
        (ready_weights(flag, (*w_first, *w_second), ()), x)
    )

    def forward_plane(x, ordered, p):
        saved = []
        for i in range(2):
            if i:
                u = exchanged(sent, tp)
            elif p == 0:
                u = rows_call(modulate_kernel, full, ends, mods[0])
            else:
                u = exchanged(rows_call(rows_in_kernel, full, x, mods[0], cost=ahead), tp)
            last = p == last_plane and i == 1
            if p == 0:
                done = block_forward(u, (*w_first, *w_second), lows[i], owns[i])
            else:
                pair = ordered[2 * i : 2 * i + 2]
                done = block_forward(u, pair[:1] if last else pair, lows[i])
            act, slope, low_in, low_part, u, *part = done
            kept = (u, (act, slope, low_in), low_part)
            if last:
                saved.append((x, *kept))
                break
            got = exchanged(part[0], tp)
            if i == 0:
                x_next, x, sent = rows_call(
                    forward_rows_kernel,
                    [some, some, full],
                    got,
                    x,
                    mask,
                    mods[0],
                    lows[0][3],
                    mods[1],
                )
            else:
                (x_next,) = rows_call(
                    forward_rows_kernel, [some], got, x, mask, mods[1], lows[1][3], mods[1]
                )
            saved.append((x, *kept))
            x = x_next
        return x, tuple(saved)

    def backward_plane(e, saved, turned, p):
        kept = [None, None]
        for i in (1, 0):
            if i == 0:
                g = exchanged(sent, tp)
            elif p == last_plane:
                g = rows_call(gate_kernel, full, ends, mods[1])
            else:
                g = exchanged(rows_call(gate_rows_kernel, full, e, mods[1], cost=ahead), tp)
            x, u, acts, low_part = saved[i]
            first = p == 0 and i == 0
            w_in_t, w_out_t = turned[2 * i : 2 * i + 2]
            g_low_in, grad_ui, grad_do, g, *part = block_backward(
                g, acts, [w_out_t] if first else [w_out_t, w_in_t], lows[i], False
            )
            kept[i] = (g, g_low_in, grad_ui, grad_do)
            if first:
                break
            got = exchanged(part[0], tp)
            out = [some, full] if i else [some]
            e, *sent = rows_call(backward_rows_kernel, out, got, e, x, mods[i], mods[0])
            sent = sent[0] if sent else None
        return e, tuple(kept)

    def zeros(*shape, dtype=BF16):
        return jnp.zeros(shape, dtype)

    def no_saved():
        acts = (zeros(rows, cols), zeros(rows, cols, dtype=F32), zeros(rows, rank))
        return (zeros(own_rows, width), zeros(rows, width), acts, zeros(rank, rows))

    def no_kept():
        return (
            zeros(rows, width),
            zeros(rank, rows),
            zeros(rank, cols, dtype=F32),
            zeros(rank, cols, dtype=F32),
        )

    saved = (no_saved(), no_saved())
    kept = (no_kept(), no_kept())
    for p in range(last_plane):
        x, saved = lax.cond(
            plane == p,
            lambda x, saved: forward_plane(x, ordered, p),
            lambda x, saved: (x, saved),
            x,
            saved,
        )
        x = lax.ppermute(x, "segment", across if CROSSED[p] != CROSSED[p + 1] else onward)
        if p == planes // 2 - 1:
            rest = ~late
            flag = jnp.stack([core, rest & ~early, rest, rest, rest]).astype(jnp.int32)
            (turned, _), x = lax.optimization_barrier(
                (ready_weights(flag, (*w_first, *w_second), turned), x)
            )

    def turn(x, saved, kept):
        x, saved = forward_plane(x, ordered, last_plane)
        e, kept = backward_plane(e_last, saved, turned, last_plane)
        return e, saved, kept

    e, saved, kept = lax.cond(
        plane == last_plane, turn, lambda x, saved, kept: (x, saved, kept), x, saved, kept
    )
    for p in range(last_plane - 1, -1, -1):
        pairs = across if CROSSED[p] != CROSSED[p + 1] else onward
        e = lax.ppermute(e, "segment", [(d, s) for s, d in pairs])
        e, kept = lax.cond(
            plane == p,
            lambda e, saved, kept: backward_plane(e, saved, turned, p),
            lambda e, saved, kept: (e, kept),
            e,
            saved,
            kept,
        )

    narrow = (saved[0][3], saved[1][3], kept[0][1], kept[1][1])
    narrow_out = shape_of(tp * 4 * rank, rows)
    got = exchanged(rows_call(narrow_kernel, narrow_out, *narrow, cost=ahead), tp)
    wide = [shape_of(*packed.shape, dtype=F32)] * 2
    per_block = [(*in_vmem(kept[i][0], saved[i][1]), kept[i][2], kept[i][3]) for i in range(2)]
    mine, sent = rows_call(
        gradients_kernel, wide, ids, got, *per_block[0], *per_block[1], scalars=1
    )
    theirs = lax.ppermute(sent, "segment", swap)
    owned = shape_of(jobs // tp, rank, width, dtype=F32)
    split = shape_of(jobs, rank, cols, dtype=F32)
    grads = rows_call(
        by_job_kernel, [owned, split, split, owned], ids, job_ids, mine, theirs, scalars=2
    )
    return tuple(grad[None] for grad in grads)


def solution(mesh):
    return jax.shard_map(
        shards,
        mesh=mesh,
        in_specs=(
            P(None, "tp", None),
            P(None, "tp", None),
            P(),
            P(),
            P("segment", None, None, None),
            P("segment", None, "tp"),
            P("segment", "tp", None),
            P("segment", None, None, None),
            P("segment", None, None, "tp"),
            P("segment", None, None, "tp"),
            P("segment", None, None, None),
        ),
        out_specs=(
            P("segment", "tp", None, None),
            P("segment", None, None, "tp"),
            P("segment", None, None, "tp"),
            P("segment", "tp", None, None),
        ),
        check_vma=False,
    )
```

```python
import functools
import math

import jax
import jax.numpy as jnp
from jax import lax
from jax.experimental import pallas as pl
from jax.experimental.pallas import tpu as pltpu
from jax.sharding import PartitionSpec as P

EPS = 1e-06
ROOT_TWO_PI = math.sqrt(2.0 / math.pi)
F32 = jnp.float32
BF16 = jnp.bfloat16
PAD = 128
CUTS = 2
PARTS = 4
PAIR = 16
CROSSED = (0, 1, 0, 1)
STAGGERED = 0
VMEM = pl.BlockSpec(memory_space=pltpu.VMEM)
HBM = pl.BlockSpec(memory_space=pltpu.HBM)
SMEM = pl.BlockSpec(memory_space=pltpu.SMEM)
PARAMS = pltpu.CompilerParams(vmem_limit_bytes=16 * 1024 * 1024)


def shape_of(*shape, dtype=BF16):
    return jax.ShapeDtypeStruct(shape, dtype)


def gelu_and_slope(values):
    inner = ROOT_TWO_PI * (values + 0.044715 * values * values * values)
    tangent = jnp.tanh(inner)
    half = 0.5 * (1.0 + tangent)
    slope = half + 0.5 * values * (1.0 - tangent * tangent) * ROOT_TWO_PI * (
        1.0 + 3.0 * 0.044715 * values * values
    )
    return values * half, slope


def rms_stats(wide):
    inv_rms = lax.rsqrt(jnp.mean(wide * wide, axis=-1, keepdims=True) + EPS)
    return wide * inv_rms, inv_rms


def dot(a, b, a_dim, b_dim):
    return lax.dot_general(a, b, (((a_dim,), (b_dim,)), ((), ())), preferred_element_type=F32)


def fetch(own, ours, theirs, buf, sem):
    @pl.when(own)
    def _():
        pltpu.make_async_copy(ours, buf, sem).start()

    @pl.when(jnp.logical_not(own))
    def _():
        pltpu.make_async_copy(theirs, buf, sem).start()


def cut(c, size, parts=CUTS):
    return pl.ds(c * (size // parts), size // parts)


def keep(buf, out, sem):
    copy = pltpu.make_async_copy(buf, out, sem)
    copy.start()
    return copy


def in_hbm(*arrays):
    return [pltpu.with_memory_space_constraint(a, pltpu.HBM) for a in arrays]


def forward_kernel(*refs, last, streamed):
    if streamed:
        own_ref, u_ref, wi_own, wi_other, wo_own, wo_other, *refs = refs
        wi_ref, wo_ref, w_sems = refs[-3:]
        refs = refs[:-3]
        width = u_ref.shape[1]
        for c in range(CUTS):
            at = (cut(c, width),)
            fetch(own_ref[0] == 1, wi_own.at[at], wi_other.at[at], wi_ref.at[at], w_sems.at[c])
        for c in range(CUTS):
            at = (slice(None), cut(c, width))
            fetch(
                own_ref[0] == 1, wo_own.at[at], wo_other.at[at], wo_ref.at[at], w_sems.at[CUTS + c]
            )
    else:
        u_ref, wi_ref, *refs = refs
        wo_ref, refs = (None, refs) if last else (refs[0], refs[1:])

    def arrived(source, held, n, at):
        if streamed:
            pltpu.make_async_copy(source.at[at], held.at[at], w_sems.at[n]).wait()

    wi_own, wo_own = (wi_own, wo_own) if streamed else (None, None)
    di_ref, ui_ref, do_ref, act_out, slope_out, low_in_out, low_out, u_out, *rest = refs
    sent_ref, rest = (None, rest) if last else (rest[0], rest[1:])
    act_ref, slope_ref, low_in_ref, low_ref, out_sems = rest
    width, rank = u_ref.shape[1], di_ref.shape[0]
    low_in = dot(u_ref[...], di_ref[...], 1, 1).astype(BF16)
    low_in_ref[...] = low_in
    copies = [keep(u_ref, u_out, out_sems.at[4]), keep(low_in_ref, low_in_out, out_sems.at[0])]
    pre = dot(low_in, ui_ref[...], 1, 0)
    for c in range(CUTS if streamed else 1):
        at = cut(c, width) if streamed else slice(None)
        arrived(wi_own, wi_ref, c, (at,))
        pre = pre + dot(u_ref[:, at], wi_ref[at], 1, 0)
    act, slope = gelu_and_slope(pre)
    act = act.astype(BF16)
    act_ref[...] = act
    slope_ref[...] = slope
    copies.append(keep(act_ref, act_out, out_sems.at[1]))
    copies.append(keep(slope_ref, slope_out, out_sems.at[2]))
    low_ref[...] = dot(do_ref[...], act, 1, 1).astype(BF16)
    copies.append(keep(low_ref, low_out, out_sems.at[3]))
    if not last:
        sent_ref[:, width:] = jnp.zeros((sent_ref.shape[0], PAD), BF16)
        sent_ref[:, width : width + rank] = dot(act, do_ref[...], 1, 1).astype(BF16)
        for c in range(CUTS):
            at = cut(c, width)
            arrived(wo_own, wo_ref, CUTS + c, (slice(None), at))
            sent_ref[:, at] = dot(act, wo_ref[:, at], 1, 0).astype(BF16)
    for copy in copies:
        copy.wait()


def backward_kernel(*refs, first, streamed):
    if streamed:
        wi_ref, wo_ref, w_sems = refs[-3:]
        g_ref, slope_in, act_in, low_in_in, wo_hbm, wi_hbm, *refs = refs[:-3]
        width = g_ref.shape[1]
        for c in range(CUTS):
            at = (cut(c, width),)
            pltpu.make_async_copy(wo_hbm.at[at], wo_ref.at[at], w_sems.at[c]).start()
        for c in range(CUTS):
            at = (slice(None), cut(c, width))
            pltpu.make_async_copy(wi_hbm.at[at], wi_ref.at[at], w_sems.at[CUTS + c]).start()
    else:
        wi_hbm = wo_hbm = None
        g_ref, slope_in, act_in, low_in_in, wo_ref, *refs = refs
        wi_ref, refs = (None, refs) if first else (refs[0], refs[1:])

    def arrived(source, held, n, at):
        if streamed:
            pltpu.make_async_copy(source.at[at], held.at[at], w_sems.at[n]).wait()

    di_ref, ui_ref, do_ref, uo_ref, g_low_out_ref, grad_ui_out, grad_do_out, g_out, *rest = refs
    part_ref, rest = (None, rest) if first else (rest[0], rest[1:])
    act_ref, slope_ref, low_in_ref, g_low_ref, grad_ui, grad_do, io_sems = rest
    width = g_ref.shape[1]
    slope_copy = keep(slope_in, slope_ref, io_sems.at[1])
    low_in_copy = keep(low_in_in, low_in_ref, io_sems.at[2])
    act_copy = keep(act_in, act_ref, io_sems.at[0])
    g_copy = keep(g_ref, g_out, io_sems.at[6])
    g_low_out = dot(g_ref[...], uo_ref[...], 1, 1).astype(BF16)
    g_act = dot(g_low_out, do_ref[...], 1, 0)
    for c in range(CUTS if streamed else 1):
        at = cut(c, width) if streamed else slice(None)
        arrived(wo_hbm, wo_ref, c, (at,))
        g_act = g_act + dot(g_ref[:, at], wo_ref[at], 1, 0)
    slope_copy.wait()
    g_pre = (g_act * slope_ref[...]).astype(BF16)
    g_low_ref[...] = dot(ui_ref[...], g_pre, 1, 1).astype(BF16)
    copies = [g_copy, keep(g_low_ref, g_low_out_ref, io_sems.at[3])]
    low_in_copy.wait()
    grad_ui[...] = dot(low_in_ref[...], g_pre, 0, 0)
    copies.append(keep(grad_ui, grad_ui_out, io_sems.at[4]))
    act_copy.wait()
    grad_do[...] = dot(g_low_out, act_ref[...], 0, 0)
    copies.append(keep(grad_do, grad_do_out, io_sems.at[5]))
    if not first:
        g_low_in = dot(g_pre, ui_ref[...], 1, 1).astype(BF16)
        for c in range(CUTS if streamed else PARTS):
            at = (slice(None), cut(c, width, CUTS if streamed else PARTS))
            arrived(wi_hbm, wi_ref, CUTS + c, at)
            part = dot(g_pre, wi_ref[at], 1, 0) + dot(g_low_in, di_ref[at], 1, 0)
            part_ref[at] = part.astype(BF16)
    for copy in copies:
        copy.wait()


def block_cost(rows, width, cols, matmuls):
    return pl.CostEstimate(
        flops=2 * matmuls * rows * width * cols,
        bytes_accessed=2 * matmuls * width * cols,
        transcendentals=rows * cols,
    )


def in_vmem(*arrays):
    return [pltpu.with_memory_space_constraint(a, pltpu.VMEM) for a in arrays]


def block_forward(u, weights, low, own=None):
    rows, width = u.shape
    streamed, last = own is not None, len(weights) == 1
    rank, cols = low[1].shape
    kept = [((rows, cols), BF16), ((rows, cols), F32), ((rows, rank), BF16), ((rank, rows), BF16)]
    out = [shape_of(*s, dtype=t) for s, t in kept] + [shape_of(rows, width)]
    out += [] if last else [shape_of(rows, width + PAD)]
    stream_scratch = [
        pltpu.VMEM((width, cols), BF16),
        pltpu.VMEM((cols, width), BF16),
        pltpu.SemaphoreType.DMA((2 * CUTS,)),
    ]
    first_specs = [SMEM, VMEM] + [HBM] * 4 if streamed else [VMEM] * (1 + len(weights))
    return pl.pallas_call(
        functools.partial(forward_kernel, last=last, streamed=streamed),
        out_shape=out,
        in_specs=first_specs + [VMEM] * 3,
        out_specs=[HBM] * (len(kept) + 1) + ([] if last else [VMEM]),
        scratch_shapes=[
            *(pltpu.VMEM(s, t) for s, t in kept),
            pltpu.SemaphoreType.DMA((len(kept) + 1,)),
            *(stream_scratch if streamed else []),
        ],
        compiler_params=PARAMS,
        cost_estimate=block_cost(rows, width, cols, 1 if last else 2),
        name="block_forward",
    )(*((own, u, *in_hbm(*weights)) if streamed else (u, *in_vmem(*weights))), *low[:3])


def block_backward(g, acts, weights, low, streamed):
    rows, width = g.shape
    first = len(weights) == 1
    rank, cols = low[1].shape
    kept = [((rank, rows), BF16), ((rank, cols), F32), ((rank, cols), F32)]
    out = [shape_of(*s, dtype=t) for s, t in kept] + [shape_of(rows, width)]
    out += [] if first else [shape_of(rows, width)]
    act, slope, low_in = acts
    stream_scratch = [
        pltpu.VMEM((cols, width), BF16),
        pltpu.VMEM((width, cols), BF16),
        pltpu.SemaphoreType.DMA((2 * CUTS,)),
    ]
    return pl.pallas_call(
        functools.partial(backward_kernel, first=first, streamed=streamed),
        out_shape=out,
        in_specs=[VMEM] + [HBM] * 3 + [HBM if streamed else VMEM] * len(weights) + [VMEM] * 4,
        out_specs=[HBM] * (len(kept) + 1) + ([] if first else [VMEM]),
        scratch_shapes=[
            pltpu.VMEM((rows, cols), BF16),
            pltpu.VMEM((rows, cols), F32),
            pltpu.VMEM((rows, rank), BF16),
            *(pltpu.VMEM(s, t) for s, t in kept),
            pltpu.SemaphoreType.DMA((7,)),
            *(stream_scratch if streamed else []),
        ],
        compiler_params=PARAMS,
        cost_estimate=block_cost(rows, width, cols, len(weights)),
        name="block_backward",
    )(g, slope, act, low_in, *(in_hbm if streamed else in_vmem)(*weights), *low)


def ready_kernel(flag_ref, *refs, order):
    if order:
        ordered, wi_buf, wo_buf, buf_sems = refs[8:12], *refs[-3:]
        refs = refs[:8] + refs[12:-3]

        @pl.when(flag_ref[5] == 1)
        def _():
            order_weights(flag_ref, refs[:4], ordered, (wi_buf, wo_buf), buf_sems)

    turn_weights(flag_ref, *refs)


def order_weights(flag_ref, refs, outs, bufs, sems):
    sources = ((refs[0], refs[1], bufs[0]), (refs[2], refs[3], bufs[1]))
    for i in range(2):
        for k, (ours, theirs, buf) in enumerate(sources):
            if i:
                pltpu.make_async_copy(buf, outs[k], sems.at[2 + k]).wait()
            fetch(flag_ref[0] == i, ours, theirs, buf, sems.at[k])
        for k, (ours, theirs, buf) in enumerate(sources):
            pltpu.make_async_copy(ours, buf, sems.at[k]).wait()
            pltpu.make_async_copy(buf, outs[2 * i + k], sems.at[2 + k]).start()
    for k, (ours, theirs, buf) in enumerate(sources):
        pltpu.make_async_copy(buf, outs[2 + k], sems.at[2 + k]).wait()


def turn_weights(flag_ref, *refs):
    narrow_buf, wide_buf, in_sems, out_sems = refs[-4:]
    outs, sources = refs[-8:-4], refs[:4]
    step = narrow_buf.shape[1]

    def turn(own, ours, theirs, target, in_buf, out_buf, by_rows):
        count = ours.shape[0 if by_rows else 1] // step

        def cut_of(ref, c, rows):
            at = pl.ds(pl.multiple_of(c * step, step), step)
            return ref.at[at] if rows else ref.at[:, at]

        def come(c):
            slot = lax.rem(c, 2)
            source, other = (cut_of(ref, c, by_rows) for ref in (ours, theirs))
            fetch(own, source, other, in_buf.at[slot], in_sems.at[slot])

        def going(c, slot):
            target_cut = cut_of(target, c, not by_rows)
            return pltpu.make_async_copy(out_buf.at[slot], target_cut, out_sems.at[slot])

        come(0)

        def body(c, carry):
            slot = lax.rem(c, 2)

            @pl.when(c + 1 < count)
            def _():
                come(c + 1)

            source = cut_of(ours, c, by_rows)
            pltpu.make_async_copy(source, in_buf.at[slot], in_sems.at[slot]).wait()

            @pl.when(c >= 2)
            def _():
                going(c - 2, slot).wait()

            out_buf[slot] = in_buf[slot].T
            going(c, slot).start()
            return carry

        lax.fori_loop(0, count, body, 0)
        going(count - 2, count % 2).wait()
        going(count - 1, 1 - count % 2).wait()

    for i in range(2):
        own = flag_ref[0] == i
        into = functools.partial(turn, own, *sources[:2], outs[2 * i], narrow_buf, wide_buf, True)
        pl.when(flag_ref[1 + 2 * i] == 1)(into)
        out = functools.partial(
            turn, own, *sources[2:], outs[2 * i + 1], wide_buf, narrow_buf, False
        )
        pl.when(flag_ref[2 + 2 * i] == 1)(out)


def ready_weights(flag, weights, held):
    width, cols = weights[0].shape
    step = 384
    turned = [shape_of(cols, width), shape_of(width, cols)] * 2
    ordered = [] if held else [shape_of(width, cols), shape_of(cols, width)] * 2
    buffers = [
        pltpu.VMEM((width, cols), BF16),
        pltpu.VMEM((cols, width), BF16),
        pltpu.SemaphoreType.DMA((4,)),
    ]
    out = pl.pallas_call(
        functools.partial(ready_kernel, order=not held),
        out_shape=turned + ordered,
        in_specs=[SMEM] + [HBM] * (4 + len(held)),
        out_specs=[HBM] * (4 + len(ordered)),
        scratch_shapes=[
            pltpu.VMEM((2, step, cols), BF16),
            pltpu.VMEM((2, cols, step), BF16),
            pltpu.SemaphoreType.DMA((2,)),
            pltpu.SemaphoreType.DMA((2,)),
            *([] if held else buffers),
        ],
        input_output_aliases={5 + k: k for k in range(len(held))},
        compiler_params=PARAMS,
        name="ready_weights",
    )(flag, *in_hbm(*weights), *held)
    return tuple(out[:4]), tuple(out[4:])


def summed(got_ref, own_rows, at):
    total = None
    for k in range(0, got_ref.shape[0], PAIR):
        part = got_ref[k : k + PAIR, at].astype(F32)
        part = part.reshape(PAIR // own_rows, own_rows, part.shape[1]).sum(0)
        total = part if total is None else total + part
    return total


def spread(out_ref, rows):
    pair = jnp.concatenate([rows] * (PAIR // rows.shape[0]), axis=0).astype(BF16)
    for k in range(0, out_ref.shape[0], PAIR):
        out_ref[k : k + PAIR] = pair


def modulated(wide, mod_ref):
    return rms_stats(wide)[0] * (1.0 + mod_ref[1:2]) + mod_ref[0:1]


def first_rows_kernel(ids_ref, counts_ref, x_ref, e_ref, out_ref, x_out, e_out, mask_out):
    at_start, tp_pos, mb = ids_ref[0], ids_ref[2], ids_ref[3]
    own_rows = x_ref.shape[1]
    row = tp_pos * own_rows + lax.broadcasted_iota(jnp.int32, (own_rows, 1), 0)
    mask = (row < counts_ref[mb]).astype(F32)
    mask_out[...] = mask
    x = x_ref[mb].astype(F32) * mask
    e = e_ref[mb].astype(F32) * mask
    x_out[...] = x.astype(BF16)
    e_out[...] = e.astype(BF16)
    spread(out_ref, jnp.where(at_start == 1, x, e))


def modulate_kernel(x_ref, mod_ref, out_ref):
    out_ref[...] = modulated(x_ref[...].astype(F32), mod_ref).astype(BF16)


def gate_kernel(e_ref, mod_ref, out_ref):
    out_ref[...] = (mod_ref[2:3] * e_ref[...].astype(F32)).astype(BF16)


def pack_kernel(ids_ref, jobs_ref, *refs):
    sources, ours, theirs, sems = refs[:-3], refs[-3], refs[-2], refs[-1]
    mb = ids_ref[3]
    copies = []
    for n, (job, out) in enumerate(((jobs_ref[mb], ours), (jobs_ref[1 - mb], theirs))):
        start = 0
        for k, source in enumerate(sources):
            at = pl.ds(start, source.shape[2])
            copies.append(keep(source.at[job], out.at[:, at], sems.at[n * len(sources) + k]))
            start += source.shape[2]
    for copy in copies:
        copy.wait()


def rows_in_kernel(x_ref, mod_ref, out_ref):
    spread(out_ref, modulated(x_ref[...].astype(F32), mod_ref))


def gate_rows_kernel(e_ref, mod_ref, out_ref):
    spread(out_ref, mod_ref[2:3] * e_ref[...].astype(F32))


def forward_rows_kernel(got_ref, x_ref, mask_ref, mod_ref, uo_ref, next_ref, x_out, *outs):
    own_rows, width = x_ref.shape
    rank = uo_ref.shape[0]
    low = summed(got_ref, own_rows, pl.ds(width, PAD)).astype(BF16)[:, :rank]
    branch = summed(got_ref, own_rows, pl.ds(0, width)) + dot(low, uo_ref[...], 1, 0)
    x = x_ref[...].astype(F32) + mod_ref[2:3] * branch * mask_ref[...]
    x = x.astype(BF16)
    x_out[...] = x
    if outs:
        x_saved, spread_out = outs
        x_saved[...] = x_ref[...]
        spread(spread_out, modulated(x.astype(F32), next_ref))


def backward_rows_kernel(got_ref, e_ref, x_ref, mod_ref, next_ref, e_out, *spread_out):
    own_rows, width = x_ref.shape
    normed, inv_rms = rms_stats(x_ref[...].astype(F32))
    q = summed(got_ref, own_rows, pl.ds(0, width)) * (1.0 + mod_ref[1:2])
    mean = jnp.mean(q * normed, axis=-1, keepdims=True)
    e = (e_ref[...].astype(F32) + inv_rms * (q - normed * mean)).astype(BF16)
    e_out[...] = e
    for out_ref in spread_out:
        spread(out_ref, next_ref[2:3] * e.astype(F32))


def narrow_kernel(*refs):
    parts, out_ref = refs[:-1], refs[-1]
    rows = jnp.concatenate([part[...].astype(F32) for part in parts], axis=0).astype(BF16)
    for k in range(0, out_ref.shape[0], rows.shape[0]):
        out_ref[k : k + rows.shape[0]] = rows


def gradients_kernel(ids_ref, got_ref, *refs):
    per_block, (ours, theirs) = refs[:4], refs[4:]
    width = per_block[0].shape[1]
    rank = ours.shape[0]
    deep = 4 * rank
    total = None
    for k in range(0, got_ref.shape[0], deep):
        part = got_ref[k : k + deep].astype(F32)
        total = part if total is None else total + part
    for i in range(2):
        g_ref, u_ref = per_block[2 * i : 2 * i + 2]
        low_out = total[i * rank : (i + 1) * rank].astype(BF16)
        g_low = total[(2 + i) * rank : (3 + i) * rank]
        high = g_low.astype(BF16)
        rest = g_low - high.astype(F32)
        both = jnp.concatenate([high.astype(F32), rest], axis=0).astype(BF16)
        both = dot(both, u_ref[...], 1, 0)
        grads = (both[:rank] + both[rank:], dot(low_out, g_ref[...], 1, 0))

        def put(out, grads=grads):
            for k, grad in enumerate(grads):
                out[:, k * width : (k + 1) * width] = grad

        pl.when(ids_ref[1] == i)(functools.partial(put, ours))
        pl.when(ids_ref[1] != i)(functools.partial(put, theirs))


def choose_kernel(ids_ref, *refs):
    blocks, (ours, theirs) = refs[:4], refs[4:]
    cols = blocks[0].shape[1]
    for i in range(2):

        def put(out, i=i):
            for k in range(2):
                out[:, k * cols : (k + 1) * cols] = blocks[2 * i + k][...]

        pl.when(ids_ref[1] == i)(functools.partial(put, ours))
        pl.when(ids_ref[1] != i)(functools.partial(put, theirs))


def split_kernel(ids_ref, jobs_ref, ours, theirs, ui_ref, do_ref):
    mb, cols = ids_ref[3], ui_ref.shape[2]
    for out in (ui_ref, do_ref):
        out[...] = jnp.zeros(out.shape, F32)
    for job, grads in ((jobs_ref[mb], ours), (jobs_ref[1 - mb], theirs)):
        ui_ref[job] += grads[:, :cols]
        do_ref[job] += grads[:, cols:]


def owned_kernel(ids_ref, jobs_ref, ours, theirs, di_ref, uo_ref):
    tp_pos, mb = ids_ref[2], ids_ref[3]
    owners, _, width = di_ref.shape
    for out in (di_ref, uo_ref):
        out[...] = jnp.zeros(out.shape, F32)
    for job, grads in ((jobs_ref[mb], ours), (jobs_ref[1 - mb], theirs)):
        place = job - tp_pos * owners

        def owned(place=place, grads=grads):
            di_ref[place] += grads[:, :width]
            uo_ref[place] += grads[:, width:]

        pl.when((place >= 0) & (place < owners))(owned)


def rows_call(kernel, out, *operands, scalars=0, cost=None):
    return pl.pallas_call(
        kernel,
        out_shape=out,
        in_specs=[SMEM] * scalars + [VMEM] * (len(operands) - scalars),
        out_specs=jax.tree.map(lambda _: VMEM, out),
        compiler_params=PARAMS,
        cost_estimate=cost,
        name=kernel.__name__,
    )(*operands)


def exchanged(parts, tp):
    rows, width = parts.shape
    got = lax.all_to_all(parts.reshape(tp, rows // tp, width), "tp", 0, 0)
    return got.reshape(rows, width)


def shards(
    latents,
    cotangent,
    token_counts,
    job_ids,
    modulation,
    w_in,
    w_out,
    down_in,
    up_in,
    down_out,
    up_out,
):
    tp = lax.axis_size("tp")
    segments = lax.axis_size("segment")
    planes = segments // 2
    seg = lax.axis_index("segment")
    plane, core = seg // 2, seg % 2
    tp_pos = lax.axis_index("tp")
    micro, own_rows, width = latents.shape
    cols = w_in.shape[2]
    jobs, rank = down_in.shape[1], down_in.shape[2]
    rows = own_rows * tp
    swap = [(s, s ^ 1) for s in range(segments)]
    onward = [(s, (s + 2) % segments) for s in range(segments)]
    across = [(s, d ^ 1) for s, d in onward]
    last_plane = planes - 1

    mb = core ^ sum((plane == p).astype(core.dtype) for p in range(planes) if CROSSED[p])
    ids = jnp.stack([(plane == 0).astype(jnp.int32), core, tp_pos, mb]).astype(jnp.int32)
    full = shape_of(rows, width)
    some = shape_of(own_rows, width)
    w_first = (w_in[0], lax.ppermute(w_in[0], "segment", swap))
    w_second = (w_out[0], lax.ppermute(w_out[0], "segment", swap))

    ends, x, e_last, mask = rows_call(
        first_rows_kernel,
        [full, some, some, shape_of(own_rows, 1, dtype=F32)],
        ids,
        token_counts,
        latents,
        cotangent,
        scalars=2,
    )
    ends, ids, mod = lax.optimization_barrier((ends, ids, modulation[0]))
    mod_other = lax.ppermute(mod, "segment", swap)
    mods = [jnp.where(core == i, mod, mod_other)[mb] for i in range(2)]

    adapters = [a[0] for a in (down_in, up_in, down_out, up_out)]
    packed = shape_of(rank, sum(a.shape[2] for a in adapters))
    low_own, low_sent = pl.pallas_call(
        pack_kernel,
        out_shape=[packed, packed],
        in_specs=[SMEM, SMEM] + [HBM] * len(adapters),
        out_specs=[VMEM, VMEM],
        scratch_shapes=[pltpu.SemaphoreType.DMA((2 * len(adapters),))],
        compiler_params=PARAMS,
        cost_estimate=pl.CostEstimate(
            flops=0, bytes_accessed=4 * math.prod(packed.shape), transcendentals=0
        ),
        name="pack_kernel",
    )(ids, job_ids, *in_hbm(*adapters))
    low_other = lax.ppermute(low_sent, "segment", swap)
    cuts = (width, width + cols, width + 2 * cols)
    lows = [
        jnp.split(jnp.where(core == i, low_own, low_other), cuts, axis=1) for i in range(2)
    ]

    ends = exchanged(ends, tp)
    ahead = pl.CostEstimate(
        flops=16 * rows * width * cols, bytes_accessed=16 * width * cols, transcendentals=rows * width
    )
    owns = [(core == i).astype(jnp.int32).reshape(1) for i in range(2)]
    late, early = plane >= planes // 2, (plane == 0) & (core == STAGGERED)
    flag = jnp.stack([core, late | early, late, late, late, plane > 0]).astype(jnp.int32)
    ends, flag = lax.optimization_barrier((ends, flag))
    (turned, ordered), x = lax.optimization_barrier(
        (ready_weights(flag, (*w_first, *w_second), ()), x)
    )

    def forward_plane(x, ordered, p):
        saved = []
        for i in range(2):
            if i:
                u = exchanged(sent, tp)
            elif p == 0:
                u = rows_call(modulate_kernel, full, ends, mods[0])
            else:
                u = exchanged(rows_call(rows_in_kernel, full, x, mods[0], cost=ahead), tp)
            last = p == last_plane and i == 1
            if p == 0:
                done = block_forward(u, (*w_first, *w_second), lows[i], owns[i])
            else:
                pair = ordered[2 * i : 2 * i + 2]
                done = block_forward(u, pair[:1] if last else pair, lows[i])
            act, slope, low_in, low_part, u, *part = done
            kept = (u, (act, slope, low_in), low_part)
            if last:
                saved.append((x, *kept))
                break
            got = exchanged(part[0], tp)
            if i == 0:
                x_next, x, sent = rows_call(
                    forward_rows_kernel,
                    [some, some, full],
                    got,
                    x,
                    mask,
                    mods[0],
                    lows[0][3],
                    mods[1],
                )
            else:
                (x_next,) = rows_call(
                    forward_rows_kernel, [some], got, x, mask, mods[1], lows[1][3], mods[1]
                )
            saved.append((x, *kept))
            x = x_next
        return x, tuple(saved)

    def backward_plane(e, saved, turned, p):
        kept = [None, None]
        for i in (1, 0):
            if i == 0:
                g = exchanged(sent, tp)
            elif p == last_plane:
                g = rows_call(gate_kernel, full, ends, mods[1])
            else:
                g = exchanged(rows_call(gate_rows_kernel, full, e, mods[1], cost=ahead), tp)
            x, u, acts, low_part = saved[i]
            first = p == 0 and i == 0
            w_in_t, w_out_t = turned[2 * i : 2 * i + 2]
            g_low_in, grad_ui, grad_do, g, *part = block_backward(
                g, acts, [w_out_t] if first else [w_out_t, w_in_t], lows[i], False
            )
            kept[i] = (g, g_low_in, grad_ui, grad_do)
            if first:
                break
            got = exchanged(part[0], tp)
            out = [some, full] if i else [some]
            e, *sent = rows_call(backward_rows_kernel, out, got, e, x, mods[i], mods[0])
            sent = sent[0] if sent else None
        return e, tuple(kept)

    def zeros(*shape, dtype=BF16):
        return jnp.zeros(shape, dtype)

    def no_saved():
        acts = (zeros(rows, cols), zeros(rows, cols, dtype=F32), zeros(rows, rank))
        return (zeros(own_rows, width), zeros(rows, width), acts, zeros(rank, rows))

    def no_kept():
        return (
            zeros(rows, width),
            zeros(rank, rows),
            zeros(rank, cols, dtype=F32),
            zeros(rank, cols, dtype=F32),
        )

    saved = (no_saved(), no_saved())
    kept = (no_kept(), no_kept())
    for p in range(last_plane):
        x, saved = lax.cond(
            plane == p,
            lambda x, saved: forward_plane(x, ordered, p),
            lambda x, saved: (x, saved),
            x,
            saved,
        )
        x = lax.ppermute(x, "segment", across if CROSSED[p] != CROSSED[p + 1] else onward)
        if p == planes // 2 - 1:
            rest = ~late
            flag = jnp.stack([core, rest & ~early, rest, rest, rest]).astype(jnp.int32)
            (turned, _), x = lax.optimization_barrier(
                (ready_weights(flag, (*w_first, *w_second), turned), x)
            )

    def turn(x, saved, kept):
        x, saved = forward_plane(x, ordered, last_plane)
        e, kept = backward_plane(e_last, saved, turned, last_plane)
        return e, saved, kept

    e, saved, kept = lax.cond(
        plane == last_plane, turn, lambda x, saved, kept: (x, saved, kept), x, saved, kept
    )
    for p in range(last_plane - 1, -1, -1):
        pairs = across if CROSSED[p] != CROSSED[p + 1] else onward
        e = lax.ppermute(e, "segment", [(d, s) for s, d in pairs])
        e, kept = lax.cond(
            plane == p,
            lambda e, saved, kept: backward_plane(e, saved, turned, p),
            lambda e, saved, kept: (e, kept),
            e,
            saved,
            kept,
        )

    narrow = (saved[0][3], saved[1][3], kept[0][1], kept[1][1])
    narrow_out = shape_of(tp * 4 * rank, rows)
    spread_out = rows_call(narrow_kernel, narrow_out, *narrow, cost=ahead)
    pair = [shape_of(rank, 2 * cols, dtype=F32)] * 2
    split_mine, split_sent = rows_call(
        choose_kernel, pair, ids, *kept[0][2:], *kept[1][2:], scalars=1
    )
    split_theirs = lax.ppermute(split_sent, "segment", swap)
    got = exchanged(spread_out, tp)
    wide = [shape_of(rank, 2 * width, dtype=F32)] * 2
    per_block = [a for i in range(2) for a in in_vmem(kept[i][0], saved[i][1])]
    mine, sent = rows_call(gradients_kernel, wide, ids, got, *per_block, scalars=1)
    theirs = lax.ppermute(sent, "segment", swap)
    split = [shape_of(jobs, rank, cols, dtype=F32)] * 2
    grad_ui, grad_do = rows_call(
        split_kernel,
        split,
        ids,
        job_ids,
        split_mine,
        split_theirs,
        scalars=2,
        cost=pl.CostEstimate(flops=0, bytes_accessed=8 * jobs * rank * cols, transcendentals=0),
    )
    owned = [shape_of(jobs // tp, rank, width, dtype=F32)] * 2
    grad_di, grad_uo = rows_call(
        owned_kernel, owned, ids, job_ids, mine, theirs, scalars=2
    )
    return tuple(grad[None] for grad in (grad_di, grad_ui, grad_do, grad_uo))


def solution(mesh):
    return jax.shard_map(
        shards,
        mesh=mesh,
        in_specs=(
            P(None, "tp", None),
            P(None, "tp", None),
            P(),
            P(),
            P("segment", None, None, None),
            P("segment", None, "tp"),
            P("segment", "tp", None),
            P("segment", None, None, None),
            P("segment", None, None, "tp"),
            P("segment", None, None, "tp"),
            P("segment", None, None, None),
        ),
        out_specs=(
            P("segment", "tp", None, None),
            P("segment", None, None, "tp"),
            P("segment", None, None, "tp"),
            P("segment", "tp", None, None),
        ),
        check_vma=False,
    )
```

```python
import functools
import math

import jax
import jax.numpy as jnp
from jax import lax
from jax.experimental import pallas as pl
from jax.experimental.pallas import tpu as pltpu
from jax.sharding import PartitionSpec as P

EPS = 1e-06
ROOT_TWO_PI = math.sqrt(2.0 / math.pi)
F32 = jnp.float32
BF16 = jnp.bfloat16
PAD = 128
CUTS = 2
PARTS = 4
PAIR = 16
CROSSED = (0, 1, 0, 1)
STAGGERED = 0
VMEM = pl.BlockSpec(memory_space=pltpu.VMEM)
HBM = pl.BlockSpec(memory_space=pltpu.HBM)
SMEM = pl.BlockSpec(memory_space=pltpu.SMEM)
PARAMS = pltpu.CompilerParams(vmem_limit_bytes=16 * 1024 * 1024)


def shape_of(*shape, dtype=BF16):
    return jax.ShapeDtypeStruct(shape, dtype)


def gelu_and_slope(values):
    inner = ROOT_TWO_PI * (values + 0.044715 * values * values * values)
    tangent = jnp.tanh(inner)
    half = 0.5 * (1.0 + tangent)
    slope = half + 0.5 * values * (1.0 - tangent * tangent) * ROOT_TWO_PI * (
        1.0 + 3.0 * 0.044715 * values * values
    )
    return values * half, slope


def rms_stats(wide):
    inv_rms = lax.rsqrt(jnp.mean(wide * wide, axis=-1, keepdims=True) + EPS)
    return wide * inv_rms, inv_rms


def dot(a, b, a_dim, b_dim):
    return lax.dot_general(a, b, (((a_dim,), (b_dim,)), ((), ())), preferred_element_type=F32)


def fetch(own, ours, theirs, buf, sem):
    @pl.when(own)
    def _():
        pltpu.make_async_copy(ours, buf, sem).start()

    @pl.when(jnp.logical_not(own))
    def _():
        pltpu.make_async_copy(theirs, buf, sem).start()


def cut(c, size, parts=CUTS):
    return pl.ds(c * (size // parts), size // parts)


def keep(buf, out, sem):
    copy = pltpu.make_async_copy(buf, out, sem)
    copy.start()
    return copy


def in_hbm(*arrays):
    return [pltpu.with_memory_space_constraint(a, pltpu.HBM) for a in arrays]


def forward_kernel(*refs, last, streamed):
    if streamed:
        own_ref, u_ref, wi_own, wi_other, wo_own, wo_other, *refs = refs
        wi_ref, wo_ref, w_sems = refs[-3:]
        refs = refs[:-3]
        width = u_ref.shape[1]
        for c in range(CUTS):
            at = (cut(c, width),)
            fetch(own_ref[0] == 1, wi_own.at[at], wi_other.at[at], wi_ref.at[at], w_sems.at[c])
        for c in range(CUTS):
            at = (slice(None), cut(c, width))
            fetch(
                own_ref[0] == 1, wo_own.at[at], wo_other.at[at], wo_ref.at[at], w_sems.at[CUTS + c]
            )
    else:
        u_ref, wi_ref, *refs = refs
        wo_ref, refs = (None, refs) if last else (refs[0], refs[1:])

    def arrived(source, held, n, at):
        if streamed:
            pltpu.make_async_copy(source.at[at], held.at[at], w_sems.at[n]).wait()

    wi_own, wo_own = (wi_own, wo_own) if streamed else (None, None)
    di_ref, ui_ref, do_ref, act_out, slope_out, low_in_out, low_out, u_out, *rest = refs
    sent_ref, rest = (None, rest) if last else (rest[0], rest[1:])
    act_ref, slope_ref, low_in_ref, low_ref, out_sems = rest
    width, rank = u_ref.shape[1], di_ref.shape[0]
    low_in = dot(u_ref[...], di_ref[...], 1, 1).astype(BF16)
    low_in_ref[...] = low_in
    copies = [keep(u_ref, u_out, out_sems.at[4]), keep(low_in_ref, low_in_out, out_sems.at[0])]
    pre = dot(low_in, ui_ref[...], 1, 0)
    for c in range(CUTS if streamed else 1):
        at = cut(c, width) if streamed else slice(None)
        arrived(wi_own, wi_ref, c, (at,))
        pre = pre + dot(u_ref[:, at], wi_ref[at], 1, 0)
    act, slope = gelu_and_slope(pre)
    act = act.astype(BF16)
    act_ref[...] = act
    slope_ref[...] = slope
    copies.append(keep(act_ref, act_out, out_sems.at[1]))
    copies.append(keep(slope_ref, slope_out, out_sems.at[2]))
    low_ref[...] = dot(do_ref[...], act, 1, 1).astype(BF16)
    copies.append(keep(low_ref, low_out, out_sems.at[3]))
    if not last:
        sent_ref[:, width:] = jnp.zeros((sent_ref.shape[0], PAD), BF16)
        sent_ref[:, width : width + rank] = dot(act, do_ref[...], 1, 1).astype(BF16)
        for c in range(CUTS):
            at = cut(c, width)
            arrived(wo_own, wo_ref, CUTS + c, (slice(None), at))
            sent_ref[:, at] = dot(act, wo_ref[:, at], 1, 0).astype(BF16)
    for copy in copies:
        copy.wait()


def backward_kernel(*refs, first, streamed):
    if streamed:
        wi_ref, wo_ref, w_sems = refs[-3:]
        g_ref, slope_in, act_in, low_in_in, wo_hbm, wi_hbm, *refs = refs[:-3]
        width = g_ref.shape[1]
        for c in range(CUTS):
            at = (cut(c, width),)
            pltpu.make_async_copy(wo_hbm.at[at], wo_ref.at[at], w_sems.at[c]).start()
        for c in range(CUTS):
            at = (slice(None), cut(c, width))
            pltpu.make_async_copy(wi_hbm.at[at], wi_ref.at[at], w_sems.at[CUTS + c]).start()
    else:
        wi_hbm = wo_hbm = None
        g_ref, slope_in, act_in, low_in_in, wo_ref, *refs = refs
        wi_ref, refs = (None, refs) if first else (refs[0], refs[1:])

    def arrived(source, held, n, at):
        if streamed:
            pltpu.make_async_copy(source.at[at], held.at[at], w_sems.at[n]).wait()

    di_ref, ui_ref, do_ref, uo_ref, g_low_out_ref, grad_ui_out, grad_do_out, g_out, *rest = refs
    part_ref, rest = (None, rest) if first else (rest[0], rest[1:])
    act_ref, slope_ref, low_in_ref, g_low_ref, grad_ui, grad_do, io_sems = rest
    width = g_ref.shape[1]
    slope_copy = keep(slope_in, slope_ref, io_sems.at[1])
    low_in_copy = keep(low_in_in, low_in_ref, io_sems.at[2])
    act_copy = keep(act_in, act_ref, io_sems.at[0])
    g_copy = keep(g_ref, g_out, io_sems.at[6])
    g_low_out = dot(g_ref[...], uo_ref[...], 1, 1).astype(BF16)
    g_act = dot(g_low_out, do_ref[...], 1, 0)
    for c in range(CUTS if streamed else 1):
        at = cut(c, width) if streamed else slice(None)
        arrived(wo_hbm, wo_ref, c, (at,))
        g_act = g_act + dot(g_ref[:, at], wo_ref[at], 1, 0)
    slope_copy.wait()
    g_pre = (g_act * slope_ref[...]).astype(BF16)
    g_low_ref[...] = dot(ui_ref[...], g_pre, 1, 1).astype(BF16)
    copies = [g_copy, keep(g_low_ref, g_low_out_ref, io_sems.at[3])]
    low_in_copy.wait()
    grad_ui[...] = dot(low_in_ref[...], g_pre, 0, 0)
    copies.append(keep(grad_ui, grad_ui_out, io_sems.at[4]))
    act_copy.wait()
    grad_do[...] = dot(g_low_out, act_ref[...], 0, 0)
    copies.append(keep(grad_do, grad_do_out, io_sems.at[5]))
    if not first:
        g_low_in = dot(g_pre, ui_ref[...], 1, 1).astype(BF16)
        for c in range(CUTS if streamed else PARTS):
            at = (slice(None), cut(c, width, CUTS if streamed else PARTS))
            arrived(wi_hbm, wi_ref, CUTS + c, at)
            part = dot(g_pre, wi_ref[at], 1, 0) + dot(g_low_in, di_ref[at], 1, 0)
            part_ref[at] = part.astype(BF16)
    for copy in copies:
        copy.wait()


def block_cost(rows, width, cols, matmuls):
    return pl.CostEstimate(
        flops=2 * matmuls * rows * width * cols,
        bytes_accessed=2 * matmuls * width * cols,
        transcendentals=rows * cols,
    )


def in_vmem(*arrays):
    return [pltpu.with_memory_space_constraint(a, pltpu.VMEM) for a in arrays]


def block_forward(u, weights, low, own=None):
    rows, width = u.shape
    streamed, last = own is not None, len(weights) == 1
    rank, cols = low[1].shape
    kept = [((rows, cols), BF16), ((rows, cols), F32), ((rows, rank), BF16), ((rank, rows), BF16)]
    out = [shape_of(*s, dtype=t) for s, t in kept] + [shape_of(rows, width)]
    out += [] if last else [shape_of(rows, width + PAD)]
    stream_scratch = [
        pltpu.VMEM((width, cols), BF16),
        pltpu.VMEM((cols, width), BF16),
        pltpu.SemaphoreType.DMA((2 * CUTS,)),
    ]
    first_specs = [SMEM, VMEM] + [HBM] * 4 if streamed else [VMEM] * (1 + len(weights))
    return pl.pallas_call(
        functools.partial(forward_kernel, last=last, streamed=streamed),
        out_shape=out,
        in_specs=first_specs + [VMEM] * 3,
        out_specs=[HBM] * (len(kept) + 1) + ([] if last else [VMEM]),
        scratch_shapes=[
            *(pltpu.VMEM(s, t) for s, t in kept),
            pltpu.SemaphoreType.DMA((len(kept) + 1,)),
            *(stream_scratch if streamed else []),
        ],
        compiler_params=PARAMS,
        cost_estimate=block_cost(rows, width, cols, 1 if last else 2),
        name="block_forward",
    )(*((own, u, *in_hbm(*weights)) if streamed else (u, *in_vmem(*weights))), *low[:3])


def block_backward(g, acts, weights, low, streamed):
    rows, width = g.shape
    first = len(weights) == 1
    rank, cols = low[1].shape
    kept = [((rank, rows), BF16), ((rank, cols), F32), ((rank, cols), F32)]
    out = [shape_of(*s, dtype=t) for s, t in kept] + [shape_of(rows, width)]
    out += [] if first else [shape_of(rows, width)]
    act, slope, low_in = acts
    stream_scratch = [
        pltpu.VMEM((cols, width), BF16),
        pltpu.VMEM((width, cols), BF16),
        pltpu.SemaphoreType.DMA((2 * CUTS,)),
    ]
    return pl.pallas_call(
        functools.partial(backward_kernel, first=first, streamed=streamed),
        out_shape=out,
        in_specs=[VMEM] + [HBM] * 3 + [HBM if streamed else VMEM] * len(weights) + [VMEM] * 4,
        out_specs=[HBM] * (len(kept) + 1) + ([] if first else [VMEM]),
        scratch_shapes=[
            pltpu.VMEM((rows, cols), BF16),
            pltpu.VMEM((rows, cols), F32),
            pltpu.VMEM((rows, rank), BF16),
            *(pltpu.VMEM(s, t) for s, t in kept),
            pltpu.SemaphoreType.DMA((7,)),
            *(stream_scratch if streamed else []),
        ],
        compiler_params=PARAMS,
        cost_estimate=block_cost(rows, width, cols, len(weights)),
        name="block_backward",
    )(g, slope, act, low_in, *(in_hbm if streamed else in_vmem)(*weights), *low)


def ready_kernel(flag_ref, *refs, order):
    if order:
        ordered, wi_buf, wo_buf, buf_sems = refs[8:12], *refs[-3:]
        refs = refs[:8] + refs[12:-3]

        @pl.when(flag_ref[5] == 1)
        def _():
            order_weights(flag_ref, refs[:4], ordered, (wi_buf, wo_buf), buf_sems)

    turn_weights(flag_ref, *refs)


def order_weights(flag_ref, refs, outs, bufs, sems):
    sources = ((refs[0], refs[1], bufs[0]), (refs[2], refs[3], bufs[1]))
    for i in range(2):
        for k, (ours, theirs, buf) in enumerate(sources):
            if i:
                pltpu.make_async_copy(buf, outs[k], sems.at[2 + k]).wait()
            fetch(flag_ref[0] == i, ours, theirs, buf, sems.at[k])
        for k, (ours, theirs, buf) in enumerate(sources):
            pltpu.make_async_copy(ours, buf, sems.at[k]).wait()
            pltpu.make_async_copy(buf, outs[2 * i + k], sems.at[2 + k]).start()
    for k, (ours, theirs, buf) in enumerate(sources):
        pltpu.make_async_copy(buf, outs[2 + k], sems.at[2 + k]).wait()


def turn_weights(flag_ref, *refs):
    narrow_buf, wide_buf, in_sems, out_sems = refs[-4:]
    outs, sources = refs[-8:-4], refs[:4]
    step = narrow_buf.shape[1]

    def turn(own, ours, theirs, target, in_buf, out_buf, by_rows):
        count = ours.shape[0 if by_rows else 1] // step

        def cut_of(ref, c, rows):
            at = pl.ds(pl.multiple_of(c * step, step), step)
            return ref.at[at] if rows else ref.at[:, at]

        def come(c):
            slot = lax.rem(c, 2)
            source, other = (cut_of(ref, c, by_rows) for ref in (ours, theirs))
            fetch(own, source, other, in_buf.at[slot], in_sems.at[slot])

        def going(c, slot):
            target_cut = cut_of(target, c, not by_rows)
            return pltpu.make_async_copy(out_buf.at[slot], target_cut, out_sems.at[slot])

        come(0)

        def body(c, carry):
            slot = lax.rem(c, 2)

            @pl.when(c + 1 < count)
            def _():
                come(c + 1)

            source = cut_of(ours, c, by_rows)
            pltpu.make_async_copy(source, in_buf.at[slot], in_sems.at[slot]).wait()

            @pl.when(c >= 2)
            def _():
                going(c - 2, slot).wait()

            out_buf[slot] = in_buf[slot].T
            going(c, slot).start()
            return carry

        lax.fori_loop(0, count, body, 0)
        going(count - 2, count % 2).wait()
        going(count - 1, 1 - count % 2).wait()

    for i in range(2):
        own = flag_ref[0] == i
        into = functools.partial(turn, own, *sources[:2], outs[2 * i], narrow_buf, wide_buf, True)
        pl.when(flag_ref[1 + 2 * i] == 1)(into)
        out = functools.partial(
            turn, own, *sources[2:], outs[2 * i + 1], wide_buf, narrow_buf, False
        )
        pl.when(flag_ref[2 + 2 * i] == 1)(out)


def ready_weights(flag, weights, held):
    width, cols = weights[0].shape
    step = 384
    turned = [shape_of(cols, width), shape_of(width, cols)] * 2
    ordered = [] if held else [shape_of(width, cols), shape_of(cols, width)] * 2
    buffers = [
        pltpu.VMEM((width, cols), BF16),
        pltpu.VMEM((cols, width), BF16),
        pltpu.SemaphoreType.DMA((4,)),
    ]
    out = pl.pallas_call(
        functools.partial(ready_kernel, order=not held),
        out_shape=turned + ordered,
        in_specs=[SMEM] + [HBM] * (4 + len(held)),
        out_specs=[HBM] * (4 + len(ordered)),
        scratch_shapes=[
            pltpu.VMEM((2, step, cols), BF16),
            pltpu.VMEM((2, cols, step), BF16),
            pltpu.SemaphoreType.DMA((2,)),
            pltpu.SemaphoreType.DMA((2,)),
            *([] if held else buffers),
        ],
        input_output_aliases={5 + k: k for k in range(len(held))},
        compiler_params=PARAMS,
        name="ready_weights",
    )(flag, *in_hbm(*weights), *held)
    return tuple(out[:4]), tuple(out[4:])


def summed(got_ref, own_rows, at):
    total = None
    for k in range(0, got_ref.shape[0], PAIR):
        part = got_ref[k : k + PAIR, at].astype(F32)
        part = part.reshape(PAIR // own_rows, own_rows, part.shape[1]).sum(0)
        total = part if total is None else total + part
    return total


def spread(out_ref, rows):
    pair = jnp.concatenate([rows] * (PAIR // rows.shape[0]), axis=0).astype(BF16)
    for k in range(0, out_ref.shape[0], PAIR):
        out_ref[k : k + PAIR] = pair


def modulated(wide, mod_ref):
    return rms_stats(wide)[0] * (1.0 + mod_ref[1:2]) + mod_ref[0:1]


def first_rows_kernel(ids_ref, counts_ref, x_ref, e_ref, out_ref, x_out, e_out, mask_out):
    at_start, tp_pos, mb = ids_ref[0], ids_ref[2], ids_ref[3]
    own_rows = x_ref.shape[1]
    row = tp_pos * own_rows + lax.broadcasted_iota(jnp.int32, (own_rows, 1), 0)
    mask = (row < counts_ref[mb]).astype(F32)
    mask_out[...] = mask
    x = x_ref[mb].astype(F32) * mask
    e = e_ref[mb].astype(F32) * mask
    x_out[...] = x.astype(BF16)
    e_out[...] = e.astype(BF16)
    spread(out_ref, jnp.where(at_start == 1, x, e))


def modulate_kernel(x_ref, mod_ref, out_ref):
    out_ref[...] = modulated(x_ref[...].astype(F32), mod_ref).astype(BF16)


def gate_kernel(e_ref, mod_ref, out_ref):
    out_ref[...] = (mod_ref[2:3] * e_ref[...].astype(F32)).astype(BF16)


def pack_kernel(ids_ref, jobs_ref, *refs):
    sources, ours, theirs, sems = refs[:-3], refs[-3], refs[-2], refs[-1]
    mb = ids_ref[3]
    copies = []
    for n, (job, out) in enumerate(((jobs_ref[mb], ours), (jobs_ref[1 - mb], theirs))):
        start = 0
        for k, source in enumerate(sources):
            at = pl.ds(start, source.shape[2])
            copies.append(keep(source.at[job], out.at[:, at], sems.at[n * len(sources) + k]))
            start += source.shape[2]
    for copy in copies:
        copy.wait()


def rows_in_kernel(x_ref, mod_ref, out_ref):
    spread(out_ref, modulated(x_ref[...].astype(F32), mod_ref))


def gate_rows_kernel(e_ref, mod_ref, out_ref):
    spread(out_ref, mod_ref[2:3] * e_ref[...].astype(F32))


def forward_rows_kernel(got_ref, x_ref, mask_ref, mod_ref, uo_ref, next_ref, x_out, *outs):
    own_rows, width = x_ref.shape
    rank = uo_ref.shape[0]
    low = summed(got_ref, own_rows, pl.ds(width, PAD)).astype(BF16)[:, :rank]
    branch = summed(got_ref, own_rows, pl.ds(0, width)) + dot(low, uo_ref[...], 1, 0)
    x = x_ref[...].astype(F32) + mod_ref[2:3] * branch * mask_ref[...]
    x = x.astype(BF16)
    x_out[...] = x
    if outs:
        x_saved, spread_out = outs
        x_saved[...] = x_ref[...]
        spread(spread_out, modulated(x.astype(F32), next_ref))


def backward_rows_kernel(got_ref, e_ref, x_ref, mod_ref, next_ref, e_out, *spread_out):
    own_rows, width = x_ref.shape
    normed, inv_rms = rms_stats(x_ref[...].astype(F32))
    q = summed(got_ref, own_rows, pl.ds(0, width)) * (1.0 + mod_ref[1:2])
    mean = jnp.mean(q * normed, axis=-1, keepdims=True)
    e = (e_ref[...].astype(F32) + inv_rms * (q - normed * mean)).astype(BF16)
    e_out[...] = e
    for out_ref in spread_out:
        spread(out_ref, next_ref[2:3] * e.astype(F32))


def narrow_kernel(*refs):
    parts, out_ref = refs[:-1], refs[-1]
    rows = jnp.concatenate([part[...].astype(F32) for part in parts], axis=0).astype(BF16)
    for k in range(0, out_ref.shape[0], rows.shape[0]):
        out_ref[k : k + rows.shape[0]] = rows


def gradients_kernel(ids_ref, got_ref, *refs):
    per_block, (ours, theirs) = refs[:4], refs[4:]
    width = per_block[0].shape[1]
    rank = ours.shape[0]
    deep = 4 * rank
    total = None
    for k in range(0, got_ref.shape[0], deep):
        part = got_ref[k : k + deep].astype(F32)
        total = part if total is None else total + part
    for i in range(2):
        g_ref, u_ref = per_block[2 * i : 2 * i + 2]
        low_out = total[i * rank : (i + 1) * rank].astype(BF16)
        g_low = total[(2 + i) * rank : (3 + i) * rank]
        high = g_low.astype(BF16)
        rest = g_low - high.astype(F32)
        both = jnp.concatenate([high.astype(F32), rest], axis=0).astype(BF16)
        both = dot(both, u_ref[...], 1, 0)
        grads = (both[:rank] + both[rank:], dot(low_out, g_ref[...], 1, 0))

        def put(out, grads=grads):
            for k, grad in enumerate(grads):
                out[:, k * width : (k + 1) * width] = grad

        pl.when(ids_ref[1] == i)(functools.partial(put, ours))
        pl.when(ids_ref[1] != i)(functools.partial(put, theirs))


def choose_kernel(ids_ref, *refs):
    blocks, (ours, theirs) = refs[:4], refs[4:]
    cols = blocks[0].shape[1]
    for i in range(2):

        def put(out, i=i):
            for k in range(2):
                out[:, k * cols : (k + 1) * cols] = blocks[2 * i + k][...]

        pl.when(ids_ref[1] == i)(functools.partial(put, ours))
        pl.when(ids_ref[1] != i)(functools.partial(put, theirs))


def split_kernel(ids_ref, jobs_ref, ours, theirs, ui_ref, do_ref):
    mb, cols = ids_ref[3], ui_ref.shape[2]
    for out in (ui_ref, do_ref):
        out[...] = jnp.zeros(out.shape, F32)
    for job, grads in ((jobs_ref[mb], ours), (jobs_ref[1 - mb], theirs)):
        ui_ref[job] += grads[:, :cols]
        do_ref[job] += grads[:, cols:]


def owned_kernel(ids_ref, jobs_ref, ours, theirs, di_ref, uo_ref):
    tp_pos, mb = ids_ref[2], ids_ref[3]
    owners, _, width = di_ref.shape
    for out in (di_ref, uo_ref):
        out[...] = jnp.zeros(out.shape, F32)
    for job, grads in ((jobs_ref[mb], ours), (jobs_ref[1 - mb], theirs)):
        place = job - tp_pos * owners

        def owned(place=place, grads=grads):
            di_ref[place] += grads[:, :width]
            uo_ref[place] += grads[:, width:]

        pl.when((place >= 0) & (place < owners))(owned)


def rows_call(kernel, out, *operands, scalars=0, cost=None):
    return pl.pallas_call(
        kernel,
        out_shape=out,
        in_specs=[SMEM] * scalars + [VMEM] * (len(operands) - scalars),
        out_specs=jax.tree.map(lambda _: VMEM, out),
        compiler_params=PARAMS,
        cost_estimate=cost,
        name=kernel.__name__,
    )(*operands)


def exchanged(parts, tp):
    rows, width = parts.shape
    got = lax.all_to_all(parts.reshape(tp, rows // tp, width), "tp", 0, 0)
    return got.reshape(rows, width)


def shards(
    latents,
    cotangent,
    token_counts,
    job_ids,
    modulation,
    w_in,
    w_out,
    down_in,
    up_in,
    down_out,
    up_out,
):
    tp = lax.axis_size("tp")
    segments = lax.axis_size("segment")
    planes = segments // 2
    seg = lax.axis_index("segment")
    plane, core = seg // 2, seg % 2
    tp_pos = lax.axis_index("tp")
    micro, own_rows, width = latents.shape
    cols = w_in.shape[2]
    jobs, rank = down_in.shape[1], down_in.shape[2]
    rows = own_rows * tp
    swap = [(s, s ^ 1) for s in range(segments)]
    onward = [(s, (s + 2) % segments) for s in range(segments)]
    across = [(s, d ^ 1) for s, d in onward]
    last_plane = planes - 1

    mb = core ^ sum((plane == p).astype(core.dtype) for p in range(planes) if CROSSED[p])
    ids = jnp.stack([(plane == 0).astype(jnp.int32), core, tp_pos, mb]).astype(jnp.int32)
    full = shape_of(rows, width)
    some = shape_of(own_rows, width)
    w_first = (w_in[0], lax.ppermute(w_in[0], "segment", swap))
    w_second = (w_out[0], lax.ppermute(w_out[0], "segment", swap))

    ends, x, e_last, mask = rows_call(
        first_rows_kernel,
        [full, some, some, shape_of(own_rows, 1, dtype=F32)],
        ids,
        token_counts,
        latents,
        cotangent,
        scalars=2,
    )
    ends, ids, mod = lax.optimization_barrier((ends, ids, modulation[0]))
    mod_other = lax.ppermute(mod, "segment", swap)
    mods = [jnp.where(core == i, mod, mod_other)[mb] for i in range(2)]

    adapters = [a[0] for a in (down_in, up_in, down_out, up_out)]
    packed = shape_of(rank, sum(a.shape[2] for a in adapters))
    low_own, low_sent = pl.pallas_call(
        pack_kernel,
        out_shape=[packed, packed],
        in_specs=[SMEM, SMEM] + [HBM] * len(adapters),
        out_specs=[VMEM, VMEM],
        scratch_shapes=[pltpu.SemaphoreType.DMA((2 * len(adapters),))],
        compiler_params=PARAMS,
        cost_estimate=pl.CostEstimate(
            flops=0, bytes_accessed=4 * math.prod(packed.shape), transcendentals=0
        ),
        name="pack_kernel",
    )(ids, job_ids, *in_hbm(*adapters))
    low_other = lax.ppermute(low_sent, "segment", swap)
    cuts = (width, width + cols, width + 2 * cols)
    lows = [
        jnp.split(jnp.where(core == i, low_own, low_other), cuts, axis=1) for i in range(2)
    ]

    ends = exchanged(ends, tp)
    ahead = pl.CostEstimate(
        flops=16 * rows * width * cols, bytes_accessed=16 * width * cols, transcendentals=rows * width
    )
    owns = [(core == i).astype(jnp.int32).reshape(1) for i in range(2)]
    late, early = plane >= planes // 2, (plane == 0) & (core == STAGGERED)
    flag = jnp.stack([core, late | early, late, late, late, plane > 0]).astype(jnp.int32)
    ends, flag = lax.optimization_barrier((ends, flag))
    (turned, ordered), x = lax.optimization_barrier(
        (ready_weights(flag, (*w_first, *w_second), ()), x)
    )

    def forward_plane(x, ordered, p):
        saved = []
        for i in range(2):
            if i:
                u = exchanged(sent, tp)
            elif p == 0:
                u = rows_call(modulate_kernel, full, ends, mods[0])
            else:
                u = exchanged(rows_call(rows_in_kernel, full, x, mods[0], cost=ahead), tp)
            last = p == last_plane and i == 1
            if p == 0:
                done = block_forward(u, (*w_first, *w_second), lows[i], owns[i])
            else:
                pair = ordered[2 * i : 2 * i + 2]
                done = block_forward(u, pair[:1] if last else pair, lows[i])
            act, slope, low_in, low_part, u, *part = done
            kept = (u, (act, slope, low_in), low_part)
            if last:
                saved.append((x, *kept))
                break
            got = exchanged(part[0], tp)
            if i == 0:
                x_next, x, sent = rows_call(
                    forward_rows_kernel,
                    [some, some, full],
                    got,
                    x,
                    mask,
                    mods[0],
                    lows[0][3],
                    mods[1],
                )
            else:
                (x_next,) = rows_call(
                    forward_rows_kernel, [some], got, x, mask, mods[1], lows[1][3], mods[1]
                )
            saved.append((x, *kept))
            x = x_next
        return x, tuple(saved)

    def backward_plane(e, saved, turned, p):
        kept = [None, None]
        for i in (1, 0):
            if i == 0:
                g = exchanged(sent, tp)
            elif p == last_plane:
                gathered, _ = lax.optimization_barrier((ends, saved[1][3]))
                g = rows_call(gate_kernel, full, gathered, mods[1])
            else:
                g = exchanged(rows_call(gate_rows_kernel, full, e, mods[1], cost=ahead), tp)
            x, u, acts, low_part = saved[i]
            first = p == 0 and i == 0
            w_in_t, w_out_t = turned[2 * i : 2 * i + 2]
            g_low_in, grad_ui, grad_do, g, *part = block_backward(
                g, acts, [w_out_t] if first else [w_out_t, w_in_t], lows[i], False
            )
            kept[i] = (g, g_low_in, grad_ui, grad_do)
            if first:
                break
            got = exchanged(part[0], tp)
            out = [some, full] if i else [some]
            e, *sent = rows_call(backward_rows_kernel, out, got, e, x, mods[i], mods[0])
            sent = sent[0] if sent else None
        return e, tuple(kept)

    def zeros(*shape, dtype=BF16):
        return jnp.zeros(shape, dtype)

    def no_saved():
        acts = (zeros(rows, cols), zeros(rows, cols, dtype=F32), zeros(rows, rank))
        return (zeros(own_rows, width), zeros(rows, width), acts, zeros(rank, rows))

    def no_kept():
        return (
            zeros(rows, width),
            zeros(rank, rows),
            zeros(rank, cols, dtype=F32),
            zeros(rank, cols, dtype=F32),
        )

    saved = (no_saved(), no_saved())
    kept = (no_kept(), no_kept())
    for p in range(last_plane):
        x, saved = lax.cond(
            plane == p,
            lambda x, saved: forward_plane(x, ordered, p),
            lambda x, saved: (x, saved),
            x,
            saved,
        )
        x = lax.ppermute(x, "segment", across if CROSSED[p] != CROSSED[p + 1] else onward)
        if p == planes // 2 - 1:
            rest = ~late
            flag = jnp.stack([core, rest & ~early, rest, rest, rest]).astype(jnp.int32)
            (turned, _), x = lax.optimization_barrier(
                (ready_weights(flag, (*w_first, *w_second), turned), x)
            )

    def turn(x, saved, kept):
        x, saved = forward_plane(x, ordered, last_plane)
        e, kept = backward_plane(e_last, saved, turned, last_plane)
        return e, saved, kept

    e, saved, kept = lax.cond(
        plane == last_plane, turn, lambda x, saved, kept: (x, saved, kept), x, saved, kept
    )
    for p in range(last_plane - 1, -1, -1):
        pairs = across if CROSSED[p] != CROSSED[p + 1] else onward
        e = lax.ppermute(e, "segment", [(d, s) for s, d in pairs])
        e, kept = lax.cond(
            plane == p,
            lambda e, saved, kept: backward_plane(e, saved, turned, p),
            lambda e, saved, kept: (e, kept),
            e,
            saved,
            kept,
        )

    narrow = (saved[0][3], saved[1][3], kept[0][1], kept[1][1])
    narrow_out = shape_of(tp * 4 * rank, rows)
    spread_out = rows_call(narrow_kernel, narrow_out, *narrow, cost=ahead)
    pair = [shape_of(rank, 2 * cols, dtype=F32)] * 2
    split_mine, split_sent = rows_call(
        choose_kernel, pair, ids, *kept[0][2:], *kept[1][2:], scalars=1
    )
    split_theirs = lax.ppermute(split_sent, "segment", swap)
    got = exchanged(spread_out, tp)
    wide = [shape_of(rank, 2 * width, dtype=F32)] * 2
    per_block = [a for i in range(2) for a in in_vmem(kept[i][0], saved[i][1])]
    mine, sent = rows_call(gradients_kernel, wide, ids, got, *per_block, scalars=1)
    theirs = lax.ppermute(sent, "segment", swap)
    split = [shape_of(jobs, rank, cols, dtype=F32)] * 2
    grad_ui, grad_do = rows_call(
        split_kernel,
        split,
        ids,
        job_ids,
        split_mine,
        split_theirs,
        scalars=2,
        cost=pl.CostEstimate(flops=0, bytes_accessed=8 * jobs * rank * cols, transcendentals=0),
    )
    owned = [shape_of(jobs // tp, rank, width, dtype=F32)] * 2
    grad_di, grad_uo = rows_call(
        owned_kernel, owned, ids, job_ids, mine, theirs, scalars=2
    )
    return tuple(grad[None] for grad in (grad_di, grad_ui, grad_do, grad_uo))


def solution(mesh):
    return jax.shard_map(
        shards,
        mesh=mesh,
        in_specs=(
            P(None, "tp", None),
            P(None, "tp", None),
            P(),
            P(),
            P("segment", None, None, None),
            P("segment", None, "tp"),
            P("segment", "tp", None),
            P("segment", None, None, None),
            P("segment", None, None, "tp"),
            P("segment", None, None, "tp"),
            P("segment", None, None, None),
        ),
        out_specs=(
            P("segment", "tp", None, None),
            P("segment", None, None, "tp"),
            P("segment", None, None, "tp"),
            P("segment", "tp", None, None),
        ),
        check_vma=False,
    )
```

```python
import functools
import math

import jax
import jax.numpy as jnp
from jax import lax
from jax.experimental import pallas as pl
from jax.experimental.pallas import tpu as pltpu
from jax.sharding import PartitionSpec as P

EPS = 1e-06
ROOT_TWO_PI = math.sqrt(2.0 / math.pi)
F32 = jnp.float32
BF16 = jnp.bfloat16
PAD = 128
CUTS = 2
PARTS = 4
PAIR = 16
CROSSED = (0, 1, 0, 1)
STAGGERED = 0
VMEM = pl.BlockSpec(memory_space=pltpu.VMEM)
HBM = pl.BlockSpec(memory_space=pltpu.HBM)
SMEM = pl.BlockSpec(memory_space=pltpu.SMEM)
PARAMS = pltpu.CompilerParams(vmem_limit_bytes=16 * 1024 * 1024)


def shape_of(*shape, dtype=BF16):
    return jax.ShapeDtypeStruct(shape, dtype)


def gelu_and_slope(values):
    inner = ROOT_TWO_PI * (values + 0.044715 * values * values * values)
    tangent = jnp.tanh(inner)
    half = 0.5 * (1.0 + tangent)
    slope = half + 0.5 * values * (1.0 - tangent * tangent) * ROOT_TWO_PI * (
        1.0 + 3.0 * 0.044715 * values * values
    )
    return values * half, slope


def rms_stats(wide):
    inv_rms = lax.rsqrt(jnp.mean(wide * wide, axis=-1, keepdims=True) + EPS)
    return wide * inv_rms, inv_rms


def dot(a, b, a_dim, b_dim):
    return lax.dot_general(a, b, (((a_dim,), (b_dim,)), ((), ())), preferred_element_type=F32)


def fetch(own, ours, theirs, buf, sem):
    @pl.when(own)
    def _():
        pltpu.make_async_copy(ours, buf, sem).start()

    @pl.when(jnp.logical_not(own))
    def _():
        pltpu.make_async_copy(theirs, buf, sem).start()


def cut(c, size, parts=CUTS):
    return pl.ds(c * (size // parts), size // parts)


def keep(buf, out, sem):
    copy = pltpu.make_async_copy(buf, out, sem)
    copy.start()
    return copy


def in_hbm(*arrays):
    return [pltpu.with_memory_space_constraint(a, pltpu.HBM) for a in arrays]


def forward_kernel(*refs, last, streamed):
    if streamed:
        own_ref, u_ref, wi_own, wi_other, wo_own, wo_other, *refs = refs
        wi_ref, wo_ref, w_sems = refs[-3:]
        refs = refs[:-3]
        width = u_ref.shape[1]
        for c in range(CUTS):
            at = (cut(c, width),)
            fetch(own_ref[0] == 1, wi_own.at[at], wi_other.at[at], wi_ref.at[at], w_sems.at[c])
        for c in range(CUTS):
            at = (slice(None), cut(c, width))
            fetch(
                own_ref[0] == 1, wo_own.at[at], wo_other.at[at], wo_ref.at[at], w_sems.at[CUTS + c]
            )
    else:
        u_ref, wi_ref, *refs = refs
        wo_ref, refs = (None, refs) if last else (refs[0], refs[1:])

    def arrived(source, held, n, at):
        if streamed:
            pltpu.make_async_copy(source.at[at], held.at[at], w_sems.at[n]).wait()

    wi_own, wo_own = (wi_own, wo_own) if streamed else (None, None)
    di_ref, ui_ref, do_ref, act_out, slope_out, low_in_out, low_out, u_out, *rest = refs
    sent_ref, rest = (None, rest) if last else (rest[0], rest[1:])
    act_ref, slope_ref, low_in_ref, low_ref, out_sems = rest
    width, rank = u_ref.shape[1], di_ref.shape[0]
    low_in = dot(u_ref[...], di_ref[...], 1, 1).astype(BF16)
    low_in_ref[...] = low_in
    copies = [keep(u_ref, u_out, out_sems.at[4]), keep(low_in_ref, low_in_out, out_sems.at[0])]
    pre = dot(low_in, ui_ref[...], 1, 0)
    for c in range(CUTS if streamed else 1):
        at = cut(c, width) if streamed else slice(None)
        arrived(wi_own, wi_ref, c, (at,))
        pre = pre + dot(u_ref[:, at], wi_ref[at], 1, 0)
    act, slope = gelu_and_slope(pre)
    act = act.astype(BF16)
    act_ref[...] = act
    slope_ref[...] = slope
    copies.append(keep(act_ref, act_out, out_sems.at[1]))
    copies.append(keep(slope_ref, slope_out, out_sems.at[2]))
    low_ref[...] = dot(do_ref[...], act, 1, 1).astype(BF16)
    copies.append(keep(low_ref, low_out, out_sems.at[3]))
    if not last:
        sent_ref[:, width:] = jnp.zeros((sent_ref.shape[0], PAD), BF16)
        sent_ref[:, width : width + rank] = dot(act, do_ref[...], 1, 1).astype(BF16)
        for c in range(CUTS):
            at = cut(c, width)
            arrived(wo_own, wo_ref, CUTS + c, (slice(None), at))
            sent_ref[:, at] = dot(act, wo_ref[:, at], 1, 0).astype(BF16)
    for copy in copies:
        copy.wait()


def backward_kernel(*refs, first, streamed):
    if streamed:
        wi_ref, wo_ref, w_sems = refs[-3:]
        g_ref, slope_in, act_in, low_in_in, wo_hbm, wi_hbm, *refs = refs[:-3]
        width = g_ref.shape[1]
        for c in range(CUTS):
            at = (cut(c, width),)
            pltpu.make_async_copy(wo_hbm.at[at], wo_ref.at[at], w_sems.at[c]).start()
        for c in range(CUTS):
            at = (slice(None), cut(c, width))
            pltpu.make_async_copy(wi_hbm.at[at], wi_ref.at[at], w_sems.at[CUTS + c]).start()
    else:
        wi_hbm = wo_hbm = None
        g_ref, slope_in, act_in, low_in_in, wo_ref, *refs = refs
        wi_ref, refs = (None, refs) if first else (refs[0], refs[1:])

    def arrived(source, held, n, at):
        if streamed:
            pltpu.make_async_copy(source.at[at], held.at[at], w_sems.at[n]).wait()

    di_ref, ui_ref, do_ref, uo_ref, g_low_out_ref, grad_ui_out, grad_do_out, g_out, *rest = refs
    part_ref, rest = (None, rest) if first else (rest[0], rest[1:])
    act_ref, slope_ref, low_in_ref, g_low_ref, grad_ui, grad_do, io_sems = rest
    width = g_ref.shape[1]
    slope_copy = keep(slope_in, slope_ref, io_sems.at[1])
    low_in_copy = keep(low_in_in, low_in_ref, io_sems.at[2])
    act_copy = keep(act_in, act_ref, io_sems.at[0])
    g_copy = keep(g_ref, g_out, io_sems.at[6])
    g_low_out = dot(g_ref[...], uo_ref[...], 1, 1).astype(BF16)
    g_act = dot(g_low_out, do_ref[...], 1, 0)
    for c in range(CUTS if streamed else 1):
        at = cut(c, width) if streamed else slice(None)
        arrived(wo_hbm, wo_ref, c, (at,))
        g_act = g_act + dot(g_ref[:, at], wo_ref[at], 1, 0)
    slope_copy.wait()
    g_pre = (g_act * slope_ref[...]).astype(BF16)
    g_low_ref[...] = dot(ui_ref[...], g_pre, 1, 1).astype(BF16)
    copies = [g_copy, keep(g_low_ref, g_low_out_ref, io_sems.at[3])]
    low_in_copy.wait()
    grad_ui[...] = dot(low_in_ref[...], g_pre, 0, 0)
    copies.append(keep(grad_ui, grad_ui_out, io_sems.at[4]))
    act_copy.wait()
    grad_do[...] = dot(g_low_out, act_ref[...], 0, 0)
    copies.append(keep(grad_do, grad_do_out, io_sems.at[5]))
    if not first:
        g_low_in = dot(g_pre, ui_ref[...], 1, 1).astype(BF16)
        for c in range(CUTS if streamed else PARTS):
            at = (slice(None), cut(c, width, CUTS if streamed else PARTS))
            arrived(wi_hbm, wi_ref, CUTS + c, at)
            part = dot(g_pre, wi_ref[at], 1, 0) + dot(g_low_in, di_ref[at], 1, 0)
            part_ref[at] = part.astype(BF16)
    for copy in copies:
        copy.wait()


def block_cost(rows, width, cols, matmuls):
    return pl.CostEstimate(
        flops=2 * matmuls * rows * width * cols,
        bytes_accessed=2 * matmuls * width * cols,
        transcendentals=rows * cols,
    )


def in_vmem(*arrays):
    return [pltpu.with_memory_space_constraint(a, pltpu.VMEM) for a in arrays]


def block_forward(u, weights, low, own=None):
    rows, width = u.shape
    streamed, last = own is not None, len(weights) == 1
    rank, cols = low[1].shape
    kept = [((rows, cols), BF16), ((rows, cols), F32), ((rows, rank), BF16), ((rank, rows), BF16)]
    out = [shape_of(*s, dtype=t) for s, t in kept] + [shape_of(rows, width)]
    out += [] if last else [shape_of(rows, width + PAD)]
    stream_scratch = [
        pltpu.VMEM((width, cols), BF16),
        pltpu.VMEM((cols, width), BF16),
        pltpu.SemaphoreType.DMA((2 * CUTS,)),
    ]
    first_specs = [SMEM, VMEM] + [HBM] * 4 if streamed else [VMEM] * (1 + len(weights))
    return pl.pallas_call(
        functools.partial(forward_kernel, last=last, streamed=streamed),
        out_shape=out,
        in_specs=first_specs + [VMEM] * 3,
        out_specs=[HBM] * (len(kept) + 1) + ([] if last else [VMEM]),
        scratch_shapes=[
            *(pltpu.VMEM(s, t) for s, t in kept),
            pltpu.SemaphoreType.DMA((len(kept) + 1,)),
            *(stream_scratch if streamed else []),
        ],
        compiler_params=PARAMS,
        cost_estimate=block_cost(rows, width, cols, 1 if last else 2),
        name="block_forward",
    )(*((own, u, *in_hbm(*weights)) if streamed else (u, *in_vmem(*weights))), *low[:3])


def block_backward(g, acts, weights, low, streamed):
    rows, width = g.shape
    first = len(weights) == 1
    rank, cols = low[1].shape
    kept = [((rank, rows), BF16), ((rank, cols), F32), ((rank, cols), F32)]
    out = [shape_of(*s, dtype=t) for s, t in kept] + [shape_of(rows, width)]
    out += [] if first else [shape_of(rows, width)]
    act, slope, low_in = acts
    stream_scratch = [
        pltpu.VMEM((cols, width), BF16),
        pltpu.VMEM((width, cols), BF16),
        pltpu.SemaphoreType.DMA((2 * CUTS,)),
    ]
    return pl.pallas_call(
        functools.partial(backward_kernel, first=first, streamed=streamed),
        out_shape=out,
        in_specs=[VMEM] + [HBM] * 3 + [HBM if streamed else VMEM] * len(weights) + [VMEM] * 4,
        out_specs=[HBM] * (len(kept) + 1) + ([] if first else [VMEM]),
        scratch_shapes=[
            pltpu.VMEM((rows, cols), BF16),
            pltpu.VMEM((rows, cols), F32),
            pltpu.VMEM((rows, rank), BF16),
            *(pltpu.VMEM(s, t) for s, t in kept),
            pltpu.SemaphoreType.DMA((7,)),
            *(stream_scratch if streamed else []),
        ],
        compiler_params=PARAMS,
        cost_estimate=block_cost(rows, width, cols, len(weights)),
        name="block_backward",
    )(g, slope, act, low_in, *(in_hbm if streamed else in_vmem)(*weights), *low)


def ready_kernel(flag_ref, *refs, order):
    if order:
        ordered, wi_buf, wo_buf, buf_sems = refs[8:12], *refs[-3:]
        refs = refs[:8] + refs[12:-3]

        @pl.when(flag_ref[5] == 1)
        def _():
            order_weights(flag_ref, refs[:4], ordered, (wi_buf, wo_buf), buf_sems)

    turn_weights(flag_ref, *refs)


def order_weights(flag_ref, refs, outs, bufs, sems):
    sources = ((refs[0], refs[1], bufs[0]), (refs[2], refs[3], bufs[1]))
    for i in range(2):
        for k, (ours, theirs, buf) in enumerate(sources):
            if i:
                pltpu.make_async_copy(buf, outs[k], sems.at[2 + k]).wait()
            fetch(flag_ref[0] == i, ours, theirs, buf, sems.at[k])
        for k, (ours, theirs, buf) in enumerate(sources):
            pltpu.make_async_copy(ours, buf, sems.at[k]).wait()
            pltpu.make_async_copy(buf, outs[2 * i + k], sems.at[2 + k]).start()
    for k, (ours, theirs, buf) in enumerate(sources):
        pltpu.make_async_copy(buf, outs[2 + k], sems.at[2 + k]).wait()


def turn_weights(flag_ref, *refs):
    narrow_buf, wide_buf, in_sems, out_sems = refs[-4:]
    outs, sources = refs[-8:-4], refs[:4]
    step = narrow_buf.shape[1]

    def turn(own, ours, theirs, target, in_buf, out_buf, by_rows):
        count = ours.shape[0 if by_rows else 1] // step

        def cut_of(ref, c, rows):
            at = pl.ds(pl.multiple_of(c * step, step), step)
            return ref.at[at] if rows else ref.at[:, at]

        def come(c):
            slot = lax.rem(c, 2)
            source, other = (cut_of(ref, c, by_rows) for ref in (ours, theirs))
            fetch(own, source, other, in_buf.at[slot], in_sems.at[slot])

        def going(c, slot):
            target_cut = cut_of(target, c, not by_rows)
            return pltpu.make_async_copy(out_buf.at[slot], target_cut, out_sems.at[slot])

        come(0)

        def body(c, carry):
            slot = lax.rem(c, 2)

            @pl.when(c + 1 < count)
            def _():
                come(c + 1)

            source = cut_of(ours, c, by_rows)
            pltpu.make_async_copy(source, in_buf.at[slot], in_sems.at[slot]).wait()

            @pl.when(c >= 2)
            def _():
                going(c - 2, slot).wait()

            out_buf[slot] = in_buf[slot].T
            going(c, slot).start()
            return carry

        lax.fori_loop(0, count, body, 0)
        going(count - 2, count % 2).wait()
        going(count - 1, 1 - count % 2).wait()

    for i in range(2):
        own = flag_ref[0] == i
        into = functools.partial(turn, own, *sources[:2], outs[2 * i], narrow_buf, wide_buf, True)
        pl.when(flag_ref[1 + 2 * i] == 1)(into)
        out = functools.partial(
            turn, own, *sources[2:], outs[2 * i + 1], wide_buf, narrow_buf, False
        )
        pl.when(flag_ref[2 + 2 * i] == 1)(out)


def ready_weights(flag, weights, held):
    width, cols = weights[0].shape
    step = 384
    turned = [shape_of(cols, width), shape_of(width, cols)] * 2
    ordered = [] if held else [shape_of(width, cols), shape_of(cols, width)] * 2
    buffers = [
        pltpu.VMEM((width, cols), BF16),
        pltpu.VMEM((cols, width), BF16),
        pltpu.SemaphoreType.DMA((4,)),
    ]
    out = pl.pallas_call(
        functools.partial(ready_kernel, order=not held),
        out_shape=turned + ordered,
        in_specs=[SMEM] + [HBM] * (4 + len(held)),
        out_specs=[HBM] * (4 + len(ordered)),
        scratch_shapes=[
            pltpu.VMEM((2, step, cols), BF16),
            pltpu.VMEM((2, cols, step), BF16),
            pltpu.SemaphoreType.DMA((2,)),
            pltpu.SemaphoreType.DMA((2,)),
            *([] if held else buffers),
        ],
        input_output_aliases={5 + k: k for k in range(len(held))},
        compiler_params=PARAMS,
        name="ready_weights",
    )(flag, *in_hbm(*weights), *held)
    return tuple(out[:4]), tuple(out[4:])


def summed(got_ref, own_rows, at):
    total = None
    for k in range(0, got_ref.shape[0], PAIR):
        part = got_ref[k : k + PAIR, at].astype(F32)
        part = part.reshape(PAIR // own_rows, own_rows, part.shape[1]).sum(0)
        total = part if total is None else total + part
    return total


def spread(out_ref, rows):
    pair = jnp.concatenate([rows] * (PAIR // rows.shape[0]), axis=0).astype(BF16)
    for k in range(0, out_ref.shape[0], PAIR):
        out_ref[k : k + PAIR] = pair


def modulated(wide, mod_ref):
    return rms_stats(wide)[0] * (1.0 + mod_ref[1:2]) + mod_ref[0:1]


def first_rows_kernel(ids_ref, counts_ref, x_ref, e_ref, out_ref, x_out, e_out, mask_out):
    at_start, tp_pos, mb = ids_ref[0], ids_ref[2], ids_ref[3]
    own_rows = x_ref.shape[1]
    row = tp_pos * own_rows + lax.broadcasted_iota(jnp.int32, (own_rows, 1), 0)
    mask = (row < counts_ref[mb]).astype(F32)
    mask_out[...] = mask
    x = x_ref[mb].astype(F32) * mask
    e = e_ref[mb].astype(F32) * mask
    x_out[...] = x.astype(BF16)
    e_out[...] = e.astype(BF16)
    spread(out_ref, jnp.where(at_start == 1, x, e))


def modulate_kernel(x_ref, mod_ref, out_ref):
    out_ref[...] = modulated(x_ref[...].astype(F32), mod_ref).astype(BF16)


def gate_kernel(e_ref, mod_ref, out_ref):
    out_ref[...] = (mod_ref[2:3] * e_ref[...].astype(F32)).astype(BF16)


def pack_kernel(ids_ref, jobs_ref, *refs):
    sources, ours, theirs, sems = refs[:-3], refs[-3], refs[-2], refs[-1]
    mb = ids_ref[3]
    copies = []
    for n, (job, out) in enumerate(((jobs_ref[mb], ours), (jobs_ref[1 - mb], theirs))):
        start = 0
        for k, source in enumerate(sources):
            at = pl.ds(start, source.shape[2])
            copies.append(keep(source.at[job], out.at[:, at], sems.at[n * len(sources) + k]))
            start += source.shape[2]
    for copy in copies:
        copy.wait()


def rows_in_kernel(x_ref, mod_ref, out_ref):
    spread(out_ref, modulated(x_ref[...].astype(F32), mod_ref))


def gate_rows_kernel(e_ref, mod_ref, out_ref):
    spread(out_ref, mod_ref[2:3] * e_ref[...].astype(F32))


def forward_rows_kernel(got_ref, x_ref, mask_ref, mod_ref, uo_ref, next_ref, x_out, *outs):
    own_rows, width = x_ref.shape
    rank = uo_ref.shape[0]
    low = summed(got_ref, own_rows, pl.ds(width, PAD)).astype(BF16)[:, :rank]
    branch = summed(got_ref, own_rows, pl.ds(0, width)) + dot(low, uo_ref[...], 1, 0)
    x = x_ref[...].astype(F32) + mod_ref[2:3] * branch * mask_ref[...]
    x = x.astype(BF16)
    x_out[...] = x
    if outs:
        x_saved, spread_out = outs
        x_saved[...] = x_ref[...]
        spread(spread_out, modulated(x.astype(F32), next_ref))


def backward_rows_kernel(got_ref, e_ref, x_ref, mod_ref, next_ref, e_out, *spread_out):
    own_rows, width = x_ref.shape
    normed, inv_rms = rms_stats(x_ref[...].astype(F32))
    q = summed(got_ref, own_rows, pl.ds(0, width)) * (1.0 + mod_ref[1:2])
    mean = jnp.mean(q * normed, axis=-1, keepdims=True)
    e = (e_ref[...].astype(F32) + inv_rms * (q - normed * mean)).astype(BF16)
    e_out[...] = e
    for out_ref in spread_out:
        spread(out_ref, next_ref[2:3] * e.astype(F32))


def narrow_kernel(*refs):
    parts, out_ref = refs[:-1], refs[-1]
    rows = jnp.concatenate([part[...].astype(F32) for part in parts], axis=0).astype(BF16)
    for k in range(0, out_ref.shape[0], rows.shape[0]):
        out_ref[k : k + rows.shape[0]] = rows


def gradients_kernel(ids_ref, got_ref, *refs):
    per_block, (ours, theirs) = refs[:4], refs[4:]
    width = per_block[0].shape[1]
    rank = ours.shape[0]
    deep = 4 * rank
    total = None
    for k in range(0, got_ref.shape[0], deep):
        part = got_ref[k : k + deep].astype(F32)
        total = part if total is None else total + part
    for i in range(2):
        g_ref, u_ref = per_block[2 * i : 2 * i + 2]
        low_out = total[i * rank : (i + 1) * rank].astype(BF16)
        g_low = total[(2 + i) * rank : (3 + i) * rank]
        high = g_low.astype(BF16)
        rest = g_low - high.astype(F32)
        both = jnp.concatenate([high.astype(F32), rest], axis=0).astype(BF16)
        both = dot(both, u_ref[...], 1, 0)
        grads = (both[:rank] + both[rank:], dot(low_out, g_ref[...], 1, 0))

        def put(out, grads=grads):
            for k, grad in enumerate(grads):
                out[:, k * width : (k + 1) * width] = grad

        pl.when(ids_ref[1] == i)(functools.partial(put, ours))
        pl.when(ids_ref[1] != i)(functools.partial(put, theirs))


def choose_kernel(ids_ref, *refs):
    blocks, (ours, theirs) = refs[:4], refs[4:]
    cols = blocks[0].shape[1]
    for i in range(2):

        def put(out, i=i):
            for k in range(2):
                out[:, k * cols : (k + 1) * cols] = blocks[2 * i + k][...]

        pl.when(ids_ref[1] == i)(functools.partial(put, ours))
        pl.when(ids_ref[1] != i)(functools.partial(put, theirs))


def split_kernel(ids_ref, jobs_ref, ours, theirs, ui_ref, do_ref):
    mb, cols = ids_ref[3], ui_ref.shape[2]
    for out in (ui_ref, do_ref):
        out[...] = jnp.zeros(out.shape, F32)
    for job, grads in ((jobs_ref[mb], ours), (jobs_ref[1 - mb], theirs)):
        ui_ref[job] += grads[:, :cols]
        do_ref[job] += grads[:, cols:]


def owned_kernel(ids_ref, jobs_ref, ours, theirs, di_ref, uo_ref):
    tp_pos, mb = ids_ref[2], ids_ref[3]
    owners, _, width = di_ref.shape
    for out in (di_ref, uo_ref):
        out[...] = jnp.zeros(out.shape, F32)
    for job, grads in ((jobs_ref[mb], ours), (jobs_ref[1 - mb], theirs)):
        place = job - tp_pos * owners

        def owned(place=place, grads=grads):
            di_ref[place] += grads[:, :width]
            uo_ref[place] += grads[:, width:]

        pl.when((place >= 0) & (place < owners))(owned)


def rows_call(kernel, out, *operands, scalars=0, cost=None):
    return pl.pallas_call(
        kernel,
        out_shape=out,
        in_specs=[SMEM] * scalars + [VMEM] * (len(operands) - scalars),
        out_specs=jax.tree.map(lambda _: VMEM, out),
        compiler_params=PARAMS,
        cost_estimate=cost,
        name=kernel.__name__,
    )(*operands)


def exchanged(parts, tp):
    rows, width = parts.shape
    got = lax.all_to_all(parts.reshape(tp, rows // tp, width), "tp", 0, 0)
    return got.reshape(rows, width)


def shards(
    latents,
    cotangent,
    token_counts,
    job_ids,
    modulation,
    w_in,
    w_out,
    down_in,
    up_in,
    down_out,
    up_out,
):
    tp = lax.axis_size("tp")
    segments = lax.axis_size("segment")
    planes = segments // 2
    seg = lax.axis_index("segment")
    plane, core = seg // 2, seg % 2
    tp_pos = lax.axis_index("tp")
    micro, own_rows, width = latents.shape
    cols = w_in.shape[2]
    jobs, rank = down_in.shape[1], down_in.shape[2]
    rows = own_rows * tp
    swap = [(s, s ^ 1) for s in range(segments)]
    onward = [(s, (s + 2) % segments) for s in range(segments)]
    across = [(s, d ^ 1) for s, d in onward]
    last_plane = planes - 1

    mb = core ^ sum((plane == p).astype(core.dtype) for p in range(planes) if CROSSED[p])
    ids = jnp.stack([(plane == 0).astype(jnp.int32), core, tp_pos, mb]).astype(jnp.int32)
    full = shape_of(rows, width)
    some = shape_of(own_rows, width)
    w_first = (w_in[0], lax.ppermute(w_in[0], "segment", swap))
    w_second = (w_out[0], lax.ppermute(w_out[0], "segment", swap))

    ends, x, e_last, mask = rows_call(
        first_rows_kernel,
        [full, some, some, shape_of(own_rows, 1, dtype=F32)],
        ids,
        token_counts,
        *in_hbm(latents, cotangent),
        scalars=2,
    )
    ends, ids, mod = lax.optimization_barrier((ends, ids, modulation[0]))
    mod_other = lax.ppermute(mod, "segment", swap)
    mods = [jnp.where(core == i, mod, mod_other)[mb] for i in range(2)]

    adapters = [a[0] for a in (down_in, up_in, down_out, up_out)]
    packed = shape_of(rank, sum(a.shape[2] for a in adapters))
    low_own, low_sent = pl.pallas_call(
        pack_kernel,
        out_shape=[packed, packed],
        in_specs=[SMEM, SMEM] + [HBM] * len(adapters),
        out_specs=[VMEM, VMEM],
        scratch_shapes=[pltpu.SemaphoreType.DMA((2 * len(adapters),))],
        compiler_params=PARAMS,
        cost_estimate=pl.CostEstimate(
            flops=0, bytes_accessed=4 * math.prod(packed.shape), transcendentals=0
        ),
        name="pack_kernel",
    )(ids, job_ids, *in_hbm(*adapters))
    low_other = lax.ppermute(low_sent, "segment", swap)
    cuts = (width, width + cols, width + 2 * cols)
    lows = [
        jnp.split(jnp.where(core == i, low_own, low_other), cuts, axis=1) for i in range(2)
    ]

    ends = exchanged(ends, tp)
    ahead = pl.CostEstimate(
        flops=16 * rows * width * cols, bytes_accessed=16 * width * cols, transcendentals=rows * width
    )
    owns = [(core == i).astype(jnp.int32).reshape(1) for i in range(2)]
    late, early = plane >= planes // 2, (plane == 0) & (core == STAGGERED)
    flag = jnp.stack([core, late | early, late, late, late, plane > 0]).astype(jnp.int32)
    ends, flag = lax.optimization_barrier((ends, flag))
    (turned, ordered), x = lax.optimization_barrier(
        (ready_weights(flag, (*w_first, *w_second), ()), x)
    )

    def forward_plane(x, ordered, p):
        saved = []
        for i in range(2):
            if i:
                u = exchanged(sent, tp)
            elif p == 0:
                u = rows_call(modulate_kernel, full, ends, mods[0])
            else:
                u = exchanged(rows_call(rows_in_kernel, full, x, mods[0], cost=ahead), tp)
            last = p == last_plane and i == 1
            if p == 0:
                done = block_forward(u, (*w_first, *w_second), lows[i], owns[i])
            else:
                pair = ordered[2 * i : 2 * i + 2]
                done = block_forward(u, pair[:1] if last else pair, lows[i])
            act, slope, low_in, low_part, u, *part = done
            kept = (u, (act, slope, low_in), low_part)
            if last:
                saved.append((x, *kept))
                break
            got = exchanged(part[0], tp)
            if i == 0:
                x_next, x, sent = rows_call(
                    forward_rows_kernel,
                    [some, some, full],
                    got,
                    x,
                    mask,
                    mods[0],
                    lows[0][3],
                    mods[1],
                )
            else:
                (x_next,) = rows_call(
                    forward_rows_kernel, [some], got, x, mask, mods[1], lows[1][3], mods[1]
                )
            saved.append((x, *kept))
            x = x_next
        return x, tuple(saved)

    def backward_plane(e, saved, turned, p):
        kept = [None, None]
        for i in (1, 0):
            if i == 0:
                g = exchanged(sent, tp)
            elif p == last_plane:
                gathered, _ = lax.optimization_barrier((ends, saved[1][3]))
                g = rows_call(gate_kernel, full, gathered, mods[1])
            else:
                g = exchanged(rows_call(gate_rows_kernel, full, e, mods[1], cost=ahead), tp)
            x, u, acts, low_part = saved[i]
            first = p == 0 and i == 0
            w_in_t, w_out_t = turned[2 * i : 2 * i + 2]
            g_low_in, grad_ui, grad_do, g, *part = block_backward(
                g, acts, [w_out_t] if first else [w_out_t, w_in_t], lows[i], False
            )
            kept[i] = (g, g_low_in, grad_ui, grad_do)
            if first:
                break
            got = exchanged(part[0], tp)
            out = [some, full] if i else [some]
            e, *sent = rows_call(backward_rows_kernel, out, got, e, x, mods[i], mods[0])
            sent = sent[0] if sent else None
        return e, tuple(kept)

    def zeros(*shape, dtype=BF16):
        return jnp.zeros(shape, dtype)

    def no_saved():
        acts = (zeros(rows, cols), zeros(rows, cols, dtype=F32), zeros(rows, rank))
        return (zeros(own_rows, width), zeros(rows, width), acts, zeros(rank, rows))

    def no_kept():
        return (
            zeros(rows, width),
            zeros(rank, rows),
            zeros(rank, cols, dtype=F32),
            zeros(rank, cols, dtype=F32),
        )

    saved = (no_saved(), no_saved())
    kept = (no_kept(), no_kept())
    for p in range(last_plane):
        x, saved = lax.cond(
            plane == p,
            lambda x, saved: forward_plane(x, ordered, p),
            lambda x, saved: (x, saved),
            x,
            saved,
        )
        x = lax.ppermute(x, "segment", across if CROSSED[p] != CROSSED[p + 1] else onward)
        if p == planes // 2 - 1:
            rest = ~late
            flag = jnp.stack([core, rest & ~early, rest, rest, rest]).astype(jnp.int32)
            (turned, _), x = lax.optimization_barrier(
                (ready_weights(flag, (*w_first, *w_second), turned), x)
            )

    def turn(x, saved, kept):
        x, saved = forward_plane(x, ordered, last_plane)
        e, kept = backward_plane(e_last, saved, turned, last_plane)
        return e, saved, kept

    e, saved, kept = lax.cond(
        plane == last_plane, turn, lambda x, saved, kept: (x, saved, kept), x, saved, kept
    )
    for p in range(last_plane - 1, -1, -1):
        pairs = across if CROSSED[p] != CROSSED[p + 1] else onward
        e = lax.ppermute(e, "segment", [(d, s) for s, d in pairs])
        e, kept = lax.cond(
            plane == p,
            lambda e, saved, kept: backward_plane(e, saved, turned, p),
            lambda e, saved, kept: (e, kept),
            e,
            saved,
            kept,
        )

    narrow = (saved[0][3], saved[1][3], kept[0][1], kept[1][1])
    narrow_out = shape_of(tp * 4 * rank, rows)
    spread_out = rows_call(narrow_kernel, narrow_out, *narrow, cost=ahead)
    pair = [shape_of(rank, 2 * cols, dtype=F32)] * 2
    split_mine, split_sent = rows_call(
        choose_kernel, pair, ids, *kept[0][2:], *kept[1][2:], scalars=1
    )
    split_theirs = lax.ppermute(split_sent, "segment", swap)
    got = exchanged(spread_out, tp)
    wide = [shape_of(rank, 2 * width, dtype=F32)] * 2
    per_block = [a for i in range(2) for a in in_vmem(kept[i][0], saved[i][1])]
    mine, sent = rows_call(gradients_kernel, wide, ids, got, *per_block, scalars=1)
    theirs = lax.ppermute(sent, "segment", swap)
    split = [shape_of(jobs, rank, cols, dtype=F32)] * 2
    grad_ui, grad_do = rows_call(
        split_kernel,
        split,
        ids,
        job_ids,
        split_mine,
        split_theirs,
        scalars=2,
        cost=pl.CostEstimate(flops=0, bytes_accessed=8 * jobs * rank * cols, transcendentals=0),
    )
    owned = [shape_of(jobs // tp, rank, width, dtype=F32)] * 2
    grad_di, grad_uo = rows_call(
        owned_kernel, owned, ids, job_ids, mine, theirs, scalars=2
    )
    return tuple(grad[None] for grad in (grad_di, grad_ui, grad_do, grad_uo))


def solution(mesh):
    return jax.shard_map(
        shards,
        mesh=mesh,
        in_specs=(
            P(None, "tp", None),
            P(None, "tp", None),
            P(),
            P(),
            P("segment", None, None, None),
            P("segment", None, "tp"),
            P("segment", "tp", None),
            P("segment", None, None, None),
            P("segment", None, None, "tp"),
            P("segment", None, None, "tp"),
            P("segment", None, None, None),
        ),
        out_specs=(
            P("segment", "tp", None, None),
            P("segment", None, None, "tp"),
            P("segment", None, None, "tp"),
            P("segment", "tp", None, None),
        ),
        check_vma=False,
    )
```
